32 devices in a mesh: dp: 16 (over z, x, core), tensor: 2 (over y).
Axes of the slice: x: 2, y: 2, z: 4, core: 2. Of those that a mesh axis runs over, the one named last changes fastest.
Arguments:
- hidden: bfloat16 [32768, 768], P(('dp', 'tensor')), may hold values from -6 to 6
- input_gain: bfloat16 [768], replicated, may hold values from 0.5 to 1.5
- proj_gate: bfloat16 [768, 1536], P('dp', 'tensor'), may hold values from -0.21875 to 0.21875
- proj_inner: bfloat16 [768, 1536], P('dp', 'tensor'), may hold values from -0.21875 to 0.21875
- proj_shared: bfloat16 [768, 256], P('dp'), may hold values from -0.21875 to 0.21875
- proj_rate: bfloat16 [768, 24], P('dp', 'tensor'), may hold values from -0.21875 to 0.21875
- conv_inner: bfloat16 [4, 1536], replicated, may hold values from -3 to 3
- conv_inner_bias: bfloat16 [1536], replicated, may hold values from -3 to 3
- conv_shared: bfloat16 [4, 256], replicated, may hold values from -3 to 3
- conv_shared_bias: bfloat16 [256], replicated, may hold values from -3 to 3
- rate_bias: float32 [24], replicated, may hold values from -7 to -2
- decay_log: float32 [24], replicated, may hold values from 0 to 2.7
- skip_gain: float32 [24], replicated, may hold values from 0.5 to 1.5
- output_gain: bfloat16 [1536], replicated, may hold values from 0.5 to 1.5
- proj_output: bfloat16 [768, 1536], P('dp', 'tensor'), may hold values from -0.15625 to 0.15625
- cotangent: bfloat16 [32768, 768], P(('dp', 'tensor')), may hold values from -6 to 6
Outputs:
- output: bfloat16 [32768, 768], P(('dp', 'tensor'))
- grad_hidden: bfloat16 [32768, 768], P(('dp', 'tensor'))
- grad_input_gain: float32 [768], replicated
- grad_proj_gate: float32 [768, 1536], P('dp', 'tensor')
- grad_proj_inner: float32 [768, 1536], P('dp', 'tensor')
- grad_proj_shared: float32 [768, 256], P('dp')
- grad_proj_rate: float32 [768, 24], P('dp', 'tensor')
- grad_conv_inner: float32 [4, 1536], replicated
- grad_conv_inner_bias: float32 [1536], replicated
- grad_conv_shared: float32 [4, 256], replicated
- grad_conv_shared_bias: float32 [256], replicated
- grad_rate_bias: float32 [24], replicated
- grad_decay_log: float32 [24], replicated
- grad_skip_gain: float32 [24], replicated
- grad_output_gain: float32 [1536], replicated
- grad_proj_output: float32 [768, 1536], P('dp', 'tensor')
The draws below stay inside these ranges and needn't reach their ends.
All inputs are finite; a program needn't handle non-finite values.
Results may differ from the reference program's by a relative error of at most 0.02.
Values may be sent and summed in bfloat16 or wider, within the bound.
No kernel may reach another device: no remote copies, remote signals or barrier semaphores. Data moves between devices by JAX's collectives and lax.ppermute only.
A program may use at most 192 MiB of HBM per device.

```python
import jax
import jax.numpy as jnp
from jax import lax

D = 768
HEADS = 24
HEAD_DIM = 64
STATE = 128
INNER = 1536
CONV = 4
BLOCK = 256
SEQ_LEN = 2048
GROUP_TOK = 2048
TOKENS = 32768


def steps_of(stream_key, dims, shards, smallest, largest):
    factor_of = 1.0
    for position, shards_of in shards:
        heights = jax.random.uniform(jax.random.fold_in(jax.random.fold_in(stream_key, 6), position), (shards_of,), jnp.float32, smallest / len(shards), largest / len(shards))
        factor_of = factor_of * jnp.repeat(jnp.exp(heights), dims[position] // shards_of).reshape((-1,) + (1,) * (len(dims) - 1 - position))
    return factor_of


def normal_values(rng, dims, spread, limit, split=(), held_as=jnp.bfloat16):
    values = spread * jax.random.normal(rng, dims, jnp.float32)
    if split:
        values = values * steps_of(rng, dims, split, -0.22, 0.18)
    return jnp.clip(values, -limit, limit).astype(held_as)


def setup_inputs(seed: int = 0) -> dict:
    arg_keys = jax.random.split(jax.random.key(seed), 17)
    hidden = normal_values(arg_keys[0], (TOKENS, D), 1.0, 6.0, ((0, 32),))
    input_gain = jnp.clip(1.0 + 0.1 * jax.random.normal(arg_keys[1], (D,), jnp.float32), 0.5, 1.5).astype(jnp.bfloat16)
    proj_gate = normal_values(arg_keys[2], (D, INNER), D ** -0.5, 0.21875, ((0, 16), (1, 2)))
    proj_inner = normal_values(arg_keys[3], (D, INNER), D ** -0.5, 0.21875, ((0, 16), (1, 2)))
    proj_shared = normal_values(arg_keys[4], (D, 2 * STATE), D ** -0.5, 0.21875, ((0, 16),))
    proj_rate = normal_values(arg_keys[5], (D, HEADS), D ** -0.5, 0.21875, ((0, 16), (1, 2)))
    conv_inner = normal_values(arg_keys[6], (CONV, INNER), CONV ** -0.5, 3.0)
    conv_inner_bias = normal_values(arg_keys[7], (INNER,), 0.5, 3.0)
    conv_shared = normal_values(arg_keys[8], (CONV, 2 * STATE), CONV ** -0.5, 3.0)
    conv_shared_bias = normal_values(arg_keys[9], (2 * STATE,), 0.5, 3.0)
    rate_bias = jnp.clip(jax.random.uniform(arg_keys[10], (HEADS,), jnp.float32, -7.0, -2.0), -7.0, -2.0)
    decay_log = jnp.clip(jax.random.uniform(arg_keys[11], (HEADS,), jnp.float32, 0.0, 2.7), 0.0, 2.7)
    skip_gain = jnp.clip(jax.random.uniform(arg_keys[12], (HEADS,), jnp.float32, 0.5, 1.5), 0.5, 1.5)
    output_gain = jnp.clip(1.0 + 0.1 * jax.random.normal(arg_keys[13], (INNER,), jnp.float32), 0.5, 1.5).astype(jnp.bfloat16)
    proj_output = normal_values(arg_keys[14], (D, INNER), INNER ** -0.5, 0.15625, ((0, 16), (1, 2)))
    cotangent = normal_values(arg_keys[15], (TOKENS, D), 1.0, 6.0, ((0, 32),))
    return dict(hidden=hidden, input_gain=input_gain, proj_gate=proj_gate, proj_inner=proj_inner, proj_shared=proj_shared, proj_rate=proj_rate, conv_inner=conv_inner, conv_inner_bias=conv_inner_bias, conv_shared=conv_shared, conv_shared_bias=conv_shared_bias, rate_bias=rate_bias, decay_log=decay_log, skip_gain=skip_gain, output_gain=output_gain, proj_output=proj_output, cotangent=cotangent)


@jax.custom_vjp
def low(v):
    return lax.optimization_barrier(v.astype(jnp.bfloat16)).astype(jnp.float32)

@jax.custom_vjp
def low_back(v):
    return v

def low_keep(v):
    return (low(v), None)

def low_pass(kept, grad):
    return (grad,)

def back_keep(v):
    return (v, None)

def back_low(kept, grad):
    return (low(grad),)
low.defvjp(low_keep, low_pass)
low_back.defvjp(back_keep, back_low)
highest = lax.Precision.HIGHEST
eps_norm = 1e-05

def matmul(left, right):
    return jnp.dot(left, right, precision=highest, preferred_element_type=jnp.float32)

def causal_conv(values, kernel, offset):
    kernel_len = kernel.shape[0]
    length = values.shape[1]
    padded = jnp.pad(values, ((0, 0), (kernel_len - 1, 0), (0, 0)))
    summed = offset + kernel[0] * padded[:, 0:length, :]
    for tap_index in range(1, kernel_len):
        summed = summed + kernel[tap_index] * padded[:, tap_index:tap_index + length, :]
    return summed

def ssd_head(inputs, step_size, decay_rate, skip_gain, scores, key_state, queries):
    log_decay = step_size * decay_rate
    within = jnp.cumsum(log_decay, axis=-1)
    block_len = scores.shape[-1]
    causal = jnp.arange(block_len)[:, None] >= jnp.arange(block_len)[None, :]
    decay_gap = within[..., :, None] - within[..., None, :]
    weights = jnp.exp(jnp.where(causal, decay_gap, -jnp.inf))
    scaled = inputs * step_size[..., None]
    diagonal = jnp.einsum('bkqr,bkrp->bkqp', scores * weights, scaled, precision=highest)
    to_end = jnp.exp(within[..., -1:] - within)
    states = jnp.einsum('bkrn,bkrp->bknp', key_state, scaled * to_end[..., None], precision=highest)
    factors = jnp.exp(within[..., -1])

    def chain_step(carried, pair_item):
        fresh_state, factor = pair_item
        return (factor[:, None, None] * carried + fresh_state, carried)
    _, entering = lax.scan(chain_step, jnp.zeros_like(states[:, 0]), (jnp.moveaxis(states, 1, 0), jnp.moveaxis(factors, 1, 0)))
    entering = jnp.moveaxis(entering, 0, 1)
    offdiag = jnp.einsum('bkqn,bknp->bkqp', queries, entering, precision=highest) * jnp.exp(within)[..., None]
    return diagonal + offdiag + skip_gain * inputs

def layer(hidden, input_gain, proj_gate, proj_inner, proj_shared, proj_rate, conv_inner, conv_inner_bias, conv_shared, conv_shared_bias, rate_bias, decay_log, skip_gain, output_gain, proj_output):
    seq_count = hidden.shape[0] // SEQ_LEN
    block_count = SEQ_LEN // BLOCK
    root_inv = lax.rsqrt(lax.optimization_barrier(jnp.mean(hidden * hidden, axis=-1, keepdims=True)) + eps_norm)
    normed = low(hidden * root_inv * input_gain)
    gate_proj = low_back(low(matmul(normed, proj_gate)))
    inner_proj = low_back(low(matmul(normed, proj_inner)))
    shared_proj = low_back(low(matmul(normed, proj_shared)))
    rate_proj = low_back(low(matmul(normed, proj_rate)))

    def to_seq(value):
        return value.reshape(seq_count, SEQ_LEN, value.shape[-1])

    def to_block(value):
        return value.reshape(seq_count, block_count, BLOCK, value.shape[-1])
    pre_inner = causal_conv(to_seq(inner_proj), conv_inner, conv_inner_bias)
    pre_shared = causal_conv(to_seq(shared_proj), conv_shared, conv_shared_bias)
    mixed_in = low(jax.nn.silu(pre_inner))
    shared_act = low(jax.nn.silu(pre_shared))
    key_state = to_block(shared_act[..., :STATE])
    queries = to_block(shared_act[..., STATE:])
    step_size = jax.nn.softplus(to_seq(rate_proj) + rate_bias)
    decay_rate = -jnp.exp(decay_log)
    scores = jnp.einsum('bkqn,bkrn->bkqr', queries, key_state, precision=highest)
    inputs = to_block(mixed_in).reshape(seq_count, block_count, BLOCK, HEADS, HEAD_DIM)
    heads_out = jax.vmap(ssd_head, in_axes=(3, 3, 0, 0, None, None, None), out_axes=3)(inputs, to_block(step_size), decay_rate, skip_gain, scores, key_state, queries)
    mixed_out = low_back(low(heads_out.reshape(-1, INNER)))
    gated = mixed_out * jax.nn.silu(gate_proj)
    gated_root = lax.rsqrt(lax.optimization_barrier(jnp.mean(gated * gated, axis=-1, keepdims=True)) + eps_norm)
    out_normed = low(gated * gated_root * output_gain)
    return hidden + matmul(out_normed, proj_output.T)

def reference(hidden, input_gain, proj_gate, proj_inner, proj_shared, proj_rate, conv_inner, conv_inner_bias, conv_shared, conv_shared_bias, rate_bias, decay_log, skip_gain, output_gain, proj_output, cotangent):
    params = tuple((param.astype(jnp.float32) for param in (input_gain, proj_gate, proj_inner, proj_shared, proj_rate, conv_inner, conv_inner_bias, conv_shared, conv_shared_bias, rate_bias, decay_log, skip_gain, output_gain, proj_output)))
    group_count = TOKENS // GROUP_TOK
    hidden_groups = hidden.astype(jnp.float32).reshape(group_count, GROUP_TOK, D)
    cot_groups = cotangent.astype(jnp.float32).reshape(group_count, GROUP_TOK, D)

    def one_group(grad_sums, pair_item):
        rows_now, cot_now = pair_item
        result, pullback = jax.vjp(layer, rows_now, *params)
        grad_all = pullback(cot_now)
        grad_sums = tuple((running + fresh_grad for running, fresh_grad in zip(grad_sums, grad_all[1:])))
        return (grad_sums, (result.astype(jnp.bfloat16), grad_all[0].astype(jnp.bfloat16)))
    start_sums = tuple((jnp.zeros_like(param) for param in params))
    grad_sums, (out_rows, grad_rows) = lax.scan(one_group, start_sums, (hidden_groups, cot_groups))
    return (out_rows.reshape(TOKENS, D), grad_rows.reshape(TOKENS, D), grad_sums[0], grad_sums[1], grad_sums[2], grad_sums[3], grad_sums[4], grad_sums[5], grad_sums[6], grad_sums[7], grad_sums[8], grad_sums[9], grad_sums[10], grad_sums[11], grad_sums[12], grad_sums[13])
```

```python
import functools

import jax
import jax.numpy as jnp
from jax import lax
from jax.experimental import pallas as pl
from jax.experimental.pallas import tpu as pltpu
from jax.sharding import PartitionSpec as P

SEQ_LEN = 2048
CHUNK = 128
RIM = 16
LANES = 128
EPS = 1e-05
F32 = jnp.float32
BF16 = jnp.bfloat16


def mm(left, right, contract=((1,), (0,))):
    return lax.dot_general(left, right, (contract, ((), ())), preferred_element_type=F32)


NT = ((1,), (1,))
TN = ((0,), (0,))


def split3(value):
    high = value.astype(BF16)
    rest = value - high.astype(F32)
    mid = rest.astype(BF16)
    return high, mid, (rest - mid.astype(F32)).astype(BF16)


def exact_left(ones, value):
    high, mid, low = split3(value)
    return mm(ones, high) + mm(ones, mid) + mm(ones, low)


def exact_right(value, ones):
    high, mid, low = split3(value)
    return mm(high, ones) + mm(mid, ones) + mm(low, ones)


def spread_matrix(heads, inner):
    head_dim = inner // heads
    row = lax.broadcasted_iota(jnp.int32, (LANES, inner), 0)
    col = lax.broadcasted_iota(jnp.int32, (LANES, inner), 1)
    return ((col >= row * head_dim) & (col < (row + 1) * head_dim)).astype(BF16)


def iota2(shape, dim):
    return lax.broadcasted_iota(jnp.int32, shape, dim)


def softplus(v):
    return jnp.maximum(v, 0.0) + jnp.log1p(jnp.exp(-jnp.abs(v)))


def conv_rows(ext_ref, taps, bias, lo, width, rows):
    total = bias
    for k in range(4):
        total = total + taps[k : k + 1, :] * ext_ref[pl.ds(5 + k, rows), pl.ds(lo, width)]
    return total


def mix_in_kernel(
    inner, heads,
    proj_ref, rim_ref, tap_ref, bias_ref, rate_bias_ref, decay_ref,
    x_ref, bc_ref, step_ref, within_ref, final_ref, total_ref,
    ext_ref, u_ref,
):
    i = pl.program_id(0)
    shared = 2 * LANES
    conv_width = inner + shared

    @pl.when(i == 0)
    def _():
        ext_ref[0:8, :] = rim_ref[...].astype(F32)[RIM - 8 :, :conv_width]
        final_ref[...] = jnp.zeros_like(final_ref)
        total_ref[...] = jnp.zeros_like(total_ref)

    @pl.when(i > 0)
    def _():
        ext_ref[0:8, :] = ext_ref[CHUNK : CHUNK + 8, :]

    ext_ref[8:, :] = proj_ref[:, :conv_width].astype(F32)
    step = softplus(proj_ref[:, conv_width:].astype(F32) + rate_bias_ref[...])
    log_decay = step * decay_ref[...]
    lower = (iota2((CHUNK, CHUNK), 0) >= iota2((CHUNK, CHUNK), 1)).astype(BF16)
    within = exact_left(lower, log_decay)
    step_ref[...] = step
    within_ref[...] = within
    last = within[CHUNK - 1 :, :]
    total_ref[...] += last
    weight = step * jnp.exp(last - within)

    pre = conv_rows(ext_ref, tap_ref[:, inner:], bias_ref[:, inner:], inner, shared, CHUNK)
    bc = (pre * jax.nn.sigmoid(pre)).astype(BF16)
    bc_ref[...] = bc
    first = iota2((CHUNK, LANES), 1) < LANES // 2
    for p in range(inner // LANES):
        lo = p * LANES
        pre = conv_rows(
            ext_ref, tap_ref[:, lo : lo + LANES], bias_ref[:, lo : lo + LANES], lo, LANES, CHUNK
        )
        x = (pre * jax.nn.sigmoid(pre)).astype(BF16)
        x_ref[:, lo : lo + LANES] = x
        w = jnp.where(
            first,
            jnp.broadcast_to(weight[:, 2 * p : 2 * p + 1], (CHUNK, LANES)),
            jnp.broadcast_to(weight[:, 2 * p + 1 : 2 * p + 2], (CHUNK, LANES)),
        )
        u_ref[:, lo : lo + LANES] = (x.astype(F32) * w).astype(BF16)
    factor = exact_right(jnp.exp(jnp.broadcast_to(last, (8, LANES))), spread_matrix(heads, inner))
    final_ref[...] = factor[0:1, :] * final_ref[...] + mm(bc[:, :LANES], u_ref[...], TN)


def mix_in(proj, rows, taps, bias, rate_bias, decay, inner, heads):
    width = proj.shape[1]
    chunks = rows // CHUNK
    full = lambda shape: pl.BlockSpec(shape, lambda i: (0,) * len(shape))
    return pl.pallas_call(
        functools.partial(mix_in_kernel, inner, heads),
        grid=(chunks,),
        in_specs=[
            pl.BlockSpec((CHUNK, width), lambda i: (i, 0)),
            pl.BlockSpec((RIM, width), lambda i: (rows // RIM, 0)),
            full(taps.shape), full(bias.shape), full(rate_bias.shape), full(decay.shape),
        ],
        out_specs=[
            pl.BlockSpec((CHUNK, inner), lambda i: (i, 0)),
            pl.BlockSpec((CHUNK, 2 * LANES), lambda i: (i, 0)),
            pl.BlockSpec((CHUNK, LANES), lambda i: (i, 0)),
            pl.BlockSpec((CHUNK, LANES), lambda i: (i, 0)),
            full((LANES, inner)),
            full((1, LANES)),
        ],
        out_shape=[
            jax.ShapeDtypeStruct((rows, inner), BF16),
            jax.ShapeDtypeStruct((rows, 2 * LANES), BF16),
            jax.ShapeDtypeStruct((rows, LANES), F32),
            jax.ShapeDtypeStruct((rows, LANES), F32),
            jax.ShapeDtypeStruct((LANES, inner), F32),
            jax.ShapeDtypeStruct((1, LANES), F32),
        ],
        scratch_shapes=[
            pltpu.VMEM((CHUNK + 8, inner + 2 * LANES), F32),
            pltpu.VMEM((CHUNK, inner), BF16),
        ],
        compiler_params=pltpu.CompilerParams(vmem_limit_bytes=48 * 2**20),
        cost_estimate=pl.CostEstimate(
            flops=40 * rows * inner, bytes_accessed=6 * rows * inner, transcendentals=0
        ),
        name="mix_in",
    )(proj, proj, taps, bias, rate_bias, decay)


def mix_out_kernel(
    inner, heads,
    x_ref, bc_ref, step_ref, within_ref, gate_ref, gon_ref, entry_ref, skip_ref, gain_ref,
    normed_ref, gm_ref, gg_ref, state_ref, grad_entry_ref, sums_ref,
    hold_ref, y_ref, u_ref, prefix_ref,
):
    i = pl.program_id(0)

    @pl.when(i == 0)
    def _():
        hold_ref[...] = entry_ref[...].astype(F32)
        grad_entry_ref[...] = jnp.zeros_like(grad_entry_ref)
        sums_ref[...] = jnp.zeros_like(sums_ref)
        prefix_ref[...] = jnp.zeros_like(prefix_ref)

    spread = spread_matrix(heads, inner)
    key, query = bc_ref[:, :LANES], bc_ref[:, LANES:]
    within = within_ref[...]
    within_t = within.T
    last = within[CHUNK - 1 :, :]
    state = hold_ref[...].astype(BF16)
    state_ref[0] = state
    y_ref[...] = mm(query, state)
    scores = mm(query, key, NT)
    causal = iota2((CHUNK, CHUNK), 0) >= iota2((CHUNK, CHUNK), 1)
    first = iota2((CHUNK, LANES), 1) < LANES // 2
    zero = jnp.zeros((CHUNK, LANES), BF16)
    for p in range(inner // LANES):
        lo = p * LANES
        slab = slice(lo, lo + LANES)
        cols, weights = [], []
        for h in (2 * p, 2 * p + 1):
            col = jnp.broadcast_to(within[:, h : h + 1], (CHUNK, CHUNK))
            gap = jnp.where(causal, col - within_t[h : h + 1, :], -1e30)
            weights.append((scores * jnp.exp(gap)).astype(BF16))
            cols.append(col)
        a = jnp.where(first, cols[0], cols[1])
        d = jnp.where(
            first,
            jnp.broadcast_to(step_ref[:, 2 * p : 2 * p + 1], (CHUNK, LANES)),
            jnp.broadcast_to(step_ref[:, 2 * p + 1 : 2 * p + 2], (CHUNK, LANES)),
        )
        x = x_ref[:, slab].astype(F32)
        u = x * d
        ub = u.astype(BF16)
        u_ref[:, slab] = (u * jnp.exp(a[CHUNK - 1 :, :] - a)).astype(BF16)
        diagonal = mm(
            jnp.concatenate(weights, axis=1),
            jnp.concatenate([jnp.where(first, ub, zero), jnp.where(first, zero, ub)], axis=0),
        )
        y_ref[:, slab] = diagonal + jnp.exp(a) * y_ref[:, slab] + skip_ref[:, slab] * x
    factors = exact_right(
        jnp.exp(jnp.concatenate([last, prefix_ref[...], jnp.zeros((6, LANES), F32)], axis=0)),
        spread,
    )
    prefix_ref[...] += last
    hold_ref[...] = factors[0:1, :] * hold_ref[...] + mm(key, u_ref[...], TN)

    square = jnp.zeros((CHUNK, LANES), F32)
    dot = jnp.zeros((CHUNK, LANES), F32)
    for p in range(inner // LANES):
        slab = slice(p * LANES, (p + 1) * LANES)
        z = gate_ref[:, slab].astype(F32)
        m = y_ref[:, slab].astype(BF16).astype(F32)
        gated = m * (z * jax.nn.sigmoid(z))
        square = square + gated * gated
        dot = dot + gain_ref[:, slab] * gon_ref[:, slab] * gated
    square = jnp.sum(square, axis=1, keepdims=True)
    dot = jnp.sum(dot, axis=1, keepdims=True)
    root = lax.rsqrt(square / inner + EPS)
    pull = root * root * root * dot / inner
    for p in range(inner // LANES):
        slab = slice(p * LANES, (p + 1) * LANES)
        z = gate_ref[:, slab].astype(F32)
        m = y_ref[:, slab].astype(BF16).astype(F32)
        sig = jax.nn.sigmoid(z)
        act = z * sig
        gated = m * act
        gon = gon_ref[:, slab]
        unit = gated * root
        normed_ref[:, slab] = (unit * gain_ref[:, slab]).astype(BF16)
        grad = root * gain_ref[:, slab] * gon - gated * pull
        gm = (grad * act).astype(BF16)
        gm_ref[:, slab] = gm
        gg_ref[:, slab] = (grad * m * (sig * (1.0 + z * (1.0 - sig)))).astype(BF16)
        gmf = gm.astype(F32)
        sums_ref[0:1, slab] += jnp.sum(gon * unit, axis=0, keepdims=True)
        sums_ref[1:2, slab] += jnp.sum(gmf * x_ref[:, slab].astype(F32), axis=0, keepdims=True)
        a = jnp.where(
            first,
            jnp.broadcast_to(within[:, 2 * p : 2 * p + 1], (CHUNK, LANES)),
            jnp.broadcast_to(within[:, 2 * p + 1 : 2 * p + 2], (CHUNK, LANES)),
        )
        u_ref[:, slab] = (gmf * jnp.exp(a)).astype(BF16)
    grad_entry_ref[...] += factors[1:2, :] * mm(query, u_ref[...], TN)


def mix_out(x, bc, step, within, gate, gon, entry, skip, gain, heads):
    rows, inner = x.shape
    chunks = rows // CHUNK
    full = lambda shape: pl.BlockSpec(shape, lambda i: (0,) * len(shape))
    block = lambda width: pl.BlockSpec((CHUNK, width), lambda i: (i, 0))
    return pl.pallas_call(
        functools.partial(mix_out_kernel, inner, heads),
        grid=(chunks,),
        in_specs=[
            block(inner), block(2 * LANES), block(LANES), block(LANES), block(inner), block(inner),
            full(entry.shape), full(skip.shape), full(gain.shape),
        ],
        out_specs=[
            block(inner), block(inner), block(inner),
            pl.BlockSpec((1, LANES, inner), lambda i: (i, 0, 0)),
            full((LANES, inner)), full((8, inner)),
        ],
        out_shape=[
            jax.ShapeDtypeStruct((rows, inner), BF16),
            jax.ShapeDtypeStruct((rows, inner), BF16),
            jax.ShapeDtypeStruct((rows, inner), BF16),
            jax.ShapeDtypeStruct((chunks, LANES, inner), BF16),
            jax.ShapeDtypeStruct((LANES, inner), F32),
            jax.ShapeDtypeStruct((8, inner), F32),
        ],
        scratch_shapes=[
            pltpu.VMEM((LANES, inner), F32),
            pltpu.VMEM((CHUNK, inner), F32),
            pltpu.VMEM((CHUNK, inner), BF16),
            pltpu.VMEM((1, LANES), F32),
        ],
        compiler_params=pltpu.CompilerParams(vmem_limit_bytes=48 * 2**20),
        cost_estimate=pl.CostEstimate(
            flops=800 * rows * inner, bytes_accessed=16 * rows * inner, transcendentals=0
        ),
        name="mix_out",
    )(x, bc, step, within, gate, gon, entry, skip, gain)


def mix_back_kernel(
    inner, heads, chunks,
    x_ref, bc_ref, step_ref, within_ref, gm_ref, state_ref, proj_ref, prev_ref, rim_ref,
    exit_ref, skip_ref, tap_ref, bias_ref, rate_bias_ref, decay_ref,
    gproj_ref, sums_ref, heads_ref,
    hold_ref, ext_ref, ahead_ref, cs_ref, bg_ref, ue_ref, ge_ref, prod_ref, rows_ref,
):
    j = pl.program_id(0)
    i = chunks - 1 - j
    shared = 2 * LANES
    conv_width = inner + shared

    @pl.when(j == 0)
    def _():
        hold_ref[...] = exit_ref[...].astype(F32)
        sums_ref[...] = jnp.zeros_like(sums_ref)
        heads_ref[...] = jnp.zeros_like(heads_ref)
        ahead_ref[CHUNK:, :] = jnp.zeros((8, conv_width), F32)
        rows_ref[...] = jnp.zeros_like(rows_ref)

    @pl.when((j > 0) & (j < chunks))
    def _():
        ahead_ref[CHUNK:, :] = ahead_ref[0:8, :]

    @pl.when(j < chunks)
    def _():
        before = jnp.where(i == 0, rim_ref[...].astype(F32), prev_ref[...].astype(F32))
        ext_ref[0:8, :] = before[RIM - 8 :, :conv_width]
        ext_ref[8:, :] = proj_ref[:, :conv_width].astype(F32)
        spread = spread_matrix(heads, inner)
        key, query = bc_ref[:, :LANES], bc_ref[:, LANES:]
        within = within_ref[...]
        within_t = within.T
        step = step_ref[...]
        last = within[CHUNK - 1 :, :]
        state = state_ref[0]
        hold = hold_ref[...]
        exit_grad = hold.astype(BF16)
        cs_ref[...] = mm(query, state)
        bg_ref[...] = mm(key, exit_grad)
        scores_t = mm(key, query, NT)
        causal_t = iota2((CHUNK, CHUNK), 0) <= iota2((CHUNK, CHUNK), 1)
        first = iota2((CHUNK, LANES), 1) < LANES // 2
        lane = iota2((2 * CHUNK, LANES), 1)
        upper_half = iota2((2 * CHUNK, LANES), 0) >= CHUNK
        zero = jnp.zeros((CHUNK, LANES), BF16)
        grad_scores_t = jnp.zeros((CHUNK, CHUNK), F32)
        col_sums = jnp.zeros((CHUNK, LANES), F32)
        for p in range(inner // LANES):
            slab = slice(p * LANES, (p + 1) * LANES)
            x = x_ref[:, slab].astype(F32)
            gb = gm_ref[:, slab]
            g = gb.astype(F32)
            cols = [
                jnp.broadcast_to(within[:, h : h + 1], (CHUNK, LANES)) for h in (2 * p, 2 * p + 1)
            ]
            a = jnp.where(first, cols[0], cols[1])
            d = jnp.where(
                first,
                jnp.broadcast_to(step[:, 2 * p : 2 * p + 1], (CHUNK, LANES)),
                jnp.broadcast_to(step[:, 2 * p + 1 : 2 * p + 2], (CHUNK, LANES)),
            )
            u = x * d
            ub = u.astype(BF16)
            to_end = jnp.exp(a[CHUNK - 1 :, :] - a)
            ge = g * jnp.exp(a)
            ge_ref[:, slab] = ge.astype(BF16)
            ue_ref[:, slab] = (u * to_end).astype(BF16)
            gcat = jnp.concatenate([jnp.where(first, gb, zero), jnp.where(first, zero, gb)], axis=0)
            reach_t = mm(ub, gcat, NT)
            pieces, moves = [], []
            for q, h in enumerate((2 * p, 2 * p + 1)):
                gap = jnp.where(causal_t, within_t[h : h + 1, :] - cols[q], -1e30)
                weight = jnp.exp(gap)
                grad_score = reach_t[:, q * CHUNK : (q + 1) * CHUNK] * weight
                grad_scores_t = grad_scores_t + grad_score
                pieces.append((scores_t * weight).astype(BF16))
                move = (grad_score * scores_t).astype(BF16)
                moves.append(move)
                rows_ref[h : h + 1, :] = jnp.sum(move.astype(F32), axis=0, keepdims=True)
            pick = (lane == jnp.where(upper_half, 2 * p + 1, 2 * p)).astype(BF16)
            col_sums = col_sums + mm(jnp.concatenate(moves, axis=1), pick)
            grad_state_u = to_end * bg_ref[:, slab]
            grad_u = mm(jnp.concatenate(pieces, axis=1), gcat) + grad_state_u
            prod_ref[0:CHUNK, slab] = (x * grad_u).astype(BF16)
            prod_ref[CHUNK : 2 * CHUNK, slab] = (u * grad_state_u).astype(BF16)
            prod_ref[2 * CHUNK :, slab] = (ge * cs_ref[:, slab]).astype(BF16)
            grad_x = d * grad_u + skip_ref[:, slab] * g
            pre = conv_rows(ext_ref, tap_ref[:, slab], bias_ref[:, slab], p * LANES, LANES, CHUNK)
            sig = jax.nn.sigmoid(pre)
            ahead_ref[0:CHUNK, slab] = grad_x * (sig * (1.0 + pre * (1.0 - sig)))

        by_head = mm(prod_ref[...], spread, NT)
        grad_step = by_head[0:CHUNK]
        from_state = by_head[CHUNK : 2 * CHUNK]
        from_entry = by_head[2 * CHUNK :]
        factor = exact_right(jnp.exp(jnp.broadcast_to(last, (8, LANES))), spread)[0:1, :]
        whole = jnp.sum(hold * state.astype(F32), axis=0, keepdims=True) * factor
        whole = jnp.broadcast_to(whole, (8, inner))
        high, mid, _ = split3(whole)
        whole = (mm(high, spread, NT) + mm(mid, spread, NT))[0:1, :]
        later = (iota2((CHUNK, CHUNK), 0) <= iota2((CHUNK, CHUNK), 1)).astype(BF16)
        earlier = (iota2((CHUNK, CHUNK), 0) > iota2((CHUNK, CHUNK), 1)).astype(BF16)
        row_sums = rows_ref[...].T
        grad_log = (
            exact_left(later, row_sums - col_sums + from_entry)
            + exact_left(earlier, from_state)
            + whole
        )
        decay = decay_ref[...]
        grad_step = grad_step + grad_log * decay
        squash = jax.nn.sigmoid(proj_ref[:, conv_width:].astype(F32) + rate_bias_ref[...])
        grad_rate = grad_step * squash
        gproj_ref[:, conv_width:] = grad_rate.astype(BF16)
        heads_ref[0:1, :] += jnp.sum(grad_rate, axis=0, keepdims=True)
        heads_ref[1:2, :] += jnp.sum(grad_log * step, axis=0, keepdims=True) * decay

        gsb = grad_scores_t.astype(BF16)
        grad_key = mm(ue_ref[...], exit_grad, NT) + mm(gsb, query)
        grad_query = mm(ge_ref[...], state, NT) + mm(gsb, key, TN)
        hold_ref[...] = factor * hold + mm(query, ge_ref[...], TN)

        pre = conv_rows(ext_ref, tap_ref[:, inner:], bias_ref[:, inner:], inner, shared, CHUNK)
        sig = jax.nn.sigmoid(pre)
        slope = sig * (1.0 + pre * (1.0 - sig))
        ahead_ref[0:CHUNK, inner:] = jnp.concatenate([grad_key, grad_query], axis=1) * slope

        for p in range(conv_width // LANES):
            slab = slice(p * LANES, (p + 1) * LANES)
            values = ext_ref[8:, slab]
            total = jnp.zeros((CHUNK, LANES), F32)
            for k in range(4):
                moved = ahead_ref[pl.ds(3 - k, CHUNK), slab]
                total = total + tap_ref[k : k + 1, slab] * moved
                sums_ref[k : k + 1, slab] += jnp.sum(values * moved, axis=0, keepdims=True)
                if k == 3:
                    sums_ref[4:5, slab] += jnp.sum(moved, axis=0, keepdims=True)
            gproj_ref[:, slab] = total.astype(BF16)

    @pl.when(j == chunks)
    def _():
        gproj_ref[...] = jnp.zeros_like(gproj_ref)
        head = ahead_ref[0:8, :]
        at = iota2((8, conv_width), 0)
        values = rim_ref[...].astype(F32)[RIM - 8 :, :conv_width]
        total = jnp.zeros((8, conv_width), F32)
        for k in range(3):
            moved = jnp.zeros((8, conv_width), F32)
            for r in range(5 + k, 8):
                t = r - 5 - k
                moved = moved + jnp.where(at == r, head[t : t + 1, :], 0.0)
            total = total + tap_ref[k : k + 1, :] * moved
            sums_ref[k : k + 1, :] += jnp.sum(values * moved, axis=0, keepdims=True)
        gproj_ref[0:RIM, :conv_width] = jnp.concatenate(
            [jnp.zeros((RIM - 8, conv_width), F32), total], axis=0
        ).astype(BF16)


def mix_back(x, bc, step, within, gm, state, proj, exit_grad, skip, taps, bias, rate_bias, decay,
             heads):
    rows, inner = x.shape
    width = proj.shape[1]
    chunks = rows // CHUNK
    per = CHUNK // RIM
    conv_width = inner + 2 * LANES
    full = lambda shape: pl.BlockSpec(shape, lambda j: (0,) * len(shape))
    at = lambda j: jnp.maximum(chunks - 1 - j, 0)
    block = lambda w: pl.BlockSpec((CHUNK, w), lambda j: (at(j), 0))
    return pl.pallas_call(
        functools.partial(mix_back_kernel, inner, heads, chunks),
        grid=(chunks + 1,),
        in_specs=[
            block(inner), block(2 * LANES), block(LANES), block(LANES), block(inner),
            pl.BlockSpec((1, LANES, inner), lambda j: (at(j), 0, 0)),
            block(width),
            pl.BlockSpec((RIM, width), lambda j: (jnp.maximum(at(j) * per - 1, 0), 0)),
            pl.BlockSpec((RIM, width), lambda j: (rows // RIM, 0)),
            full(exit_grad.shape), full(skip.shape), full(taps.shape), full(bias.shape),
            full(rate_bias.shape), full(decay.shape),
        ],
        out_specs=[
            pl.BlockSpec((CHUNK, width), lambda j: (jnp.where(j == chunks, chunks, at(j)), 0)),
            full((8, conv_width)), full((8, LANES)),
        ],
        out_shape=[
            jax.ShapeDtypeStruct((rows + CHUNK, width), BF16),
            jax.ShapeDtypeStruct((8, conv_width), F32),
            jax.ShapeDtypeStruct((8, LANES), F32),
        ],
        scratch_shapes=[
            pltpu.VMEM((LANES, inner), F32),
            pltpu.VMEM((CHUNK + 8, conv_width), F32),
            pltpu.VMEM((CHUNK + 8, conv_width), F32),
            pltpu.VMEM((CHUNK, inner), F32),
            pltpu.VMEM((CHUNK, inner), F32),
            pltpu.VMEM((CHUNK, inner), BF16),
            pltpu.VMEM((CHUNK, inner), BF16),
            pltpu.VMEM((3 * CHUNK, inner), BF16),
            pltpu.VMEM((LANES, CHUNK), F32),
        ],
        compiler_params=pltpu.CompilerParams(vmem_limit_bytes=48 * 2**20),
        cost_estimate=pl.CostEstimate(
            flops=1600 * rows * inner, bytes_accessed=16 * rows * inner, transcendentals=0
        ),
        name="mix_back",
    )(x, bc, step, within, gm, state, proj, proj, proj, exit_grad, skip, taps, bias, rate_bias,
      decay)


def swap(value, axis, bit):
    size = lax.axis_size(axis)
    return lax.ppermute(value, axis, [(i, i ^ bit) for i in range(size)])


def bits_of(axis):
    size = lax.axis_size(axis)
    bits = []
    bit = 1
    while bit < size:
        bits.append(bit)
        bit *= 2
    return bits


def gather_dp(value):
    size = lax.axis_size("dp")
    stack = value
    pos = lax.axis_index("dp")
    done = []
    for bit in reversed(bits_of("dp")):
        other = swap(stack, "dp", bit)
        high = (pos & bit) != 0
        axis = len(done)
        stack = jnp.where(
            high, jnp.stack([other, stack], axis=axis), jnp.stack([stack, other], axis=axis)
        )
        done.append(bit)
    return stack.reshape(size * value.shape[0], value.shape[1])


def gather_tensor_cols(value):
    return lax.all_gather(value, "tensor", axis=1, tiled=True)


def scatter_dp(value):
    size = lax.axis_size("dp")
    rows = value.shape[0] // size
    pos = lax.axis_index("dp")
    stack = value.reshape(size, rows, value.shape[1])
    for bit in bits_of("dp"):
        mine = (pos & bit) != 0
        pairs = stack.reshape(stack.shape[0] // 2, 2, rows, value.shape[1])
        keep = jnp.where(mine, pairs[:, 1], pairs[:, 0])
        give = jnp.where(mine, pairs[:, 0], pairs[:, 1]).astype(BF16)
        stack = keep + swap(give, "dp", bit).astype(F32)
    return stack.reshape(rows, value.shape[1])


def sum_all(value):
    for axis in ("dp", "tensor"):
        for bit in bits_of(axis):
            value = value + swap(value, axis, bit)
    return value


def local(
    hidden, input_gain, proj_gate, proj_inner, proj_shared, proj_rate, conv_inner,
    conv_inner_bias, conv_shared, conv_shared_bias, rate_bias, decay_log, skip_gain,
    output_gain, proj_output, cotangent,
):
    tensor_size = lax.axis_size("tensor")
    tensor_pos = lax.axis_index("tensor")
    rows, features = hidden.shape
    heads = rate_bias.shape[0]
    inner = output_gain.shape[0]
    shared = conv_shared.shape[1]
    head_dim = inner // heads
    conv_width = inner + shared
    per_seq = SEQ_LEN // rows
    seq_pos = lax.rem(tensor_pos, per_seq)
    part = inner // tensor_size
    rate_part = heads // tensor_size
    forward = [(i, i + 1) for i in range(tensor_size - 1)]
    backward = [(i + 1, i) for i in range(tensor_size - 1)]

    small = jnp.concatenate([proj_shared, gather_tensor_cols(proj_rate)], axis=1)
    small = jnp.pad(small, ((0, 0), (0, LANES - heads)))
    first_w = jnp.concatenate([gather_tensor_cols(proj_inner), small], axis=1)
    first_w = gather_dp(first_w)
    gate_w = gather_dp(gather_tensor_cols(proj_gate))
    output_w = gather_dp(gather_tensor_cols(proj_output))

    rim = lax.ppermute(hidden[rows - RIM :], "tensor", forward)
    rim = jnp.where(seq_pos == 0, jnp.zeros_like(rim), rim)
    extended = jnp.pad(
        jnp.concatenate([hidden, rim], axis=0), ((0, CHUNK - RIM), (0, 0))
    ).astype(F32)
    gain_in = input_gain.astype(F32)
    root = lax.rsqrt(jnp.mean(extended * extended, axis=-1, keepdims=True) + EPS)
    normed = (extended * root * gain_in).astype(BF16)

    proj = mm(normed, first_w).astype(BF16)
    taps = jnp.concatenate([conv_inner, conv_shared], axis=1).astype(F32)
    bias = jnp.concatenate([conv_inner_bias, conv_shared_bias])[None].astype(F32)
    pad_heads = lambda v: jnp.pad(v, (0, LANES - heads))[None]
    rate_bias_row = pad_heads(rate_bias)
    decay_row = pad_heads(-jnp.exp(decay_log))
    skip_row = jnp.repeat(skip_gain, head_dim)[None]
    gain_row = output_gain[None].astype(F32)
    x, bc, step, within, final, total = mix_in(
        proj, rows, taps, bias, rate_bias_row, decay_row, inner, heads
    )
    whole = jnp.repeat(jnp.exp(total[0, :heads]), head_dim)[None]

    entry = jnp.zeros_like(final)
    for _ in range(per_seq - 1):
        sent = lax.ppermute((final + whole * entry).astype(BF16), "tensor", forward)
        entry = jnp.where(seq_pos == 0, 0.0, sent.astype(F32))

    gate = mm(normed[:rows], gate_w).astype(BF16)
    gon = mm(cotangent, output_w)
    out_normed, grad_mixed, grad_gate, states, grad_entry, out_sums = mix_out(
        x, bc, step, within, gate, gon, entry, skip_row, gain_row, heads
    )
    exit_grad = jnp.zeros_like(grad_entry)
    for _ in range(per_seq - 1):
        sent = lax.ppermute((grad_entry + whole * exit_grad).astype(BF16), "tensor", backward)
        exit_grad = jnp.where(seq_pos == per_seq - 1, 0.0, sent.astype(F32))

    output = (hidden.astype(F32) + mm(out_normed, output_w, NT)).astype(BF16)
    grad_out_w = scatter_dp(mm(cotangent, out_normed, TN))
    grad_gate_w = scatter_dp(mm(normed[:rows], grad_gate, TN))

    grad_proj, conv_sums, head_sums = mix_back(
        x, bc, step, within, grad_mixed, states, proj, exit_grad, skip_row, taps, bias,
        rate_bias_row, decay_row, heads,
    )
    grad_first_w = scatter_dp(mm(normed, grad_proj, TN))

    grad_ext = mm(grad_proj, first_w, NT)
    rim_grad = lax.ppermute(grad_ext[rows : rows + RIM], "tensor", backward)
    rim_grad = jnp.where(seq_pos == per_seq - 1, 0.0, rim_grad)
    grad_normed = grad_ext[:rows] + mm(grad_gate, gate_w, NT)
    grad_normed = grad_normed + jnp.pad(rim_grad, ((rows - RIM, 0), (0, 0)))
    unit = hidden.astype(F32) * root[:rows]
    scaled = grad_normed * gain_in
    grad_hidden = (
        cotangent.astype(F32)
        + root[:rows] * (scaled - unit * jnp.mean(scaled * unit, axis=-1, keepdims=True))
    ).astype(BF16)
    grad_gain_in = jnp.sum(grad_normed * unit, axis=0)

    def own_cols(value):
        return lax.psum_scatter(value, "tensor", scatter_dimension=1, tiled=True)

    grad_out_w = own_cols(grad_out_w)
    grad_gate_w = own_cols(grad_gate_w)
    grad_inner_w = own_cols(grad_first_w[:, :inner])
    grad_shared_w = lax.psum(grad_first_w[:, inner:conv_width], "tensor")
    grad_rate_w = own_cols(grad_first_w[:, conv_width : conv_width + heads])

    tail = jnp.concatenate(
        [
            conv_sums[:5, inner:].reshape(-1),
            head_sums[0, :heads],
            head_sums[1, :heads],
            jnp.sum(out_sums[1].reshape(heads, head_dim), axis=1),
            grad_gain_in,
        ]
    )
    packed = jnp.concatenate([conv_sums[:5, :inner].reshape(-1), out_sums[0], tail])
    packed = jnp.pad(packed, (0, -packed.shape[0] % 1024)).reshape(-1, LANES)
    packed = sum_all(packed).reshape(-1)
    sizes = [4 * inner, inner, inner, 4 * shared, shared, heads, heads, heads, features]
    pieces, at = [], 0
    for size in sizes:
        pieces.append(packed[at : at + size])
        at += size
    (g_conv, g_conv_bias, g_out_gain, g_conv_sh, g_conv_sh_bias, g_rate_bias, g_decay, g_skip,
     g_gain_in) = pieces
    return (
        output, grad_hidden, g_gain_in, grad_gate_w, grad_inner_w, grad_shared_w, grad_rate_w,
        g_conv.reshape(4, inner), g_conv_bias, g_conv_sh.reshape(4, shared), g_conv_sh_bias,
        g_rate_bias, g_decay, g_skip, g_out_gain, grad_out_w,
    )


def solution(mesh):
    tokens = P(("dp", "tensor"), None)
    weight = P("dp", "tensor")
    in_specs = (
        tokens, P(), weight, weight, P("dp", None), weight, P(), P(), P(), P(), P(), P(), P(),
        P(), weight, tokens,
    )
    out_specs = (
        tokens, tokens, P(), weight, weight, P("dp", None), weight, P(), P(), P(), P(), P(),
        P(), P(), P(), weight,
    )
    return jax.shard_map(local, mesh=mesh, in_specs=in_specs, out_specs=out_specs, check_vma=False)
```

```python
import functools

import jax
import jax.numpy as jnp
from jax import lax
from jax.experimental import pallas as pl
from jax.experimental.pallas import tpu as pltpu
from jax.sharding import PartitionSpec as P

SEQ_LEN = 2048
CHUNK = 128
RIM = 16
LANES = 128
EPS = 1e-05
F32 = jnp.float32
BF16 = jnp.bfloat16


def mm(left, right, contract=((1,), (0,))):
    return lax.dot_general(left, right, (contract, ((), ())), preferred_element_type=F32)


NT = ((1,), (1,))
TN = ((0,), (0,))


def split3(value):
    high = value.astype(BF16)
    rest = value - high.astype(F32)
    mid = rest.astype(BF16)
    return high, mid, (rest - mid.astype(F32)).astype(BF16)


def exact_left(ones, value):
    high, mid, low = split3(value)
    return mm(ones, high) + mm(ones, mid) + mm(ones, low)


def exact_right(value, ones):
    high, mid, low = split3(value)
    return mm(high, ones) + mm(mid, ones) + mm(low, ones)


def spread_matrix(heads, inner):
    head_dim = inner // heads
    row = lax.broadcasted_iota(jnp.int32, (LANES, inner), 0)
    col = lax.broadcasted_iota(jnp.int32, (LANES, inner), 1)
    return ((col >= row * head_dim) & (col < (row + 1) * head_dim)).astype(BF16)


def iota2(shape, dim):
    return lax.broadcasted_iota(jnp.int32, shape, dim)


def softplus(v):
    return jnp.maximum(v, 0.0) + jnp.log1p(jnp.exp(-jnp.abs(v)))


def conv_rows(ext_ref, taps, bias, lo, width, rows):
    total = bias
    for k in range(4):
        total = total + taps[k : k + 1, :] * ext_ref[pl.ds(5 + k, rows), pl.ds(lo, width)]
    return total


def spread_columns(target_ref, rows, block, inner):
    half, shared = inner // 2, 2 * LANES
    target_ref[rows, :half] = block[:, :half]
    target_ref[rows, half:inner] = block[:, half + shared + LANES :]
    target_ref[rows, inner:] = block[:, half : half + shared]


def column_of(lo, inner):
    half = inner // 2
    if lo >= inner:
        return lo - inner + half
    return lo if lo < half else lo + 3 * LANES


def mix_in_kernel(
    inner, heads,
    proj_ref, rim_ref, tap_ref, bias_ref, rate_bias_ref, decay_ref,
    x_ref, bc_ref, step_ref, within_ref, final_ref, total_ref,
    ext_ref, u_ref,
):
    i = pl.program_id(0)
    shared = 2 * LANES

    @pl.when(i == 0)
    def _():
        spread_columns(ext_ref, slice(0, 8), rim_ref[...].astype(F32)[RIM - 8 :], inner)
        final_ref[...] = jnp.zeros_like(final_ref)
        total_ref[...] = jnp.zeros_like(total_ref)

    @pl.when(i > 0)
    def _():
        ext_ref[0:8, :] = ext_ref[CHUNK : CHUNK + 8, :]

    spread_columns(ext_ref, slice(8, CHUNK + 8), proj_ref[...].astype(F32), inner)
    at = inner // 2 + shared
    step = softplus(proj_ref[:, at : at + LANES].astype(F32) + rate_bias_ref[...])
    log_decay = step * decay_ref[...]
    lower = (iota2((CHUNK, CHUNK), 0) >= iota2((CHUNK, CHUNK), 1)).astype(BF16)
    within = exact_left(lower, log_decay)
    step_ref[...] = step
    within_ref[...] = within
    last = within[CHUNK - 1 :, :]
    total_ref[...] += last
    weight = step * jnp.exp(last - within)

    pre = conv_rows(ext_ref, tap_ref[:, inner:], bias_ref[:, inner:], inner, shared, CHUNK)
    bc = (pre * jax.nn.sigmoid(pre)).astype(BF16)
    bc_ref[...] = bc
    first = iota2((CHUNK, LANES), 1) < LANES // 2
    for p in range(inner // LANES):
        lo = p * LANES
        pre = conv_rows(
            ext_ref, tap_ref[:, lo : lo + LANES], bias_ref[:, lo : lo + LANES], lo, LANES, CHUNK
        )
        x = (pre * jax.nn.sigmoid(pre)).astype(BF16)
        x_ref[:, lo : lo + LANES] = x
        w = jnp.where(
            first,
            jnp.broadcast_to(weight[:, 2 * p : 2 * p + 1], (CHUNK, LANES)),
            jnp.broadcast_to(weight[:, 2 * p + 1 : 2 * p + 2], (CHUNK, LANES)),
        )
        u_ref[:, lo : lo + LANES] = (x.astype(F32) * w).astype(BF16)
    factor = exact_right(jnp.exp(jnp.broadcast_to(last, (8, LANES))), spread_matrix(heads, inner))
    final_ref[...] = factor[0:1, :] * final_ref[...] + mm(bc[:, :LANES], u_ref[...], TN)


def mix_in(proj, rows, taps, bias, rate_bias, decay, inner, heads):
    width = proj.shape[1]
    chunks = rows // CHUNK
    full = lambda shape: pl.BlockSpec(shape, lambda i: (0,) * len(shape))
    return pl.pallas_call(
        functools.partial(mix_in_kernel, inner, heads),
        grid=(chunks,),
        in_specs=[
            pl.BlockSpec((CHUNK, width), lambda i: (i, 0)),
            pl.BlockSpec((RIM, width), lambda i: (rows // RIM, 0)),
            full(taps.shape), full(bias.shape), full(rate_bias.shape), full(decay.shape),
        ],
        out_specs=[
            pl.BlockSpec((CHUNK, inner), lambda i: (i, 0)),
            pl.BlockSpec((CHUNK, 2 * LANES), lambda i: (i, 0)),
            pl.BlockSpec((CHUNK, LANES), lambda i: (i, 0)),
            pl.BlockSpec((CHUNK, LANES), lambda i: (i, 0)),
            full((LANES, inner)),
            full((1, LANES)),
        ],
        out_shape=[
            jax.ShapeDtypeStruct((rows, inner), BF16),
            jax.ShapeDtypeStruct((rows, 2 * LANES), BF16),
            jax.ShapeDtypeStruct((rows, LANES), F32),
            jax.ShapeDtypeStruct((rows, LANES), F32),
            jax.ShapeDtypeStruct((LANES, inner), F32),
            jax.ShapeDtypeStruct((1, LANES), F32),
        ],
        scratch_shapes=[
            pltpu.VMEM((CHUNK + 8, inner + 2 * LANES), F32),
            pltpu.VMEM((CHUNK, inner), BF16),
        ],
        compiler_params=pltpu.CompilerParams(vmem_limit_bytes=48 * 2**20),
        cost_estimate=pl.CostEstimate(
            flops=11000 * rows * inner, bytes_accessed=6 * rows * inner, transcendentals=0
        ),
        name="mix_in",
    )(proj, proj, taps, bias, rate_bias, decay)


def mix_out_kernel(
    inner, heads,
    x_ref, bc_ref, step_ref, within_ref, gate_ref, gon_ref, entry_ref, skip_ref, gain_ref,
    normed_ref, gm_ref, gg_ref, state_ref, grad_entry_ref, sums_ref,
    hold_ref, y_ref, u_ref, prefix_ref,
):
    i = pl.program_id(0)

    @pl.when(i == 0)
    def _():
        hold_ref[...] = entry_ref[...].astype(F32)
        grad_entry_ref[...] = jnp.zeros_like(grad_entry_ref)
        sums_ref[...] = jnp.zeros_like(sums_ref)
        prefix_ref[...] = jnp.zeros_like(prefix_ref)

    spread = spread_matrix(heads, inner)
    key, query = bc_ref[:, :LANES], bc_ref[:, LANES:]
    within = within_ref[...]
    within_t = within.T
    last = within[CHUNK - 1 :, :]
    state = hold_ref[...].astype(BF16)
    state_ref[0] = state
    y_ref[...] = mm(query, state)
    scores = mm(query, key, NT)
    causal = iota2((CHUNK, CHUNK), 0) >= iota2((CHUNK, CHUNK), 1)
    first = iota2((CHUNK, LANES), 1) < LANES // 2
    zero = jnp.zeros((CHUNK, LANES), BF16)
    for p in range(inner // LANES):
        lo = p * LANES
        slab = slice(lo, lo + LANES)
        cols, weights = [], []
        for h in (2 * p, 2 * p + 1):
            col = jnp.broadcast_to(within[:, h : h + 1], (CHUNK, CHUNK))
            gap = jnp.where(causal, col - within_t[h : h + 1, :], -1e30)
            weights.append((scores * jnp.exp(gap)).astype(BF16))
            cols.append(col)
        a = jnp.where(first, cols[0], cols[1])
        d = jnp.where(
            first,
            jnp.broadcast_to(step_ref[:, 2 * p : 2 * p + 1], (CHUNK, LANES)),
            jnp.broadcast_to(step_ref[:, 2 * p + 1 : 2 * p + 2], (CHUNK, LANES)),
        )
        x = x_ref[:, slab].astype(F32)
        u = x * d
        ub = u.astype(BF16)
        u_ref[:, slab] = (u * jnp.exp(a[CHUNK - 1 :, :] - a)).astype(BF16)
        diagonal = mm(
            jnp.concatenate(weights, axis=1),
            jnp.concatenate([jnp.where(first, ub, zero), jnp.where(first, zero, ub)], axis=0),
        )
        y_ref[:, slab] = diagonal + jnp.exp(a) * y_ref[:, slab] + skip_ref[:, slab] * x
    factors = exact_right(
        jnp.exp(jnp.concatenate([last, prefix_ref[...], jnp.zeros((6, LANES), F32)], axis=0)),
        spread,
    )
    prefix_ref[...] += last
    hold_ref[...] = factors[0:1, :] * hold_ref[...] + mm(key, u_ref[...], TN)

    square = jnp.zeros((CHUNK, LANES), F32)
    dot = jnp.zeros((CHUNK, LANES), F32)
    for p in range(inner // LANES):
        slab = slice(p * LANES, (p + 1) * LANES)
        z = gate_ref[:, slab].astype(F32)
        m = y_ref[:, slab].astype(BF16).astype(F32)
        gated = m * (z * jax.nn.sigmoid(z))
        square = square + gated * gated
        dot = dot + gain_ref[:, slab] * gon_ref[:, slab].astype(F32) * gated
    square = jnp.sum(square, axis=1, keepdims=True)
    dot = jnp.sum(dot, axis=1, keepdims=True)
    root = lax.rsqrt(square / inner + EPS)
    pull = root * root * root * dot / inner
    for p in range(inner // LANES):
        slab = slice(p * LANES, (p + 1) * LANES)
        z = gate_ref[:, slab].astype(F32)
        m = y_ref[:, slab].astype(BF16).astype(F32)
        sig = jax.nn.sigmoid(z)
        act = z * sig
        gated = m * act
        gon = gon_ref[:, slab].astype(F32)
        unit = gated * root
        normed_ref[:, slab] = (unit * gain_ref[:, slab]).astype(BF16)
        grad = root * gain_ref[:, slab] * gon - gated * pull
        gm = (grad * act).astype(BF16)
        gm_ref[:, slab] = gm
        gg_ref[:, slab] = (grad * m * (sig * (1.0 + z * (1.0 - sig)))).astype(BF16)
        gmf = gm.astype(F32)
        sums_ref[0:1, slab] += jnp.sum(gon * unit, axis=0, keepdims=True)
        sums_ref[1:2, slab] += jnp.sum(gmf * x_ref[:, slab].astype(F32), axis=0, keepdims=True)
        a = jnp.where(
            first,
            jnp.broadcast_to(within[:, 2 * p : 2 * p + 1], (CHUNK, LANES)),
            jnp.broadcast_to(within[:, 2 * p + 1 : 2 * p + 2], (CHUNK, LANES)),
        )
        u_ref[:, slab] = (gmf * jnp.exp(a)).astype(BF16)
    grad_entry_ref[...] += factors[1:2, :] * mm(query, u_ref[...], TN)


def mix_out(x, bc, step, within, gate, gon, entry, skip, gain, heads):
    rows, inner = x.shape
    chunks = rows // CHUNK
    full = lambda shape: pl.BlockSpec(shape, lambda i: (0,) * len(shape))
    block = lambda width: pl.BlockSpec((CHUNK, width), lambda i: (i, 0))
    return pl.pallas_call(
        functools.partial(mix_out_kernel, inner, heads),
        grid=(chunks,),
        in_specs=[
            block(inner), block(2 * LANES), block(LANES), block(LANES), block(inner), block(inner),
            full(entry.shape), full(skip.shape), full(gain.shape),
        ],
        out_specs=[
            block(inner), block(inner), block(inner),
            pl.BlockSpec((1, LANES, inner), lambda i: (i, 0, 0)),
            full((LANES, inner)), full((8, inner)),
        ],
        out_shape=[
            jax.ShapeDtypeStruct((rows, inner), BF16),
            jax.ShapeDtypeStruct((rows, inner), BF16),
            jax.ShapeDtypeStruct((rows, inner), BF16),
            jax.ShapeDtypeStruct((chunks, LANES, inner), BF16),
            jax.ShapeDtypeStruct((LANES, inner), F32),
            jax.ShapeDtypeStruct((8, inner), F32),
        ],
        scratch_shapes=[
            pltpu.VMEM((LANES, inner), F32),
            pltpu.VMEM((CHUNK, inner), F32),
            pltpu.VMEM((CHUNK, inner), BF16),
            pltpu.VMEM((1, LANES), F32),
        ],
        compiler_params=pltpu.CompilerParams(vmem_limit_bytes=48 * 2**20),
        cost_estimate=pl.CostEstimate(
            flops=17000 * rows * inner, bytes_accessed=16 * rows * inner, transcendentals=0
        ),
        name="mix_out",
    )(x, bc, step, within, gate, gon, entry, skip, gain)


def mix_back_kernel(
    inner, heads, top, count, inside, rim_step,
    x_ref, bc_ref, step_ref, within_ref, gm_ref, state_ref, proj_ref, prev_ref, rim_ref,
    exit_ref, next_ref, sums_in_ref, heads_in_ref,
    skip_ref, tap_ref, bias_ref, rate_bias_ref, decay_ref,
    *rest,
):
    if inside:
        rest = rest[1:]
    (
        gproj_ref, hold_ref, head_ref, sums_ref, heads_ref,
        ext_ref, ahead_ref, cs_ref, bg_ref, ue_ref, ge_ref, prod_ref, rows_ref,
    ) = rest
    j = pl.program_id(0)
    i = top - j
    shared = 2 * LANES
    conv_width = inner + shared

    @pl.when(j == 0)
    def _():
        hold_ref[...] = exit_ref[...].astype(F32)
        sums_ref[...] = sums_in_ref[...]
        heads_ref[...] = heads_in_ref[...]
        ahead_ref[CHUNK:, :] = next_ref[...]
        rows_ref[...] = jnp.zeros_like(rows_ref)

    @pl.when((j > 0) & (j < count))
    def _():
        ahead_ref[CHUNK:, :] = ahead_ref[0:8, :]

    @pl.when(j < count)
    def _():
        before = jnp.where(i == 0, rim_ref[...].astype(F32), prev_ref[...].astype(F32))
        spread_columns(ext_ref, slice(0, 8), before[RIM - 8 :], inner)
        spread_columns(ext_ref, slice(8, CHUNK + 8), proj_ref[...].astype(F32), inner)
        spread = spread_matrix(heads, inner)
        key, query = bc_ref[:, :LANES], bc_ref[:, LANES:]
        within = within_ref[...]
        within_t = within.T
        step = step_ref[...]
        last = within[CHUNK - 1 :, :]
        state = state_ref[0]
        hold = hold_ref[...]
        exit_grad = hold.astype(BF16)
        cs_ref[...] = mm(query, state)
        bg_ref[...] = mm(key, exit_grad)
        scores_t = mm(key, query, NT)
        causal_t = iota2((CHUNK, CHUNK), 0) <= iota2((CHUNK, CHUNK), 1)
        first = iota2((CHUNK, LANES), 1) < LANES // 2
        lane = iota2((2 * CHUNK, LANES), 1)
        upper_half = iota2((2 * CHUNK, LANES), 0) >= CHUNK
        zero = jnp.zeros((CHUNK, LANES), BF16)
        grad_scores_t = jnp.zeros((CHUNK, CHUNK), F32)
        col_sums = jnp.zeros((CHUNK, LANES), F32)
        for p in range(inner // LANES):
            slab = slice(p * LANES, (p + 1) * LANES)
            x = x_ref[:, slab].astype(F32)
            gb = gm_ref[:, slab]
            g = gb.astype(F32)
            cols = [
                jnp.broadcast_to(within[:, h : h + 1], (CHUNK, LANES)) for h in (2 * p, 2 * p + 1)
            ]
            a = jnp.where(first, cols[0], cols[1])
            d = jnp.where(
                first,
                jnp.broadcast_to(step[:, 2 * p : 2 * p + 1], (CHUNK, LANES)),
                jnp.broadcast_to(step[:, 2 * p + 1 : 2 * p + 2], (CHUNK, LANES)),
            )
            u = x * d
            ub = u.astype(BF16)
            to_end = jnp.exp(a[CHUNK - 1 :, :] - a)
            ge = g * jnp.exp(a)
            ge_ref[:, slab] = ge.astype(BF16)
            ue_ref[:, slab] = (u * to_end).astype(BF16)
            gcat = jnp.concatenate([jnp.where(first, gb, zero), jnp.where(first, zero, gb)], axis=0)
            reach_t = mm(ub, gcat, NT)
            pieces, moves = [], []
            for q, h in enumerate((2 * p, 2 * p + 1)):
                gap = jnp.where(causal_t, within_t[h : h + 1, :] - cols[q], -1e30)
                weight = jnp.exp(gap)
                grad_score = reach_t[:, q * CHUNK : (q + 1) * CHUNK] * weight
                grad_scores_t = grad_scores_t + grad_score
                pieces.append((scores_t * weight).astype(BF16))
                move = (grad_score * scores_t).astype(BF16)
                moves.append(move)
                rows_ref[h : h + 1, :] = jnp.sum(move.astype(F32), axis=0, keepdims=True)
            pick = (lane == jnp.where(upper_half, 2 * p + 1, 2 * p)).astype(BF16)
            col_sums = col_sums + mm(jnp.concatenate(moves, axis=1), pick)
            grad_state_u = to_end * bg_ref[:, slab]
            grad_u = mm(jnp.concatenate(pieces, axis=1), gcat) + grad_state_u
            prod_ref[0:CHUNK, slab] = (x * grad_u).astype(BF16)
            prod_ref[CHUNK : 2 * CHUNK, slab] = (u * grad_state_u).astype(BF16)
            prod_ref[2 * CHUNK :, slab] = (ge * cs_ref[:, slab]).astype(BF16)
            grad_x = d * grad_u + skip_ref[:, slab] * g
            pre = conv_rows(ext_ref, tap_ref[:, slab], bias_ref[:, slab], p * LANES, LANES, CHUNK)
            sig = jax.nn.sigmoid(pre)
            ahead_ref[0:CHUNK, slab] = grad_x * (sig * (1.0 + pre * (1.0 - sig)))

        by_head = mm(prod_ref[...], spread, NT)
        grad_step = by_head[0:CHUNK]
        from_state = by_head[CHUNK : 2 * CHUNK]
        from_entry = by_head[2 * CHUNK :]
        factor = exact_right(jnp.exp(jnp.broadcast_to(last, (8, LANES))), spread)[0:1, :]
        whole = jnp.sum(hold * state.astype(F32), axis=0, keepdims=True) * factor
        whole = jnp.broadcast_to(whole, (8, inner))
        high, mid, _ = split3(whole)
        whole = (mm(high, spread, NT) + mm(mid, spread, NT))[0:1, :]
        later = (iota2((CHUNK, CHUNK), 0) <= iota2((CHUNK, CHUNK), 1)).astype(BF16)
        earlier = (iota2((CHUNK, CHUNK), 0) > iota2((CHUNK, CHUNK), 1)).astype(BF16)
        row_sums = rows_ref[...].T
        grad_log = (
            exact_left(later, row_sums - col_sums + from_entry)
            + exact_left(earlier, from_state)
            + whole
        )
        decay = decay_ref[...]
        grad_step = grad_step + grad_log * decay
        rates = slice(inner // 2 + shared, inner // 2 + shared + LANES)
        squash = jax.nn.sigmoid(proj_ref[:, rates].astype(F32) + rate_bias_ref[...])
        grad_rate = grad_step * squash
        gproj_ref[:, rates] = grad_rate.astype(BF16)
        heads_ref[0:1, :] += jnp.sum(grad_rate, axis=0, keepdims=True)
        heads_ref[1:2, :] += jnp.sum(grad_log * step, axis=0, keepdims=True) * decay

        gsb = grad_scores_t.astype(BF16)
        grad_key = mm(ue_ref[...], exit_grad, NT) + mm(gsb, query)
        grad_query = mm(ge_ref[...], state, NT) + mm(gsb, key, TN)
        hold_ref[...] = factor * hold + mm(query, ge_ref[...], TN)

        pre = conv_rows(ext_ref, tap_ref[:, inner:], bias_ref[:, inner:], inner, shared, CHUNK)
        sig = jax.nn.sigmoid(pre)
        slope = sig * (1.0 + pre * (1.0 - sig))
        ahead_ref[0:CHUNK, inner:] = jnp.concatenate([grad_key, grad_query], axis=1) * slope

        for p in range(conv_width // LANES):
            slab = slice(p * LANES, (p + 1) * LANES)
            values = ext_ref[8:, slab]
            total = jnp.zeros((CHUNK, LANES), F32)
            for k in range(4):
                moved = ahead_ref[pl.ds(3 - k, CHUNK), slab]
                total = total + tap_ref[k : k + 1, slab] * moved
                sums_ref[k : k + 1, slab] += jnp.sum(values * moved, axis=0, keepdims=True)
                if k == 3:
                    sums_ref[4:5, slab] += jnp.sum(moved, axis=0, keepdims=True)
            lo = column_of(p * LANES, inner)
            gproj_ref[:, lo : lo + LANES] = total.astype(BF16)
        head_ref[...] = ahead_ref[0:8, :]

    if not rim_step:
        return

    @pl.when(j == count)
    def _():
        gproj_ref[...] = jnp.zeros_like(gproj_ref)
        head = ahead_ref[0:8, :]
        at = iota2((8, conv_width), 0)
        spread_columns(ext_ref, slice(0, 8), rim_ref[...].astype(F32)[RIM - 8 :], inner)
        values = ext_ref[0:8, :]
        total = jnp.zeros((8, conv_width), F32)
        for k in range(3):
            moved = jnp.zeros((8, conv_width), F32)
            for r in range(5 + k, 8):
                t = r - 5 - k
                moved = moved + jnp.where(at == r, head[t : t + 1, :], 0.0)
            total = total + tap_ref[k : k + 1, :] * moved
            sums_ref[k : k + 1, :] += jnp.sum(values * moved, axis=0, keepdims=True)
        total = jnp.concatenate([jnp.zeros((RIM - 8, conv_width), F32), total], axis=0)
        total = total.astype(BF16)
        half = inner // 2
        gproj_ref[0:RIM, :half] = total[:, :half]
        gproj_ref[0:RIM, half : half + shared] = total[:, inner:]
        gproj_ref[0:RIM, half + shared + LANES :] = total[:, half:inner]


def mix_back(x, bc, step, within, gm, state, proj, carried, consts, heads, top, count, gproj,
             rim_step):
    inside = gproj is not None
    rows, inner = x.shape
    width = proj.shape[1]
    chunks = rows // CHUNK
    per = CHUNK // RIM
    conv_width = inner + 2 * LANES
    full = lambda shape: pl.BlockSpec(shape, lambda j: (0,) * len(shape))
    at = lambda j: jnp.maximum(top - j, top - count + 1)
    block = lambda w: pl.BlockSpec((CHUNK, w), lambda j: (at(j), 0))
    operands = [x, bc, step, within, gm, state, proj, proj, proj, *carried, *consts]
    in_specs = [
        block(inner), block(2 * LANES), block(LANES), block(LANES), block(inner),
        pl.BlockSpec((1, LANES, inner), lambda j: (at(j), 0, 0)),
        block(width),
        pl.BlockSpec((RIM, width), lambda j: (jnp.maximum(at(j) * per - 1, 0), 0)),
        pl.BlockSpec((RIM, width), lambda j: (rows // RIM, 0)),
        *[full(v.shape) for v in (*carried, *consts)],
    ]
    if inside:
        operands.append(gproj)
        in_specs.append(pl.BlockSpec(memory_space=pl.ANY))
    return pl.pallas_call(
        functools.partial(mix_back_kernel, inner, heads, top, count, inside, rim_step),
        grid=(count + 1 if rim_step else count,),
        in_specs=in_specs,
        out_specs=[
            pl.BlockSpec((CHUNK, width), lambda j: (jnp.where(j == count, chunks, at(j)), 0)),
            full((LANES, inner)), full((8, conv_width)), full((8, conv_width)), full((8, LANES)),
        ],
        out_shape=[
            jax.ShapeDtypeStruct((rows + CHUNK, width), BF16),
            jax.ShapeDtypeStruct((LANES, inner), F32),
            jax.ShapeDtypeStruct((8, conv_width), F32),
            jax.ShapeDtypeStruct((8, conv_width), F32),
            jax.ShapeDtypeStruct((8, LANES), F32),
        ],
        scratch_shapes=[
            pltpu.VMEM((CHUNK + 8, conv_width), F32),
            pltpu.VMEM((CHUNK + 8, conv_width), F32),
            pltpu.VMEM((CHUNK, inner), F32),
            pltpu.VMEM((CHUNK, inner), F32),
            pltpu.VMEM((CHUNK, inner), BF16),
            pltpu.VMEM((CHUNK, inner), BF16),
            pltpu.VMEM((3 * CHUNK, inner), BF16),
            pltpu.VMEM((LANES, CHUNK), F32),
        ],
        input_output_aliases={len(operands) - 1: 0} if inside else {},
        compiler_params=pltpu.CompilerParams(vmem_limit_bytes=48 * 2**20),
        cost_estimate=pl.CostEstimate(
            flops=32768 * count * CHUNK * inner, bytes_accessed=16 * count * CHUNK * inner,
            transcendentals=0,
        ),
        name="mix_back",
    )(*operands)


def swap(value, axis, bit):
    size = lax.axis_size(axis)
    return lax.ppermute(value, axis, [(i, i ^ bit) for i in range(size)])


def bits_of(axis):
    size = lax.axis_size(axis)
    return [1 << k for k in range(size.bit_length() - 1)]


def join(value, axis, bit, dim):
    other = swap(value, axis, bit)
    high = (lax.axis_index(axis) & bit) != 0
    return jnp.where(high, jnp.stack([other, value], axis=dim), jnp.stack([value, other], axis=dim))


def join_cols(value):
    for bit in bits_of("tensor"):
        other = swap(value, "tensor", bit)
        high = (lax.axis_index("tensor") & bit) != 0
        value = jnp.where(
            high,
            jnp.concatenate([other, value], axis=-1),
            jnp.concatenate([value, other], axis=-1),
        )
    return value


def join_dp(stack, bits, done):
    for bit in bits:
        stack = join(stack, "dp", bit, done)
        done += 1
    return stack


def side(axis, bit):
    return jnp.where((lax.axis_index(axis) & bit) != 0, 1, 0)


def fold_rows(value, bit, dim=0):
    mine = side("dp", bit)
    shape = value.shape
    pairs = value.reshape(*shape[:dim], shape[dim] // 2, 2, *shape[dim + 1 :])
    pick = lambda k: lax.dynamic_index_in_dim(pairs, k, dim + 1, keepdims=False)
    return pick(mine), pick(1 - mine)


def fold_cols(value, bit, rest=0):
    high = side("tensor", bit) == 1
    half = (value.shape[-1] - rest) // 2
    low_part, high_part = value[..., : half + rest], value[..., half:]
    return jnp.where(high, high_part, low_part), jnp.where(high, low_part, high_part)


def plus(keep, got):
    return (keep.astype(F32) + got.astype(F32)).astype(BF16)


def in_order(value, rest):
    high = side("tensor", lax.axis_size("tensor") // 2) == 1
    half = value.shape[-1] - rest
    turned = jnp.concatenate([value[..., rest:], value[..., :rest]], axis=-1)
    return jnp.where(high, turned, value)


def more_cols(value, rest=0):
    bits = bits_of("tensor")[-2::-1]
    if not bits:
        return value
    if rest:
        value = in_order(value, rest)
    for bit in bits:
        width = value.shape[-1] - rest
        keep, give = fold_cols(value[..., :width], bit)
        tail = value[..., width:]
        give = jnp.concatenate([give, tail], axis=-1)
        value = plus(jnp.concatenate([keep, tail], axis=-1), swap(give, "tensor", bit))
    return value


def local(
    hidden, input_gain, proj_gate, proj_inner, proj_shared, proj_rate, conv_inner,
    conv_inner_bias, conv_shared, conv_shared_bias, rate_bias, decay_log, skip_gain,
    output_gain, proj_output, cotangent,
):
    tensor_size = lax.axis_size("tensor")
    tensor_pos = lax.axis_index("tensor")
    rows, features = hidden.shape
    heads = rate_bias.shape[0]
    inner = output_gain.shape[0]
    shared = conv_shared.shape[1]
    head_dim = inner // heads
    conv_width = inner + shared
    per_seq = SEQ_LEN // rows
    seq_pos = lax.rem(tensor_pos, per_seq)
    part = inner // tensor_size
    rate_part = heads // tensor_size
    forward = [(i, i + 1) for i in range(tensor_size - 1)]
    backward = [(i + 1, i) for i in range(tensor_size - 1)]

    dp_bits = bits_of("dp")
    far, near = dp_bits[:0:-1], dp_bits[:1]
    dp_size, part_rows = lax.axis_size("dp"), proj_inner.shape[0]
    early = jnp.concatenate(
        [proj_inner, jnp.pad(proj_rate, ((0, 0), (0, LANES - rate_part)))], axis=1
    )
    early = [early]
    for bit in bits_of("tensor"):
        high = (tensor_pos & bit) != 0
        other = [swap(jnp.concatenate(early, axis=1), "tensor", bit)]
        size = early[0].shape[1]
        other = [other[0][:, k * size : (k + 1) * size] for k in range(len(early))]
        early = [jnp.where(high, o, e) for o, e in zip(other, early)] + [
            jnp.where(high, e, o) for o, e in zip(other, early)
        ]
    rate_cols = [e[:, part : part + rate_part] for e in early]
    inner_cols = [e[:, :part] for e in early]
    first_w = jnp.concatenate(
        inner_cols[: tensor_size // 2]
        + [proj_shared, *rate_cols, jnp.zeros((part_rows, LANES - heads), BF16)]
        + inner_cols[tensor_size // 2 :],
        axis=1,
    )
    far_z, far_x = far[:-1], far[-1:]
    first_w = join_dp(first_w, far_z, 0)
    first_w, output_w, gate_w = lax.optimization_barrier((first_w, proj_output, proj_gate))
    first_w = join_dp(first_w, far_x, len(far_z))
    gate_w = join_dp(gate_w, far_z, 0)
    output_w = join_dp(output_w, far_z, 0)
    first_w, gate_w, output_w = lax.optimization_barrier((first_w, gate_w, output_w))
    first_w = join_dp(first_w, near, len(far)).reshape(dp_size * part_rows, -1)
    gate_w = join_dp(gate_w, far_x, len(far_z))
    output_w = join_cols(output_w)

    rim = lax.ppermute(hidden[rows - RIM :], "tensor", forward)
    rim = jnp.where(seq_pos == 0, jnp.zeros_like(rim), rim)
    extended = jnp.pad(
        jnp.concatenate([hidden, rim], axis=0), ((0, CHUNK - RIM), (0, 0))
    ).astype(F32)
    gain_in = input_gain.astype(F32)
    root = lax.rsqrt(jnp.mean(extended * extended, axis=-1, keepdims=True) + EPS)
    normed = (extended * root * gain_in).astype(BF16)

    proj = mm(normed, first_w).astype(BF16)
    proj, gate_w, output_w = lax.optimization_barrier((proj, gate_w, output_w))
    gate_w = join_cols(gate_w)
    output_w = join_dp(output_w, far_x, len(far_z))
    taps = jnp.concatenate([conv_inner, conv_shared], axis=1).astype(F32)
    bias = jnp.concatenate([conv_inner_bias, conv_shared_bias])[None].astype(F32)
    pad_heads = lambda v: jnp.pad(v, (0, LANES - heads))[None]
    rate_bias_row = pad_heads(rate_bias)
    decay_row = pad_heads(-jnp.exp(decay_log))
    skip_row = jnp.repeat(skip_gain, head_dim)[None]
    gain_row = output_gain[None].astype(F32)
    x, bc, step, within, final, total = mix_in(
        proj, rows, taps, bias, rate_bias_row, decay_row, inner, heads
    )
    whole = jnp.repeat(jnp.exp(total[0, :heads]), head_dim)[None]
    final, gate_w, output_w = lax.optimization_barrier((final, gate_w, output_w))
    gate_w = join_dp(gate_w, near, len(far)).reshape(dp_size * part_rows, inner)
    output_w = join_dp(output_w, near, len(far)).reshape(dp_size * part_rows, inner)

    entry = jnp.zeros_like(final)
    for _ in range(per_seq - 1):
        sent = lax.ppermute((final + whole * entry).astype(BF16), "tensor", forward)
        entry = jnp.where(seq_pos == 0, 0.0, sent.astype(F32))

    gate = mm(normed[:rows], gate_w).astype(BF16)
    gon = mm(cotangent, output_w).astype(BF16)
    out_normed, grad_mixed, grad_gate, states, grad_entry, out_sums = mix_out(
        x, bc, step, within, gate, gon, entry, skip_row, gain_row, heads
    )
    exit_grad = jnp.zeros_like(grad_entry)
    for _ in range(per_seq - 1):
        sent = lax.ppermute((grad_entry + whole * exit_grad).astype(BF16), "tensor", backward)
        exit_grad = jnp.where(seq_pos == per_seq - 1, 0.0, sent.astype(F32))

    core, cross, long = dp_bits[0], dp_bits[1], dp_bits[2:]
    tensor_top = bits_of("tensor")[-1]
    blocks = lambda v: v.astype(BF16).reshape(dp_size, part_rows, -1)
    grad_out_w = blocks(mm(cotangent, out_normed, TN))
    grad_gate_w = blocks(mm(normed[:rows], grad_gate, TN))
    keep_o, give_o = fold_rows(grad_out_w, core)
    keep_g, give_g = fold_rows(grad_gate_w, core)
    exit_grad, give_o, give_g = lax.optimization_barrier((exit_grad, give_o, give_g))
    got_o, got_g = swap(give_o, "dp", core), swap(give_g, "dp", core)

    consts = [skip_row, taps, bias, rate_bias_row, decay_row]
    chunks = rows // CHUNK
    counts = [chunks // 4, (chunks - chunks // 4) // 2]
    counts.append(chunks - sum(counts))
    tops = [chunks - 1, chunks - 1 - counts[0], counts[2] - 1]
    carried = [
        exit_grad, jnp.zeros((8, conv_width), F32), jnp.zeros((8, conv_width), F32),
        jnp.zeros((8, LANES), F32),
    ]
    back = lambda k, *more: mix_back(
        x, bc, step, within, grad_mixed, states, proj, carried, consts, heads, tops[k], counts[k],
        *more,
    )
    grad_proj, *carried = back(0, None, False)
    grad_proj, got_g, got_o = lax.optimization_barrier((grad_proj, got_g, got_o))
    keep_g, give_g = fold_rows(plus(keep_g, got_g), cross)
    keep_o, give_o = fold_cols(plus(keep_o, got_o), tensor_top)
    grad_proj, give_g, give_o = lax.optimization_barrier((grad_proj, give_g, give_o))
    got_g, got_o = swap(give_g, "dp", cross), swap(give_o, "tensor", tensor_top)
    grad_proj, *carried = back(1, grad_proj, False)
    grad_proj, got_g, got_o = lax.optimization_barrier((grad_proj, got_g, got_o))
    keep_g, give_g = fold_cols(plus(keep_g, got_g), tensor_top)
    keep_o, give_o = fold_rows(more_cols(plus(keep_o, got_o)), cross)
    grad_proj, give_g, give_o = lax.optimization_barrier((grad_proj, give_g, give_o))
    got_g, got_o = swap(give_g, "tensor", tensor_top), swap(give_o, "dp", cross)
    grad_proj, _, _, conv_sums, head_sums = back(2, grad_proj, True)
    grad_proj, got_g, got_o = lax.optimization_barrier((grad_proj, got_g, got_o))

    rest = shared + LANES
    first = blocks(mm(normed, grad_proj, TN))
    keep, give = fold_rows(first, core)
    grad_proj, give = lax.optimization_barrier((grad_proj, give))
    got = swap(give, "dp", core)
    grad_ext = mm(grad_proj, first_w, NT)
    grad_ext, got = lax.optimization_barrier((grad_ext, got))
    first = plus(keep, got)
    first = first.reshape(first.shape[0] // 4, 2, 2, part_rows, first.shape[-1])
    pick = lambda v, k: lax.dynamic_index_in_dim(v, k, 1, keepdims=False)
    on_x = side("dp", cross)
    left, right = first[:, 1], first[:, 0]
    keep_l, give_l = pick(left, on_x), pick(left, 1 - on_x)
    keep_r, give_r = fold_cols(right, tensor_top, rest)
    give_l, give_r, grad_ext, grad_gate, got_o = lax.optimization_barrier(
        (give_l, give_r, grad_ext, grad_gate, got_o)
    )
    got_l, got_r = swap(give_l, "dp", cross), swap(give_r, "tensor", tensor_top)
    gate_back = mm(grad_gate, gate_w, NT)
    pair = jnp.stack([more_cols(plus(keep_g, got_g)), plus(keep_o, got_o)])
    keep_p, give_p = fold_rows(pair, long[0], 1)
    got_p = swap(give_p, "dp", long[0])
    rim_grad = lax.ppermute(grad_ext[rows : rows + RIM], "tensor", backward)
    rim_grad = jnp.where(seq_pos == per_seq - 1, 0.0, rim_grad)
    grad_normed = grad_ext[:rows] + gate_back
    grad_normed = grad_normed + jnp.pad(rim_grad, ((rows - RIM, 0), (0, 0)))
    unit = hidden.astype(F32) * root[:rows]
    scaled = grad_normed * gain_in
    grad_hidden = (
        cotangent.astype(F32)
        + root[:rows] * (scaled - unit * jnp.mean(scaled * unit, axis=-1, keepdims=True))
    ).astype(BF16)
    grad_gain_in = jnp.sum(grad_normed * unit, axis=0)

    tail = jnp.concatenate(
        [
            conv_sums[:5, inner:].reshape(-1),
            head_sums[0, :heads],
            head_sums[1, :heads],
            jnp.sum(out_sums[1].reshape(heads, head_dim), axis=1),
            grad_gain_in,
        ]
    )
    packed = jnp.concatenate([conv_sums[:5, :inner].reshape(-1), out_sums[0], tail])
    packed = jnp.pad(packed, (0, -packed.shape[0] % 1024)).reshape(-1, LANES)

    got_l, got_r, got_s, out_normed = lax.optimization_barrier(
        (got_l, got_r, swap(packed, "dp", core), out_normed)
    )
    output = (hidden.astype(F32) + mm(out_normed, output_w, NT)).astype(BF16)
    packed = packed + got_s
    left, right = plus(keep_l, got_l), more_cols(plus(keep_r, got_r), rest)
    keep_l, give_l = fold_cols(left, tensor_top, rest)
    keep_r, give_r = pick(right, on_x), pick(right, 1 - on_x)
    got_l, got_r, got_s = lax.optimization_barrier(
        (swap(give_l, "tensor", tensor_top), swap(give_r, "dp", cross), swap(packed, "dp", cross))
    )
    packed = packed + got_s
    left, right = more_cols(plus(keep_l, got_l), rest), plus(keep_r, got_r)
    on_z = side("dp", long[0]) == 1
    keep, give = jnp.where(on_z, left, right), jnp.where(on_z, right, left)
    bits = bits_of("tensor")
    sums = [("tensor", bit) for bit in bits] + [("dp", bit) for bit in long]
    pair = plus(keep_p, got_p)
    for bit in long[1:]:
        got, got_s = lax.optimization_barrier(
            (swap(give, "dp", bit >> 1), swap(packed, *sums[0]))
        )
        packed, sums = packed + got_s, sums[1:]
        keep_p, give_p = fold_rows(pair, bit, 1)
        pair = keep_p.astype(F32) + swap(give_p, "dp", bit).astype(F32)
        keep, give = fold_rows(plus(keep, got), bit)
    got, got_s = lax.optimization_barrier((swap(give, "dp", long[-1]), swap(packed, *sums[0])))
    packed, sums = packed + got_s, sums[1:]
    joined = (keep.astype(F32) + got.astype(F32)).reshape(part_rows, -1)
    if len(bits) == 1:
        joined = in_order(joined, rest)
    for axis, bit in sums:
        packed = packed + swap(packed, axis, bit)
    packed = packed.reshape(-1)
    pair = pair.astype(F32).reshape(2, part_rows, part)
    grad_gate_w, grad_out_w = pair[0], pair[1]
    grad_inner_w = joined[:, :part]
    grad_shared_w = joined[:, part : part + shared]
    grad_rate_w = lax.dynamic_slice_in_dim(
        joined[:, part + shared :], tensor_pos * rate_part, rate_part, 1
    )
    sizes = [4 * inner, inner, inner, 4 * shared, shared, heads, heads, heads, features]
    pieces, at = [], 0
    for size in sizes:
        pieces.append(packed[at : at + size])
        at += size
    (g_conv, g_conv_bias, g_out_gain, g_conv_sh, g_conv_sh_bias, g_rate_bias, g_decay, g_skip,
     g_gain_in) = pieces
    return (
        output, grad_hidden, g_gain_in, grad_gate_w, grad_inner_w, grad_shared_w, grad_rate_w,
        g_conv.reshape(4, inner), g_conv_bias, g_conv_sh.reshape(4, shared), g_conv_sh_bias,
        g_rate_bias, g_decay, g_skip, g_out_gain, grad_out_w,
    )


def solution(mesh):
    tokens = P(("dp", "tensor"), None)
    weight = P("dp", "tensor")
    in_specs = (
        tokens, P(), weight, weight, P("dp", None), weight, P(), P(), P(), P(), P(), P(), P(),
        P(), weight, tokens,
    )
    out_specs = (
        tokens, tokens, P(), weight, weight, P("dp", None), weight, P(), P(), P(), P(), P(),
        P(), P(), P(), weight,
    )
    return jax.shard_map(local, mesh=mesh, in_specs=in_specs, out_specs=out_specs, check_vma=False)
```

```python
import functools

import jax
import jax.numpy as jnp
from jax import lax
from jax.experimental import pallas as pl
from jax.experimental.pallas import tpu as pltpu
from jax.sharding import PartitionSpec as P

SEQ_LEN = 2048
CHUNK = 128
RIM = 16
LANES = 128
EPS = 1e-05
F32 = jnp.float32
BF16 = jnp.bfloat16


def mm(left, right, contract=((1,), (0,))):
    return lax.dot_general(left, right, (contract, ((), ())), preferred_element_type=F32)


NT = ((1,), (1,))
TN = ((0,), (0,))


def split3(value):
    high = value.astype(BF16)
    rest = value - high.astype(F32)
    mid = rest.astype(BF16)
    return high, mid, (rest - mid.astype(F32)).astype(BF16)


def exact_left(ones, value):
    high, mid, low = split3(value)
    return mm(ones, high) + mm(ones, mid) + mm(ones, low)


def exact_right(value, ones):
    high, mid, low = split3(value)
    return mm(high, ones) + mm(mid, ones) + mm(low, ones)


def spread_matrix(heads, inner):
    head_dim = inner // heads
    row = lax.broadcasted_iota(jnp.int32, (LANES, inner), 0)
    col = lax.broadcasted_iota(jnp.int32, (LANES, inner), 1)
    return ((col >= row * head_dim) & (col < (row + 1) * head_dim)).astype(BF16)


def iota2(shape, dim):
    return lax.broadcasted_iota(jnp.int32, shape, dim)


def softplus(v):
    return jnp.maximum(v, 0.0) + jnp.log1p(jnp.exp(-jnp.abs(v)))


def conv_rows(ext_ref, taps, bias, lo, width, rows):
    total = bias
    for k in range(4):
        total = total + taps[k : k + 1, :] * ext_ref[pl.ds(5 + k, rows), pl.ds(lo, width)]
    return total


def spread_columns(target_ref, rows, block, inner):
    half, shared = inner // 2, 2 * LANES
    target_ref[rows, :half] = block[:, :half]
    target_ref[rows, half:inner] = block[:, half + shared + LANES :]
    target_ref[rows, inner:] = block[:, half : half + shared]


def column_of(lo, inner):
    half = inner // 2
    if lo >= inner:
        return lo - inner + half
    return lo if lo < half else lo + 3 * LANES


def mix_in_kernel(
    inner, heads,
    proj_ref, rim_ref, final_in_ref, total_in_ref, tap_ref, bias_ref, rate_bias_ref, decay_ref,
    *rest,
):
    x_ref, bc_ref, step_ref, within_ref, slope_ref, final_ref, total_ref, ext_ref, u_ref = rest[-9:]
    i = pl.program_id(0)
    shared = 2 * LANES

    @pl.when(i == 0)
    def _():
        spread_columns(ext_ref, slice(0, 8), rim_ref[...].astype(F32)[RIM - 8 :], inner)
        final_ref[...] = final_in_ref[...]
        total_ref[...] = total_in_ref[...]

    @pl.when(i > 0)
    def _():
        ext_ref[0:8, :] = ext_ref[CHUNK : CHUNK + 8, :]

    spread_columns(ext_ref, slice(8, CHUNK + 8), proj_ref[...].astype(F32), inner)
    at = inner // 2 + shared
    step = softplus(proj_ref[:, at : at + LANES].astype(F32) + rate_bias_ref[...])
    log_decay = step * decay_ref[...]
    lower = (iota2((CHUNK, CHUNK), 0) >= iota2((CHUNK, CHUNK), 1)).astype(BF16)
    within = exact_left(lower, log_decay)
    step_ref[...] = step
    within_ref[...] = within
    last = within[CHUNK - 1 :, :]
    total_ref[...] += last
    weight = step * jnp.exp(last - within)

    pre = conv_rows(ext_ref, tap_ref[:, inner:], bias_ref[:, inner:], inner, shared, CHUNK)
    sig = jax.nn.sigmoid(pre)
    bc = (pre * sig).astype(BF16)
    bc_ref[...] = bc
    slope_ref[:, inner:] = (sig * (1.0 + pre * (1.0 - sig))).astype(BF16)
    first = iota2((CHUNK, LANES), 1) < LANES // 2
    for p in range(inner // LANES):
        lo = p * LANES
        pre = conv_rows(
            ext_ref, tap_ref[:, lo : lo + LANES], bias_ref[:, lo : lo + LANES], lo, LANES, CHUNK
        )
        sig = jax.nn.sigmoid(pre)
        act = pre * sig
        x = act.astype(BF16)
        x_ref[:, lo : lo + LANES] = x
        slope_ref[:, lo : lo + LANES] = (sig + act * (1.0 - sig)).astype(BF16)
        w = jnp.where(
            first,
            jnp.broadcast_to(weight[:, 2 * p : 2 * p + 1], (CHUNK, LANES)),
            jnp.broadcast_to(weight[:, 2 * p + 1 : 2 * p + 2], (CHUNK, LANES)),
        )
        u_ref[:, lo : lo + LANES] = (x.astype(F32) * w).astype(BF16)
    factor = exact_right(jnp.exp(jnp.broadcast_to(last, (8, LANES))), spread_matrix(heads, inner))
    final_ref[...] = factor[0:1, :] * final_ref[...] + mm(bc[:, :LANES], u_ref[...], TN)


def mix_in(proj, rows, carried, consts, inner, heads, start, count, held=()):
    width = proj.shape[1]
    full = lambda shape: pl.BlockSpec(shape, lambda i: (0,) * len(shape))
    block = lambda w: pl.BlockSpec((CHUNK, w), lambda i: (start + i, 0))
    before = start * CHUNK // RIM - 1 if start else rows // RIM
    operands = [proj, proj, *carried, *consts, *held]
    return pl.pallas_call(
        functools.partial(mix_in_kernel, inner, heads),
        grid=(count,),
        in_specs=[
            block(width),
            pl.BlockSpec((RIM, width), lambda i: (before, 0)),
            *[full(v.shape) for v in (*carried, *consts)],
            *[pl.BlockSpec(memory_space=pl.ANY) for _ in held],
        ],
        out_specs=[
            block(inner), block(2 * LANES), block(LANES), block(LANES), block(inner + 2 * LANES),
            full((LANES, inner)), full((1, LANES)),
        ],
        out_shape=[
            jax.ShapeDtypeStruct((rows, inner), BF16),
            jax.ShapeDtypeStruct((rows, 2 * LANES), BF16),
            jax.ShapeDtypeStruct((rows, LANES), F32),
            jax.ShapeDtypeStruct((rows, LANES), F32),
            jax.ShapeDtypeStruct((rows, inner + 2 * LANES), BF16),
            jax.ShapeDtypeStruct((LANES, inner), F32),
            jax.ShapeDtypeStruct((1, LANES), F32),
        ],
        input_output_aliases={len(operands) - len(held) + k: k for k in range(len(held))},
        scratch_shapes=[
            pltpu.VMEM((CHUNK + 8, inner + 2 * LANES), F32),
            pltpu.VMEM((CHUNK, inner), BF16),
        ],
        compiler_params=pltpu.CompilerParams(vmem_limit_bytes=48 * 2**20),
        cost_estimate=pl.CostEstimate(
            flops=14000 * count * CHUNK * inner, bytes_accessed=8 * count * CHUNK * inner, transcendentals=0
        ),
        name="mix_in",
    )(*operands)


def mix_out_kernel(
    inner, heads,
    x_ref, bc_ref, step_ref, within_ref, gate_ref, gon_ref, entry_ref, skip_ref, gain_ref,
    normed_ref, gm_ref, gg_ref, state_ref, grad_entry_ref, sums_ref,
    hold_ref, y_ref, u_ref, prefix_ref, grow_ref, sig_ref,
):
    i = pl.program_id(0)

    @pl.when(i == 0)
    def _():
        hold_ref[...] = entry_ref[...].astype(F32)
        grad_entry_ref[...] = jnp.zeros_like(grad_entry_ref)
        sums_ref[...] = jnp.zeros_like(sums_ref)
        prefix_ref[...] = jnp.zeros_like(prefix_ref)

    spread = spread_matrix(heads, inner)
    key, query = bc_ref[:, :LANES], bc_ref[:, LANES:]
    within = within_ref[...]
    within_t = within.T
    last = within[CHUNK - 1 :, :]
    state = hold_ref[...].astype(BF16)
    state_ref[0] = state
    y_ref[...] = mm(query, state)
    scores = mm(query, key, NT)
    causal = iota2((CHUNK, CHUNK), 0) >= iota2((CHUNK, CHUNK), 1)
    first = iota2((CHUNK, LANES), 1) < LANES // 2
    zero = jnp.zeros((CHUNK, LANES), BF16)
    for p in range(inner // LANES):
        lo = p * LANES
        slab = slice(lo, lo + LANES)
        cols, weights = [], []
        for h in (2 * p, 2 * p + 1):
            col = jnp.broadcast_to(within[:, h : h + 1], (CHUNK, CHUNK))
            gap = jnp.where(causal, col - within_t[h : h + 1, :], -1e30)
            weights.append((scores * jnp.exp(gap)).astype(BF16))
            cols.append(col)
        a = jnp.where(first, cols[0], cols[1])
        d = jnp.where(
            first,
            jnp.broadcast_to(step_ref[:, 2 * p : 2 * p + 1], (CHUNK, LANES)),
            jnp.broadcast_to(step_ref[:, 2 * p + 1 : 2 * p + 2], (CHUNK, LANES)),
        )
        x = x_ref[:, slab].astype(F32)
        u = x * d
        ub = u.astype(BF16)
        u_ref[:, slab] = (u * jnp.exp(a[CHUNK - 1 :, :] - a)).astype(BF16)
        diagonal = mm(
            jnp.concatenate(weights, axis=1),
            jnp.concatenate([jnp.where(first, ub, zero), jnp.where(first, zero, ub)], axis=0),
        )
        grow = jnp.exp(a)
        grow_ref[:, slab] = grow
        y_ref[:, slab] = diagonal + grow * y_ref[:, slab] + skip_ref[:, slab] * x
    factors = exact_right(
        jnp.exp(jnp.concatenate([last, prefix_ref[...], jnp.zeros((6, LANES), F32)], axis=0)),
        spread,
    )
    prefix_ref[...] += last
    hold_ref[...] = factors[0:1, :] * hold_ref[...] + mm(key, u_ref[...], TN)

    square = jnp.zeros((CHUNK, LANES), F32)
    dot = jnp.zeros((CHUNK, LANES), F32)
    for p in range(inner // LANES):
        slab = slice(p * LANES, (p + 1) * LANES)
        z = gate_ref[:, slab].astype(F32)
        m = y_ref[:, slab].astype(BF16).astype(F32)
        sig = jax.nn.sigmoid(z)
        sig_ref[:, slab] = sig
        gated = m * (z * sig)
        square = square + gated * gated
        dot = dot + gain_ref[:, slab] * gon_ref[:, slab].astype(F32) * gated
    square = jnp.sum(square, axis=1, keepdims=True)
    dot = jnp.sum(dot, axis=1, keepdims=True)
    root = lax.rsqrt(square / inner + EPS)
    pull = root * root * root * dot / inner
    for p in range(inner // LANES):
        slab = slice(p * LANES, (p + 1) * LANES)
        z = gate_ref[:, slab].astype(F32)
        m = y_ref[:, slab].astype(BF16).astype(F32)
        sig = sig_ref[:, slab]
        act = z * sig
        gated = m * act
        gon = gon_ref[:, slab].astype(F32)
        unit = gated * root
        normed_ref[:, slab] = (unit * gain_ref[:, slab]).astype(BF16)
        grad = root * gain_ref[:, slab] * gon - gated * pull
        gm = (grad * act).astype(BF16)
        gm_ref[:, slab] = gm
        gg_ref[:, slab] = (grad * m * (sig * (1.0 + z * (1.0 - sig)))).astype(BF16)
        gmf = gm.astype(F32)
        sums_ref[0:1, slab] += jnp.sum(gon * unit, axis=0, keepdims=True)
        sums_ref[1:2, slab] += jnp.sum(gmf * x_ref[:, slab].astype(F32), axis=0, keepdims=True)
        u_ref[:, slab] = (gmf * grow_ref[:, slab]).astype(BF16)
    grad_entry_ref[...] += factors[1:2, :] * mm(query, u_ref[...], TN)


def mix_out(x, bc, step, within, gate, gon, entry, skip, gain, heads):
    rows, inner = x.shape
    chunks = rows // CHUNK
    full = lambda shape: pl.BlockSpec(shape, lambda i: (0,) * len(shape))
    block = lambda width: pl.BlockSpec((CHUNK, width), lambda i: (i, 0))
    return pl.pallas_call(
        functools.partial(mix_out_kernel, inner, heads),
        grid=(chunks,),
        in_specs=[
            block(inner), block(2 * LANES), block(LANES), block(LANES), block(inner), block(inner),
            full(entry.shape), full(skip.shape), full(gain.shape),
        ],
        out_specs=[
            block(inner), block(inner), block(inner),
            pl.BlockSpec((1, LANES, inner), lambda i: (i, 0, 0)),
            full((LANES, inner)), full((8, inner)),
        ],
        out_shape=[
            jax.ShapeDtypeStruct((rows, inner), BF16),
            jax.ShapeDtypeStruct((rows, inner), BF16),
            jax.ShapeDtypeStruct((rows, inner), BF16),
            jax.ShapeDtypeStruct((chunks, LANES, inner), BF16),
            jax.ShapeDtypeStruct((LANES, inner), F32),
            jax.ShapeDtypeStruct((8, inner), F32),
        ],
        scratch_shapes=[
            pltpu.VMEM((LANES, inner), F32),
            pltpu.VMEM((CHUNK, inner), F32),
            pltpu.VMEM((CHUNK, inner), BF16),
            pltpu.VMEM((1, LANES), F32),
            pltpu.VMEM((CHUNK, inner), F32),
            pltpu.VMEM((CHUNK, inner), F32),
        ],
        compiler_params=pltpu.CompilerParams(vmem_limit_bytes=48 * 2**20),
        cost_estimate=pl.CostEstimate(
            flops=17000 * rows * inner, bytes_accessed=16 * rows * inner, transcendentals=0
        ),
        name="mix_out",
    )(x, bc, step, within, gate, gon, entry, skip, gain)


def mix_back_kernel(
    inner, heads, count, inside, rim_step,
    x_ref, bc_ref, step_ref, within_ref, gm_ref, state_ref, proj_ref, slope_ref, rim_ref,
    exit_ref, next_ref, sums_in_ref, heads_in_ref,
    skip_ref, tap_ref, rate_bias_ref, decay_ref,
    *rest,
):
    if inside:
        rest = rest[1:]
    (
        gproj_ref, hold_ref, head_ref, sums_ref, heads_ref,
        ext_ref, ahead_ref, cs_ref, bg_ref, ue_ref, ge_ref, prod_ref, rows_ref,
    ) = rest
    j = pl.program_id(0)
    shared = 2 * LANES
    conv_width = inner + shared

    @pl.when(j == 0)
    def _():
        hold_ref[...] = exit_ref[...].astype(F32)
        sums_ref[...] = sums_in_ref[...]
        heads_ref[...] = heads_in_ref[...]
        ahead_ref[CHUNK:, :] = next_ref[...]
        rows_ref[...] = jnp.zeros_like(rows_ref)

    @pl.when((j > 0) & (j < count))
    def _():
        ahead_ref[CHUNK:, :] = ahead_ref[0:8, :]

    @pl.when(j < count)
    def _():
        spread = spread_matrix(heads, inner)
        key, query = bc_ref[:, :LANES], bc_ref[:, LANES:]
        within = within_ref[...]
        within_t = within.T
        step = step_ref[...]
        last = within[CHUNK - 1 :, :]
        state = state_ref[0]
        hold = hold_ref[...]
        exit_grad = hold.astype(BF16)
        cs_ref[...] = mm(query, state)
        bg_ref[...] = mm(key, exit_grad)
        scores_t = mm(key, query, NT)
        causal_t = iota2((CHUNK, CHUNK), 0) <= iota2((CHUNK, CHUNK), 1)
        first = iota2((CHUNK, LANES), 1) < LANES // 2
        lane = iota2((2 * CHUNK, LANES), 1)
        upper_half = iota2((2 * CHUNK, LANES), 0) >= CHUNK
        zero = jnp.zeros((CHUNK, LANES), BF16)
        grad_scores_t = jnp.zeros((CHUNK, CHUNK), F32)
        col_sums = jnp.zeros((CHUNK, LANES), F32)
        for p in range(inner // LANES):
            slab = slice(p * LANES, (p + 1) * LANES)
            x = x_ref[:, slab].astype(F32)
            gb = gm_ref[:, slab]
            g = gb.astype(F32)
            cols = [
                jnp.broadcast_to(within[:, h : h + 1], (CHUNK, LANES)) for h in (2 * p, 2 * p + 1)
            ]
            a = jnp.where(first, cols[0], cols[1])
            d = jnp.where(
                first,
                jnp.broadcast_to(step[:, 2 * p : 2 * p + 1], (CHUNK, LANES)),
                jnp.broadcast_to(step[:, 2 * p + 1 : 2 * p + 2], (CHUNK, LANES)),
            )
            u = x * d
            ub = u.astype(BF16)
            to_end = jnp.exp(a[CHUNK - 1 :, :] - a)
            ge = g * jnp.exp(a)
            ge_ref[:, slab] = ge.astype(BF16)
            ue_ref[:, slab] = (u * to_end).astype(BF16)
            gcat = jnp.concatenate([jnp.where(first, gb, zero), jnp.where(first, zero, gb)], axis=0)
            reach_t = mm(ub, gcat, NT)
            pieces, moves = [], []
            for q, h in enumerate((2 * p, 2 * p + 1)):
                gap = jnp.where(causal_t, within_t[h : h + 1, :] - cols[q], -1e30)
                weight = jnp.exp(gap)
                grad_score = reach_t[:, q * CHUNK : (q + 1) * CHUNK] * weight
                grad_scores_t = grad_scores_t + grad_score
                pieces.append((scores_t * weight).astype(BF16))
                move = (grad_score * scores_t).astype(BF16)
                moves.append(move)
                rows_ref[h : h + 1, :] = jnp.sum(move.astype(F32), axis=0, keepdims=True)
            pick = (lane == jnp.where(upper_half, 2 * p + 1, 2 * p)).astype(BF16)
            col_sums = col_sums + mm(jnp.concatenate(moves, axis=1), pick)
            grad_state_u = to_end * bg_ref[:, slab]
            grad_u = mm(jnp.concatenate(pieces, axis=1), gcat) + grad_state_u
            prod_ref[0:CHUNK, slab] = (x * grad_u).astype(BF16)
            prod_ref[CHUNK : 2 * CHUNK, slab] = (u * grad_state_u).astype(BF16)
            prod_ref[2 * CHUNK :, slab] = (ge * cs_ref[:, slab]).astype(BF16)
            grad_x = d * grad_u + skip_ref[:, slab] * g
            ahead_ref[0:CHUNK, slab] = grad_x * slope_ref[:, slab].astype(F32)

        by_head = mm(prod_ref[...], spread, NT)
        grad_step = by_head[0:CHUNK]
        from_state = by_head[CHUNK : 2 * CHUNK]
        from_entry = by_head[2 * CHUNK :]
        factor = exact_right(jnp.exp(jnp.broadcast_to(last, (8, LANES))), spread)[0:1, :]
        whole = jnp.sum(hold * state.astype(F32), axis=0, keepdims=True) * factor
        whole = jnp.broadcast_to(whole, (8, inner))
        high, mid, _ = split3(whole)
        whole = (mm(high, spread, NT) + mm(mid, spread, NT))[0:1, :]
        later = (iota2((CHUNK, CHUNK), 0) <= iota2((CHUNK, CHUNK), 1)).astype(BF16)
        earlier = (iota2((CHUNK, CHUNK), 0) > iota2((CHUNK, CHUNK), 1)).astype(BF16)
        row_sums = rows_ref[...].T
        grad_log = (
            exact_left(later, row_sums - col_sums + from_entry)
            + exact_left(earlier, from_state)
            + whole
        )
        decay = decay_ref[...]
        grad_step = grad_step + grad_log * decay
        rates = slice(inner // 2 + shared, inner // 2 + shared + LANES)
        squash = jax.nn.sigmoid(proj_ref[:, rates].astype(F32) + rate_bias_ref[...])
        grad_rate = grad_step * squash
        gproj_ref[:, rates] = grad_rate.astype(BF16)
        heads_ref[0:1, :] += jnp.sum(grad_rate, axis=0, keepdims=True)
        heads_ref[1:2, :] += jnp.sum(grad_log * step, axis=0, keepdims=True) * decay

        gsb = grad_scores_t.astype(BF16)
        grad_key = mm(ue_ref[...], exit_grad, NT) + mm(gsb, query)
        grad_query = mm(ge_ref[...], state, NT) + mm(gsb, key, TN)
        hold_ref[...] = factor * hold + mm(query, ge_ref[...], TN)

        slope = slope_ref[:, inner:].astype(F32)
        ahead_ref[0:CHUNK, inner:] = jnp.concatenate([grad_key, grad_query], axis=1) * slope

        for p in range(conv_width // LANES):
            slab = slice(p * LANES, (p + 1) * LANES)
            lo = column_of(p * LANES, inner)
            values = proj_ref[:, lo : lo + LANES].astype(F32)
            total = jnp.zeros((CHUNK, LANES), F32)
            for k in range(4):
                moved = ahead_ref[pl.ds(3 - k, CHUNK), slab]
                total = total + tap_ref[k : k + 1, slab] * moved
                sums_ref[k : k + 1, slab] += jnp.sum(values * moved, axis=0, keepdims=True)
                if k == 3:
                    sums_ref[4:5, slab] += jnp.sum(moved, axis=0, keepdims=True)
            gproj_ref[:, lo : lo + LANES] = total.astype(BF16)
        head_ref[...] = ahead_ref[0:8, :]

    if not rim_step:
        return

    @pl.when(j == count)
    def _():
        gproj_ref[...] = jnp.zeros_like(gproj_ref)
        head = ahead_ref[0:8, :]
        at = iota2((8, conv_width), 0)
        spread_columns(ext_ref, slice(0, 8), rim_ref[...].astype(F32)[RIM - 8 :], inner)
        values = ext_ref[0:8, :]
        total = jnp.zeros((8, conv_width), F32)
        for k in range(3):
            moved = jnp.zeros((8, conv_width), F32)
            for r in range(5 + k, 8):
                t = r - 5 - k
                moved = moved + jnp.where(at == r, head[t : t + 1, :], 0.0)
            total = total + tap_ref[k : k + 1, :] * moved
            sums_ref[k : k + 1, :] += jnp.sum(values * moved, axis=0, keepdims=True)
        total = jnp.concatenate([jnp.zeros((RIM - 8, conv_width), F32), total], axis=0)
        total = total.astype(BF16)
        half = inner // 2
        gproj_ref[0:RIM, :half] = total[:, :half]
        gproj_ref[0:RIM, half : half + shared] = total[:, inner:]
        gproj_ref[0:RIM, half + shared + LANES :] = total[:, half:inner]


def mix_back(x, bc, step, within, gm, state, proj, slope, carried, consts, heads, top, count, gproj,
             rim_step):
    inside = gproj is not None
    rows, inner = x.shape
    width = proj.shape[1]
    chunks = rows // CHUNK
    conv_width = inner + 2 * LANES
    full = lambda shape: pl.BlockSpec(shape, lambda j: (0,) * len(shape))
    at = lambda j: jnp.maximum(top - j, top - count + 1)
    block = lambda w: pl.BlockSpec((CHUNK, w), lambda j: (at(j), 0))
    operands = [x, bc, step, within, gm, state, proj, slope, proj, *carried, *consts]
    in_specs = [
        block(inner), block(2 * LANES), block(LANES), block(LANES), block(inner),
        pl.BlockSpec((1, LANES, inner), lambda j: (at(j), 0, 0)),
        block(width),
        block(conv_width),
        pl.BlockSpec((RIM, width), lambda j: (rows // RIM, 0)),
        *[full(v.shape) for v in (*carried, *consts)],
    ]
    if inside:
        operands.append(gproj)
        in_specs.append(pl.BlockSpec(memory_space=pl.ANY))
    return pl.pallas_call(
        functools.partial(mix_back_kernel, inner, heads, count, inside, rim_step),
        grid=(count + 1 if rim_step else count,),
        in_specs=in_specs,
        out_specs=[
            pl.BlockSpec((CHUNK, width), lambda j: (jnp.where(j == count, chunks, at(j)), 0)),
            full((LANES, inner)), full((8, conv_width)), full((8, conv_width)), full((8, LANES)),
        ],
        out_shape=[
            jax.ShapeDtypeStruct((rows + CHUNK, width), BF16),
            jax.ShapeDtypeStruct((LANES, inner), F32),
            jax.ShapeDtypeStruct((8, conv_width), F32),
            jax.ShapeDtypeStruct((8, conv_width), F32),
            jax.ShapeDtypeStruct((8, LANES), F32),
        ],
        scratch_shapes=[
            pltpu.VMEM((8, conv_width), F32),
            pltpu.VMEM((CHUNK + 8, conv_width), F32),
            pltpu.VMEM((CHUNK, inner), F32),
            pltpu.VMEM((CHUNK, inner), F32),
            pltpu.VMEM((CHUNK, inner), BF16),
            pltpu.VMEM((CHUNK, inner), BF16),
            pltpu.VMEM((3 * CHUNK, inner), BF16),
            pltpu.VMEM((LANES, CHUNK), F32),
        ],
        input_output_aliases={len(operands) - 1: 0} if inside else {},
        compiler_params=pltpu.CompilerParams(vmem_limit_bytes=48 * 2**20),
        cost_estimate=pl.CostEstimate(
            flops=32768 * count * CHUNK * inner, bytes_accessed=16 * count * CHUNK * inner,
            transcendentals=0,
        ),
        name="mix_back",
    )(*operands)


def swap(value, axis, bit):
    size = lax.axis_size(axis)
    return lax.ppermute(value, axis, [(i, i ^ bit) for i in range(size)])


def sum_square(value, dp_bit, tensor_bit):
    count = lax.axis_size("tensor")
    flip = dp_bit * count + tensor_bit
    pairs = [(i, i ^ flip) for i in range(lax.axis_size("dp") * count)]
    beside_x, beside_y = swap(value, "dp", dp_bit), swap(value, "tensor", tensor_bit)
    return (value + beside_x) + (beside_y + lax.ppermute(value, ("dp", "tensor"), pairs))


def bits_of(axis):
    size = lax.axis_size(axis)
    return [1 << k for k in range(size.bit_length() - 1)]


def join(value, axis, bit, dim):
    return beside(value, swap(value, axis, bit), axis, bit, dim)


def beside(value, other, axis, bit, dim):
    high = (lax.axis_index(axis) & bit) != 0
    return jnp.where(high, jnp.stack([other, value], axis=dim), jnp.stack([value, other], axis=dim))


def join_cols(value):
    for bit in bits_of("tensor"):
        other = swap(value, "tensor", bit)
        high = (lax.axis_index("tensor") & bit) != 0
        value = jnp.where(
            high,
            jnp.concatenate([other, value], axis=-1),
            jnp.concatenate([value, other], axis=-1),
        )
    return value


def join_dp(stack, bits, done):
    for bit in bits:
        stack = join(stack, "dp", bit, done)
        done += 1
    return stack


def side(axis, bit):
    return jnp.where((lax.axis_index(axis) & bit) != 0, 1, 0)


def fold_rows(value, bit, dim=0):
    mine = side("dp", bit)
    shape = value.shape
    pairs = value.reshape(*shape[:dim], shape[dim] // 2, 2, *shape[dim + 1 :])
    pick = lambda k: lax.dynamic_index_in_dim(pairs, k, dim + 1, keepdims=False)
    return pick(mine), pick(1 - mine)


def fold_cols(value, bit, rest=0):
    high = side("tensor", bit) == 1
    half = (value.shape[-1] - rest) // 2
    low_part, high_part = value[..., : half + rest], value[..., half:]
    return jnp.where(high, high_part, low_part), jnp.where(high, low_part, high_part)


def plus(keep, got):
    return (keep.astype(F32) + got.astype(F32)).astype(BF16)


def in_order(value, rest):
    high = side("tensor", lax.axis_size("tensor") // 2) == 1
    half = value.shape[-1] - rest
    turned = jnp.concatenate([value[..., rest:], value[..., :rest]], axis=-1)
    return jnp.where(high, turned, value)


def more_cols(value, rest=0):
    bits = bits_of("tensor")[-2::-1]
    if not bits:
        return value
    if rest:
        value = in_order(value, rest)
    for bit in bits:
        width = value.shape[-1] - rest
        keep, give = fold_cols(value[..., :width], bit)
        tail = value[..., width:]
        give = jnp.concatenate([give, tail], axis=-1)
        value = plus(jnp.concatenate([keep, tail], axis=-1), swap(give, "tensor", bit))
    return value


def local(
    hidden, input_gain, proj_gate, proj_inner, proj_shared, proj_rate, conv_inner,
    conv_inner_bias, conv_shared, conv_shared_bias, rate_bias, decay_log, skip_gain,
    output_gain, proj_output, cotangent,
):
    tensor_size = lax.axis_size("tensor")
    tensor_pos = lax.axis_index("tensor")
    rows, features = hidden.shape
    heads = rate_bias.shape[0]
    inner = output_gain.shape[0]
    shared = conv_shared.shape[1]
    head_dim = inner // heads
    conv_width = inner + shared
    per_seq = SEQ_LEN // rows
    seq_pos = lax.rem(tensor_pos, per_seq)
    part = inner // tensor_size
    rate_part = heads // tensor_size
    forward = [(i, i + 1) for i in range(tensor_size - 1)]
    backward = [(i + 1, i) for i in range(tensor_size - 1)]

    dp_bits = bits_of("dp")
    far, near = dp_bits[:0:-1], dp_bits[:1]
    dp_size, part_rows = lax.axis_size("dp"), proj_inner.shape[0]
    far_z, far_x = far[:-1], far[-1:]
    shared_part = shared // tensor_size
    rate_block = lax.dynamic_update_slice(
        jnp.zeros((part_rows, LANES), BF16), proj_rate, (0, tensor_pos * rate_part)
    )
    shared_block = lax.dynamic_slice_in_dim(proj_shared, tensor_pos * shared_part, shared_part, 1)
    piece = jnp.concatenate([proj_inner, shared_block, rate_block], axis=1)
    first_w = join_dp(piece, far_z, 0)
    first_w, output_w, gate_w = lax.optimization_barrier((first_w, proj_output, proj_gate))
    upper, lower = join_cols(first_w[0]), join_dp(first_w[1], far_x, len(far_z) - 1)
    upper, lower = lax.optimization_barrier((upper, lower))
    upper, lower = join_dp(upper, far_x, len(far_z) - 1), join_cols(lower)
    first_w = lax.optimization_barrier(jnp.stack([upper, lower]))
    pieces = [
        first_w[..., k * piece.shape[1] : (k + 1) * piece.shape[1]] for k in range(tensor_size)
    ]
    inner_cols = [v[..., :part] for v in pieces]
    rate_cols = sum(v[..., part + shared_part :] for v in pieces)
    first_w = jnp.concatenate(
        inner_cols[: tensor_size // 2]
        + [v[..., part : part + shared_part] for v in pieces]
        + [rate_cols]
        + inner_cols[tensor_size // 2 :],
        axis=-1,
    )
    gate_w = join_dp(gate_w, far_z, 0)
    output_w = join_dp(output_w, far_z, 0)
    first_w, gate_w, output_w = lax.optimization_barrier((first_w, gate_w, output_w))
    first_w = join_dp(first_w, near, len(far)).reshape(dp_size * part_rows, -1)
    gate_w = join_dp(gate_w, far_x, len(far_z))
    output_w = join_cols(output_w)

    rim = lax.ppermute(hidden[rows - RIM :], "tensor", forward)
    rim = jnp.where(seq_pos == 0, jnp.zeros_like(rim), rim)
    extended = jnp.pad(
        jnp.concatenate([hidden, rim], axis=0), ((0, CHUNK - RIM), (0, 0))
    ).astype(F32)
    gain_in = input_gain.astype(F32)
    root = lax.rsqrt(jnp.mean(extended * extended, axis=-1, keepdims=True) + EPS)
    normed = (extended * root * gain_in).astype(BF16)

    proj = mm(normed, first_w).astype(BF16)
    proj, gate_w, output_w = lax.optimization_barrier((proj, gate_w, output_w))
    gate_w = join_cols(gate_w)
    output_w = join_dp(output_w, far_x, len(far_z))
    taps = jnp.concatenate([conv_inner, conv_shared], axis=1).astype(F32)
    bias = jnp.concatenate([conv_inner_bias, conv_shared_bias])[None].astype(F32)
    pad_heads = lambda v: jnp.pad(v, (0, LANES - heads))[None]
    rate_bias_row = pad_heads(rate_bias)
    decay_row = pad_heads(-jnp.exp(decay_log))
    skip_row = jnp.repeat(skip_gain, head_dim)[None]
    gain_row = output_gain[None].astype(F32)
    chunks = rows // CHUNK
    lead_count = chunks - max(chunks // 4, 1)
    consts = [taps, bias, rate_bias_row, decay_row]
    *held, final, total = mix_in(
        proj, rows, [jnp.zeros((LANES, inner), F32), jnp.zeros((1, LANES), F32)], consts, inner,
        heads, 0, lead_count,
    )
    final, gate_w, output_w = lax.optimization_barrier((final, gate_w, output_w))
    gate_near, output_near = swap(gate_w, "dp", near[0]), swap(output_w, "dp", near[0])
    x, bc, step, within, slope, final, total = mix_in(
        proj, rows, [final, total], consts, inner, heads, lead_count, chunks - lead_count, held
    )
    final, gate_near, output_near = lax.optimization_barrier((final, gate_near, output_near))
    whole = jnp.repeat(jnp.exp(total[0, :heads]), head_dim)[None]
    entry = jnp.zeros_like(final)
    for _ in range(per_seq - 1):
        sent = lax.ppermute((final + whole * entry).astype(BF16), "tensor", forward)
        entry = jnp.where(seq_pos == 0, 0.0, sent.astype(F32))

    gate_w = beside(gate_w, gate_near, "dp", near[0], len(far)).reshape(dp_size * part_rows, inner)
    output_w = beside(output_w, output_near, "dp", near[0], len(far))
    output_w = output_w.reshape(dp_size * part_rows, inner)
    gate = mm(normed[:rows], gate_w).astype(BF16)
    gon = mm(cotangent, output_w).astype(BF16)
    out_normed, grad_mixed, grad_gate, states, grad_entry, out_sums = mix_out(
        x, bc, step, within, gate, gon, entry, skip_row, gain_row, heads
    )
    exit_grad = jnp.zeros_like(grad_entry)
    for _ in range(per_seq - 1):
        sent = lax.ppermute((grad_entry + whole * exit_grad).astype(BF16), "tensor", backward)
        exit_grad = jnp.where(seq_pos == per_seq - 1, 0.0, sent.astype(F32))

    core, cross, long = dp_bits[0], dp_bits[1], dp_bits[2:]
    tensor_top = bits_of("tensor")[-1]
    blocks = lambda v: v.astype(BF16).reshape(dp_size, part_rows, -1)
    grad_out_w = blocks(mm(cotangent, out_normed, TN))
    grad_gate_w = blocks(mm(normed[:rows], grad_gate, TN))
    keep_o, give_o = fold_rows(grad_out_w, core)
    keep_g, give_g = fold_rows(grad_gate_w, core)
    exit_grad, give_o, give_g = lax.optimization_barrier((exit_grad, give_o, give_g))
    got_o, got_g = swap(give_o, "dp", core), swap(give_g, "dp", core)

    consts = [skip_row, taps, rate_bias_row, decay_row]
    counts = [chunks // 4, (chunks - chunks // 4) // 2]
    counts.append(chunks - sum(counts))
    tops = [chunks - 1, chunks - 1 - counts[0], counts[2] - 1]
    carried = [
        exit_grad, jnp.zeros((8, conv_width), F32), jnp.zeros((8, conv_width), F32),
        jnp.zeros((8, LANES), F32),
    ]
    back = lambda k, *more: mix_back(
        x, bc, step, within, grad_mixed, states, proj, slope, carried, consts, heads, tops[k], counts[k],
        *more,
    )
    grad_proj, *carried = back(0, None, False)
    grad_proj, got_g, got_o = lax.optimization_barrier((grad_proj, got_g, got_o))
    keep_g, give_g = fold_rows(plus(keep_g, got_g), cross)
    keep_o, give_o = fold_cols(plus(keep_o, got_o), tensor_top)
    grad_proj, give_g, give_o = lax.optimization_barrier((grad_proj, give_g, give_o))
    got_g, got_o = swap(give_g, "dp", cross), swap(give_o, "tensor", tensor_top)
    grad_proj, *carried = back(1, grad_proj, False)
    grad_proj, got_g, got_o = lax.optimization_barrier((grad_proj, got_g, got_o))
    keep_g, give_g = fold_cols(plus(keep_g, got_g), tensor_top)
    keep_o, give_o = fold_rows(more_cols(plus(keep_o, got_o)), cross)
    grad_proj, give_g, give_o = lax.optimization_barrier((grad_proj, give_g, give_o))
    got_g, got_o = swap(give_g, "tensor", tensor_top), swap(give_o, "dp", cross)
    grad_proj, _, _, conv_sums, head_sums = back(2, grad_proj, True)
    grad_proj, got_g, got_o = lax.optimization_barrier((grad_proj, got_g, got_o))

    rest = shared + LANES
    first = blocks(mm(normed, grad_proj, TN))
    keep, give = fold_rows(first, core)
    grad_proj, give = lax.optimization_barrier((grad_proj, give))
    got = swap(give, "dp", core)
    tail = jnp.concatenate(
        [
            conv_sums[:5, inner:].reshape(-1),
            head_sums[0, :heads],
            head_sums[1, :heads],
            jnp.sum(out_sums[1].reshape(heads, head_dim), axis=1),
        ]
    )
    packed = jnp.concatenate([conv_sums[:5, :inner].reshape(-1), out_sums[0], tail])
    packed = jnp.pad(packed, (0, -packed.shape[0] % 1024)).reshape(-1, LANES)

    got_s = swap(packed, "dp", core)
    grad_ext = mm(grad_proj, first_w, NT)
    grad_ext, got, got_s = lax.optimization_barrier((grad_ext, got, got_s))
    packed = packed + got_s
    first = plus(keep, got)
    first = first.reshape(first.shape[0] // 4, 2, 2, part_rows, first.shape[-1])
    pick = lambda v, k: lax.dynamic_index_in_dim(v, k, 1, keepdims=False)
    on_x = side("dp", cross)
    left, right = first[:, 1], first[:, 0]
    keep_l, give_l = pick(left, on_x), pick(left, 1 - on_x)
    keep_r, give_r = fold_cols(right, tensor_top, rest)
    give_l, give_r, grad_ext, grad_gate, got_o, got_g, packed = lax.optimization_barrier(
        (give_l, give_r, grad_ext, grad_gate, got_o, got_g, packed)
    )
    got_l, got_r = swap(give_l, "dp", cross), swap(give_r, "tensor", tensor_top)
    packed = sum_square(packed, cross, tensor_top)
    gate_back = mm(grad_gate, gate_w, NT)
    pair = jnp.stack([more_cols(plus(keep_g, got_g)), plus(keep_o, got_o)])
    keep_p, give_p = fold_rows(pair, long[0], 1)
    got_p = swap(give_p, "dp", long[0])
    rim_grad = lax.ppermute(grad_ext[rows : rows + RIM], "tensor", backward)
    rim_grad = jnp.where(seq_pos == per_seq - 1, 0.0, rim_grad)
    grad_normed = grad_ext[:rows] + gate_back
    grad_normed = grad_normed + jnp.pad(rim_grad, ((rows - RIM, 0), (0, 0)))
    unit = hidden.astype(F32) * root[:rows]
    scaled = grad_normed * gain_in
    grad_hidden = (
        cotangent.astype(F32)
        + root[:rows] * (scaled - unit * jnp.mean(scaled * unit, axis=-1, keepdims=True))
    ).astype(BF16)
    grad_gain_in = jnp.sum(grad_normed * unit, axis=0)

    gain_sum = grad_gain_in + swap(grad_gain_in, "dp", core)
    got_l, got_r, gain_sum, packed, out_normed = lax.optimization_barrier(
        (got_l, got_r, gain_sum, packed, out_normed)
    )
    output = (hidden.astype(F32) + mm(out_normed, output_w, NT)).astype(BF16)
    left, right = plus(keep_l, got_l), more_cols(plus(keep_r, got_r), rest)
    keep_l, give_l = fold_cols(left, tensor_top, rest)
    keep_r, give_r = pick(right, on_x), pick(right, 1 - on_x)
    bits = bits_of("tensor")
    sums = [("dp", bit) for bit in long] + [("tensor", bit) for bit in bits[:-1]]
    got_l, got_r, gain_sum, packed = lax.optimization_barrier(
        (
            swap(give_l, "tensor", tensor_top),
            swap(give_r, "dp", cross),
            sum_square(gain_sum, cross, tensor_top),
            packed + swap(packed, *sums[0]),
        )
    )
    left, right = more_cols(plus(keep_l, got_l), rest), plus(keep_r, got_r)
    on_z = side("dp", long[0]) == 1
    keep, give = jnp.where(on_z, left, right), jnp.where(on_z, right, left)
    pair = plus(keep_p, got_p)
    for k, bit in enumerate(long[1:]):
        got, gain_sum, packed = lax.optimization_barrier(
            (
                swap(give, "dp", bit >> 1),
                gain_sum + swap(gain_sum, *sums[k]),
                packed + swap(packed, *sums[k + 1]),
            )
        )
        keep_p, give_p = fold_rows(pair, bit, 1)
        pair = keep_p.astype(F32) + swap(give_p, "dp", bit).astype(F32)
        keep, give = fold_rows(plus(keep, got), bit)
    got = swap(give, "dp", long[-1])
    for axis, bit in sums[len(long) - 1 :]:
        gain_sum = gain_sum + swap(gain_sum, axis, bit)
    for axis, bit in sums[len(long) :]:
        packed = packed + swap(packed, axis, bit)
    joined = (keep.astype(F32) + got.astype(F32)).reshape(part_rows, -1)
    if len(bits) == 1:
        joined = in_order(joined, rest)
    packed = packed.reshape(-1)
    pair = pair.astype(F32).reshape(2, part_rows, part)
    grad_gate_w, grad_out_w = pair[0], pair[1]
    grad_inner_w = joined[:, :part]
    grad_shared_w = joined[:, part : part + shared]
    grad_rate_w = lax.dynamic_slice_in_dim(
        joined[:, part + shared :], tensor_pos * rate_part, rate_part, 1
    )
    sizes = [4 * inner, inner, inner, 4 * shared, shared, heads, heads, heads]
    pieces, at = [], 0
    for size in sizes:
        pieces.append(packed[at : at + size])
        at += size
    g_conv, g_conv_bias, g_out_gain, g_conv_sh, g_conv_sh_bias, g_rate_bias, g_decay, g_skip = pieces
    g_gain_in = gain_sum
    return (
        output, grad_hidden, g_gain_in, grad_gate_w, grad_inner_w, grad_shared_w, grad_rate_w,
        g_conv.reshape(4, inner), g_conv_bias, g_conv_sh.reshape(4, shared), g_conv_sh_bias,
        g_rate_bias, g_decay, g_skip, g_out_gain, grad_out_w,
    )


def solution(mesh):
    tokens = P(("dp", "tensor"), None)
    weight = P("dp", "tensor")
    in_specs = (
        tokens, P(), weight, weight, P("dp", None), weight, P(), P(), P(), P(), P(), P(), P(),
        P(), weight, tokens,
    )
    out_specs = (
        tokens, tokens, P(), weight, weight, P("dp", None), weight, P(), P(), P(), P(), P(),
        P(), P(), P(), weight,
    )
    return jax.shard_map(local, mesh=mesh, in_specs=in_specs, out_specs=out_specs, check_vma=False)
```

```python
import functools

import jax
import jax.numpy as jnp
from jax import lax
from jax.experimental import pallas as pl
from jax.experimental.pallas import tpu as pltpu
from jax.sharding import PartitionSpec as P

SEQ_LEN = 2048
CHUNK = 128
RIM = 16
LANES = 128
EPS = 1e-05
F32 = jnp.float32
BF16 = jnp.bfloat16


def mm(left, right, contract=((1,), (0,))):
    return lax.dot_general(left, right, (contract, ((), ())), preferred_element_type=F32)


NT = ((1,), (1,))
TN = ((0,), (0,))


def split3(value):
    high = value.astype(BF16)
    rest = value - high.astype(F32)
    mid = rest.astype(BF16)
    return high, mid, (rest - mid.astype(F32)).astype(BF16)


def exact_left(ones, value):
    high, mid, low = split3(value)
    return mm(ones, high) + mm(ones, mid) + mm(ones, low)


def exact_right(value, ones):
    high, mid, low = split3(value)
    return mm(high, ones) + mm(mid, ones) + mm(low, ones)


def spread_matrix(heads, inner):
    head_dim = inner // heads
    row = lax.broadcasted_iota(jnp.int32, (LANES, inner), 0)
    col = lax.broadcasted_iota(jnp.int32, (LANES, inner), 1)
    return ((col >= row * head_dim) & (col < (row + 1) * head_dim)).astype(BF16)


def iota2(shape, dim):
    return lax.broadcasted_iota(jnp.int32, shape, dim)


def softplus(v):
    return jnp.maximum(v, 0.0) + jnp.log1p(jnp.exp(-jnp.abs(v)))


def conv_rows(ext_ref, taps, bias, lo, width, rows):
    total = bias
    for k in range(4):
        total = total + taps[k : k + 1, :] * ext_ref[pl.ds(5 + k, rows), pl.ds(lo, width)]
    return total


def spread_columns(target_ref, rows, block, inner):
    half, shared = inner // 2, 2 * LANES
    target_ref[rows, :half] = block[:, :half]
    target_ref[rows, half:inner] = block[:, half + shared + LANES :]
    target_ref[rows, inner:] = block[:, half : half + shared]


def column_of(lo, inner):
    half = inner // 2
    if lo >= inner:
        return lo - inner + half
    return lo if lo < half else lo + 3 * LANES


def mix_in_kernel(
    inner, heads,
    proj_ref, rim_ref, final_in_ref, total_in_ref, tap_ref, bias_ref, rate_bias_ref, decay_ref,
    *rest,
):
    x_ref, bc_ref, step_ref, within_ref, slope_ref, final_ref, total_ref, ext_ref, u_ref = rest[-9:]
    i = pl.program_id(0)
    shared = 2 * LANES

    @pl.when(i == 0)
    def _():
        spread_columns(ext_ref, slice(0, 8), rim_ref[...].astype(F32)[RIM - 8 :], inner)
        final_ref[...] = final_in_ref[...]
        total_ref[...] = total_in_ref[...]

    @pl.when(i > 0)
    def _():
        ext_ref[0:8, :] = ext_ref[CHUNK : CHUNK + 8, :]

    spread_columns(ext_ref, slice(8, CHUNK + 8), proj_ref[...].astype(F32), inner)
    at = inner // 2 + shared
    step = softplus(proj_ref[:, at : at + LANES].astype(F32) + rate_bias_ref[...])
    log_decay = step * decay_ref[...]
    lower = (iota2((CHUNK, CHUNK), 0) >= iota2((CHUNK, CHUNK), 1)).astype(BF16)
    within = exact_left(lower, log_decay)
    step_ref[...] = step
    within_ref[...] = within
    last = within[CHUNK - 1 :, :]
    total_ref[...] += last
    weight = step * jnp.exp(last - within)

    pre = conv_rows(ext_ref, tap_ref[:, inner:], bias_ref[:, inner:], inner, shared, CHUNK)
    sig = jax.nn.sigmoid(pre)
    bc = (pre * sig).astype(BF16)
    bc_ref[...] = bc
    slope_ref[:, inner:] = (sig * (1.0 + pre * (1.0 - sig))).astype(BF16)
    first = iota2((CHUNK, LANES), 1) < LANES // 2
    for p in range(inner // LANES):
        lo = p * LANES
        pre = conv_rows(
            ext_ref, tap_ref[:, lo : lo + LANES], bias_ref[:, lo : lo + LANES], lo, LANES, CHUNK
        )
        sig = jax.nn.sigmoid(pre)
        act = pre * sig
        x = act.astype(BF16)
        x_ref[:, lo : lo + LANES] = x
        slope_ref[:, lo : lo + LANES] = (sig + act * (1.0 - sig)).astype(BF16)
        w = jnp.where(
            first,
            jnp.broadcast_to(weight[:, 2 * p : 2 * p + 1], (CHUNK, LANES)),
            jnp.broadcast_to(weight[:, 2 * p + 1 : 2 * p + 2], (CHUNK, LANES)),
        )
        u_ref[:, lo : lo + LANES] = (x.astype(F32) * w).astype(BF16)
    factor = exact_right(jnp.exp(jnp.broadcast_to(last, (8, LANES))), spread_matrix(heads, inner))
    final_ref[...] = factor[0:1, :] * final_ref[...] + mm(bc[:, :LANES], u_ref[...], TN)


def mix_in(proj, rows, carried, consts, inner, heads, start, count, held=()):
    width = proj.shape[1]
    full = lambda shape: pl.BlockSpec(shape, lambda i: (0,) * len(shape))
    block = lambda w: pl.BlockSpec((CHUNK, w), lambda i: (start + i, 0))
    before = start * CHUNK // RIM - 1 if start else rows // RIM
    operands = [proj, proj, *carried, *consts, *held]
    return pl.pallas_call(
        functools.partial(mix_in_kernel, inner, heads),
        grid=(count,),
        in_specs=[
            block(width),
            pl.BlockSpec((RIM, width), lambda i: (before, 0)),
            *[full(v.shape) for v in (*carried, *consts)],
            *[pl.BlockSpec(memory_space=pl.ANY) for _ in held],
        ],
        out_specs=[
            block(inner), block(2 * LANES), block(LANES), block(LANES), block(inner + 2 * LANES),
            full((LANES, inner)), full((1, LANES)),
        ],
        out_shape=[
            jax.ShapeDtypeStruct((rows, inner), BF16),
            jax.ShapeDtypeStruct((rows, 2 * LANES), BF16),
            jax.ShapeDtypeStruct((rows, LANES), F32),
            jax.ShapeDtypeStruct((rows, LANES), F32),
            jax.ShapeDtypeStruct((rows, inner + 2 * LANES), BF16),
            jax.ShapeDtypeStruct((LANES, inner), F32),
            jax.ShapeDtypeStruct((1, LANES), F32),
        ],
        input_output_aliases={len(operands) - len(held) + k: k for k in range(len(held))},
        scratch_shapes=[
            pltpu.VMEM((CHUNK + 8, inner + 2 * LANES), F32),
            pltpu.VMEM((CHUNK, inner), BF16),
        ],
        compiler_params=pltpu.CompilerParams(vmem_limit_bytes=48 * 2**20),
        cost_estimate=pl.CostEstimate(
            flops=14000 * count * CHUNK * inner, bytes_accessed=8 * count * CHUNK * inner, transcendentals=0
        ),
        name="mix_in",
    )(*operands)


def mix_out_kernel(
    inner, heads,
    x_ref, bc_ref, step_ref, within_ref, gate_ref, gon_ref, entry_ref, skip_ref, gain_ref,
    normed_ref, gm_ref, gg_ref, state_ref, grad_entry_ref, sums_ref,
    hold_ref, y_ref, u_ref, prefix_ref, grow_ref, sig_ref,
):
    i = pl.program_id(0)

    @pl.when(i == 0)
    def _():
        hold_ref[...] = entry_ref[...].astype(F32)
        grad_entry_ref[...] = jnp.zeros_like(grad_entry_ref)
        sums_ref[...] = jnp.zeros_like(sums_ref)
        prefix_ref[...] = jnp.zeros_like(prefix_ref)

    spread = spread_matrix(heads, inner)
    key, query = bc_ref[:, :LANES], bc_ref[:, LANES:]
    within = within_ref[...]
    within_t = within.T
    last = within[CHUNK - 1 :, :]
    state = hold_ref[...].astype(BF16)
    state_ref[0] = state
    y_ref[...] = mm(query, state)
    scores = mm(query, key, NT)
    causal = iota2((CHUNK, CHUNK), 0) >= iota2((CHUNK, CHUNK), 1)
    first = iota2((CHUNK, LANES), 1) < LANES // 2
    zero = jnp.zeros((CHUNK, LANES), BF16)
    for p in range(inner // LANES):
        lo = p * LANES
        slab = slice(lo, lo + LANES)
        cols, weights = [], []
        for h in (2 * p, 2 * p + 1):
            col = jnp.broadcast_to(within[:, h : h + 1], (CHUNK, CHUNK))
            gap = jnp.where(causal, col - within_t[h : h + 1, :], -1e30)
            weights.append((scores * jnp.exp(gap)).astype(BF16))
            cols.append(col)
        a = jnp.where(first, cols[0], cols[1])
        d = jnp.where(
            first,
            jnp.broadcast_to(step_ref[:, 2 * p : 2 * p + 1], (CHUNK, LANES)),
            jnp.broadcast_to(step_ref[:, 2 * p + 1 : 2 * p + 2], (CHUNK, LANES)),
        )
        x = x_ref[:, slab].astype(F32)
        u = x * d
        ub = u.astype(BF16)
        u_ref[:, slab] = (u * jnp.exp(a[CHUNK - 1 :, :] - a)).astype(BF16)
        both = mm(jnp.concatenate(weights, axis=0), ub)
        diagonal = jnp.where(first, both[:CHUNK], both[CHUNK:])
        grow = jnp.exp(a)
        grow_ref[:, slab] = grow
        y_ref[:, slab] = diagonal + grow * y_ref[:, slab] + skip_ref[:, slab] * x
    factors = exact_right(
        jnp.exp(jnp.concatenate([last, prefix_ref[...], jnp.zeros((6, LANES), F32)], axis=0)),
        spread,
    )
    prefix_ref[...] += last
    hold_ref[...] = factors[0:1, :] * hold_ref[...] + mm(key, u_ref[...], TN)

    square = jnp.zeros((CHUNK, LANES), F32)
    dot = jnp.zeros((CHUNK, LANES), F32)
    for p in range(inner // LANES):
        slab = slice(p * LANES, (p + 1) * LANES)
        z = gate_ref[:, slab].astype(F32)
        m = y_ref[:, slab].astype(BF16).astype(F32)
        sig = jax.nn.sigmoid(z)
        sig_ref[:, slab] = sig
        gated = m * (z * sig)
        square = square + gated * gated
        dot = dot + gain_ref[:, slab] * gon_ref[:, slab].astype(F32) * gated
    square = jnp.sum(square, axis=1, keepdims=True)
    dot = jnp.sum(dot, axis=1, keepdims=True)
    root = lax.rsqrt(square / inner + EPS)
    pull = root * root * root * dot / inner
    for p in range(inner // LANES):
        slab = slice(p * LANES, (p + 1) * LANES)
        z = gate_ref[:, slab].astype(F32)
        m = y_ref[:, slab].astype(BF16).astype(F32)
        sig = sig_ref[:, slab]
        act = z * sig
        gated = m * act
        gon = gon_ref[:, slab].astype(F32)
        unit = gated * root
        normed_ref[:, slab] = (unit * gain_ref[:, slab]).astype(BF16)
        grad = root * gain_ref[:, slab] * gon - gated * pull
        gm = (grad * act).astype(BF16)
        gm_ref[:, slab] = gm
        gg_ref[:, slab] = (grad * m * (sig * (1.0 + z * (1.0 - sig)))).astype(BF16)
        gmf = gm.astype(F32)
        sums_ref[0:1, slab] += jnp.sum(gon * unit, axis=0, keepdims=True)
        sums_ref[1:2, slab] += jnp.sum(gmf * x_ref[:, slab].astype(F32), axis=0, keepdims=True)
        u_ref[:, slab] = (gmf * grow_ref[:, slab]).astype(BF16)
    grad_entry_ref[...] += factors[1:2, :] * mm(query, u_ref[...], TN)


def mix_out(x, bc, step, within, gate, gon, entry, skip, gain, heads):
    rows, inner = x.shape
    chunks = rows // CHUNK
    full = lambda shape: pl.BlockSpec(shape, lambda i: (0,) * len(shape))
    block = lambda width: pl.BlockSpec((CHUNK, width), lambda i: (i, 0))
    return pl.pallas_call(
        functools.partial(mix_out_kernel, inner, heads),
        grid=(chunks,),
        in_specs=[
            block(inner), block(2 * LANES), block(LANES), block(LANES), block(inner), block(inner),
            full(entry.shape), full(skip.shape), full(gain.shape),
        ],
        out_specs=[
            block(inner), block(inner), block(inner),
            pl.BlockSpec((1, LANES, inner), lambda i: (i, 0, 0)),
            full((LANES, inner)), full((8, inner)),
        ],
        out_shape=[
            jax.ShapeDtypeStruct((rows, inner), BF16),
            jax.ShapeDtypeStruct((rows, inner), BF16),
            jax.ShapeDtypeStruct((rows, inner), BF16),
            jax.ShapeDtypeStruct((chunks, LANES, inner), BF16),
            jax.ShapeDtypeStruct((LANES, inner), F32),
            jax.ShapeDtypeStruct((8, inner), F32),
        ],
        scratch_shapes=[
            pltpu.VMEM((LANES, inner), F32),
            pltpu.VMEM((CHUNK, inner), F32),
            pltpu.VMEM((CHUNK, inner), BF16),
            pltpu.VMEM((1, LANES), F32),
            pltpu.VMEM((CHUNK, inner), F32),
            pltpu.VMEM((CHUNK, inner), F32),
        ],
        compiler_params=pltpu.CompilerParams(vmem_limit_bytes=48 * 2**20),
        cost_estimate=pl.CostEstimate(
            flops=17000 * rows * inner, bytes_accessed=16 * rows * inner, transcendentals=0
        ),
        name="mix_out",
    )(x, bc, step, within, gate, gon, entry, skip, gain)


def mix_back_kernel(
    inner, heads, count, inside, rim_step,
    x_ref, bc_ref, step_ref, within_ref, gm_ref, state_ref, proj_ref, slope_ref, rim_ref,
    exit_ref, next_ref, sums_in_ref, heads_in_ref,
    skip_ref, tap_ref, rate_bias_ref, decay_ref,
    *rest,
):
    if inside:
        rest = rest[1:]
    (
        gproj_ref, hold_ref, head_ref, sums_ref, heads_ref,
        ext_ref, ahead_ref, cs_ref, bg_ref, ue_ref, ge_ref, prod_ref, rows_ref,
    ) = rest
    j = pl.program_id(0)
    shared = 2 * LANES
    conv_width = inner + shared

    @pl.when(j == 0)
    def _():
        hold_ref[...] = exit_ref[...].astype(F32)
        sums_ref[...] = sums_in_ref[...]
        heads_ref[...] = heads_in_ref[...]
        ahead_ref[CHUNK:, :] = next_ref[...]
        rows_ref[...] = jnp.zeros_like(rows_ref)

    @pl.when((j > 0) & (j < count))
    def _():
        ahead_ref[CHUNK:, :] = ahead_ref[0:8, :]

    @pl.when(j < count)
    def _():
        spread = spread_matrix(heads, inner)
        key, query = bc_ref[:, :LANES], bc_ref[:, LANES:]
        within = within_ref[...]
        within_t = within.T
        step = step_ref[...]
        last = within[CHUNK - 1 :, :]
        state = state_ref[0]
        hold = hold_ref[...]
        exit_grad = hold.astype(BF16)
        cs_ref[...] = mm(query, state)
        bg_ref[...] = mm(key, exit_grad)
        scores_t = mm(key, query, NT)
        causal_t = iota2((CHUNK, CHUNK), 0) <= iota2((CHUNK, CHUNK), 1)
        first = iota2((CHUNK, LANES), 1) < LANES // 2
        lane = iota2((2 * CHUNK, LANES), 1)
        upper_half = iota2((2 * CHUNK, LANES), 0) >= CHUNK
        zero = jnp.zeros((CHUNK, LANES), BF16)
        grad_scores_t = jnp.zeros((CHUNK, CHUNK), F32)
        col_sums = jnp.zeros((CHUNK, LANES), F32)
        for p in range(inner // LANES):
            slab = slice(p * LANES, (p + 1) * LANES)
            x = x_ref[:, slab].astype(F32)
            gb = gm_ref[:, slab]
            g = gb.astype(F32)
            cols = [
                jnp.broadcast_to(within[:, h : h + 1], (CHUNK, LANES)) for h in (2 * p, 2 * p + 1)
            ]
            a = jnp.where(first, cols[0], cols[1])
            d = jnp.where(
                first,
                jnp.broadcast_to(step[:, 2 * p : 2 * p + 1], (CHUNK, LANES)),
                jnp.broadcast_to(step[:, 2 * p + 1 : 2 * p + 2], (CHUNK, LANES)),
            )
            u = x * d
            ub = u.astype(BF16)
            to_end = jnp.exp(a[CHUNK - 1 :, :] - a)
            ge = g * jnp.exp(a)
            ge_ref[:, slab] = ge.astype(BF16)
            ue_ref[:, slab] = (u * to_end).astype(BF16)
            ucat = jnp.concatenate([jnp.where(first, ub, zero), jnp.where(first, zero, ub)], axis=0)
            reach_t = mm(ucat, gb, NT)
            pieces, moves = [], []
            for q, h in enumerate((2 * p, 2 * p + 1)):
                gap = jnp.where(causal_t, within_t[h : h + 1, :] - cols[q], -1e30)
                weight = jnp.exp(gap)
                grad_score = reach_t[q * CHUNK : (q + 1) * CHUNK] * weight
                grad_scores_t = grad_scores_t + grad_score
                pieces.append((scores_t * weight).astype(BF16))
                move = grad_score * scores_t
                moves.append(move)
                rows_ref[h : h + 1, :] = jnp.sum(move, axis=0, keepdims=True)
                col = jnp.sum(move, axis=1, keepdims=True)
                col_sums = jnp.where(lane[:CHUNK] == h, col, col_sums)
            pick = (lane == jnp.where(upper_half, 2 * p + 1, 2 * p)).astype(BF16)
            grad_state_u = to_end * bg_ref[:, slab]
            both = mm(jnp.concatenate(pieces, axis=0), gb)
            grad_u = jnp.where(first, both[:CHUNK], both[CHUNK:]) + grad_state_u
            prod_ref[0:CHUNK, slab] = (x * grad_u).astype(BF16)
            prod_ref[CHUNK : 2 * CHUNK, slab] = (u * grad_state_u).astype(BF16)
            prod_ref[2 * CHUNK :, slab] = (ge * cs_ref[:, slab]).astype(BF16)
            grad_x = d * grad_u + skip_ref[:, slab] * g
            ahead_ref[0:CHUNK, slab] = grad_x * slope_ref[:, slab].astype(F32)

        by_head = mm(prod_ref[...], spread, NT)
        grad_step = by_head[0:CHUNK]
        from_state = by_head[CHUNK : 2 * CHUNK]
        from_entry = by_head[2 * CHUNK :]
        factor = exact_right(jnp.exp(jnp.broadcast_to(last, (8, LANES))), spread)[0:1, :]
        whole = jnp.sum(hold * state.astype(F32), axis=0, keepdims=True) * factor
        whole = jnp.broadcast_to(whole, (8, inner))
        high, mid, _ = split3(whole)
        whole = (mm(high, spread, NT) + mm(mid, spread, NT))[0:1, :]
        later = (iota2((CHUNK, CHUNK), 0) <= iota2((CHUNK, CHUNK), 1)).astype(BF16)
        earlier = (iota2((CHUNK, CHUNK), 0) > iota2((CHUNK, CHUNK), 1)).astype(BF16)
        row_sums = rows_ref[...].T
        grad_log = (
            exact_left(later, row_sums - col_sums + from_entry)
            + exact_left(earlier, from_state)
            + whole
        )
        decay = decay_ref[...]
        grad_step = grad_step + grad_log * decay
        rates = slice(inner // 2 + shared, inner // 2 + shared + LANES)
        squash = jax.nn.sigmoid(proj_ref[:, rates].astype(F32) + rate_bias_ref[...])
        grad_rate = grad_step * squash
        gproj_ref[:, rates] = grad_rate.astype(BF16)
        heads_ref[0:1, :] += jnp.sum(grad_rate, axis=0, keepdims=True)
        heads_ref[1:2, :] += jnp.sum(grad_log * step, axis=0, keepdims=True) * decay

        gsb = grad_scores_t.astype(BF16)
        grad_key = mm(ue_ref[...], exit_grad, NT) + mm(gsb, query)
        grad_query = mm(ge_ref[...], state, NT) + mm(gsb, key, TN)
        hold_ref[...] = factor * hold + mm(query, ge_ref[...], TN)

        slope = slope_ref[:, inner:].astype(F32)
        ahead_ref[0:CHUNK, inner:] = jnp.concatenate([grad_key, grad_query], axis=1) * slope

        for p in range(conv_width // LANES):
            slab = slice(p * LANES, (p + 1) * LANES)
            lo = column_of(p * LANES, inner)
            values = proj_ref[:, lo : lo + LANES].astype(F32)
            total = jnp.zeros((CHUNK, LANES), F32)
            for k in range(4):
                moved = ahead_ref[pl.ds(3 - k, CHUNK), slab]
                total = total + tap_ref[k : k + 1, slab] * moved
                sums_ref[k : k + 1, slab] += jnp.sum(values * moved, axis=0, keepdims=True)
                if k == 3:
                    sums_ref[4:5, slab] += jnp.sum(moved, axis=0, keepdims=True)
            gproj_ref[:, lo : lo + LANES] = total.astype(BF16)
        head_ref[...] = ahead_ref[0:8, :]

    if not rim_step:
        return

    @pl.when(j == count)
    def _():
        gproj_ref[...] = jnp.zeros_like(gproj_ref)
        head = ahead_ref[0:8, :]
        at = iota2((8, conv_width), 0)
        spread_columns(ext_ref, slice(0, 8), rim_ref[...].astype(F32)[RIM - 8 :], inner)
        values = ext_ref[0:8, :]
        total = jnp.zeros((8, conv_width), F32)
        for k in range(3):
            moved = jnp.zeros((8, conv_width), F32)
            for r in range(5 + k, 8):
                t = r - 5 - k
                moved = moved + jnp.where(at == r, head[t : t + 1, :], 0.0)
            total = total + tap_ref[k : k + 1, :] * moved
            sums_ref[k : k + 1, :] += jnp.sum(values * moved, axis=0, keepdims=True)
        total = jnp.concatenate([jnp.zeros((RIM - 8, conv_width), F32), total], axis=0)
        total = total.astype(BF16)
        half = inner // 2
        gproj_ref[0:RIM, :half] = total[:, :half]
        gproj_ref[0:RIM, half : half + shared] = total[:, inner:]
        gproj_ref[0:RIM, half + shared + LANES :] = total[:, half:inner]


def mix_back(x, bc, step, within, gm, state, proj, slope, carried, consts, heads, top, count, gproj,
             rim_step):
    inside = gproj is not None
    rows, inner = x.shape
    width = proj.shape[1]
    chunks = rows // CHUNK
    conv_width = inner + 2 * LANES
    full = lambda shape: pl.BlockSpec(shape, lambda j: (0,) * len(shape))
    at = lambda j: jnp.maximum(top - j, top - count + 1)
    block = lambda w: pl.BlockSpec((CHUNK, w), lambda j: (at(j), 0))
    operands = [x, bc, step, within, gm, state, proj, slope, proj, *carried, *consts]
    in_specs = [
        block(inner), block(2 * LANES), block(LANES), block(LANES), block(inner),
        pl.BlockSpec((1, LANES, inner), lambda j: (at(j), 0, 0)),
        block(width),
        block(conv_width),
        pl.BlockSpec((RIM, width), lambda j: (rows // RIM, 0)),
        *[full(v.shape) for v in (*carried, *consts)],
    ]
    if inside:
        operands.append(gproj)
        in_specs.append(pl.BlockSpec(memory_space=pl.ANY))
    return pl.pallas_call(
        functools.partial(mix_back_kernel, inner, heads, count, inside, rim_step),
        grid=(count + 1 if rim_step else count,),
        in_specs=in_specs,
        out_specs=[
            pl.BlockSpec((CHUNK, width), lambda j: (jnp.where(j == count, chunks, at(j)), 0)),
            full((LANES, inner)), full((8, conv_width)), full((8, conv_width)), full((8, LANES)),
        ],
        out_shape=[
            jax.ShapeDtypeStruct((rows + CHUNK, width), BF16),
            jax.ShapeDtypeStruct((LANES, inner), F32),
            jax.ShapeDtypeStruct((8, conv_width), F32),
            jax.ShapeDtypeStruct((8, conv_width), F32),
            jax.ShapeDtypeStruct((8, LANES), F32),
        ],
        scratch_shapes=[
            pltpu.VMEM((8, conv_width), F32),
            pltpu.VMEM((CHUNK + 8, conv_width), F32),
            pltpu.VMEM((CHUNK, inner), F32),
            pltpu.VMEM((CHUNK, inner), F32),
            pltpu.VMEM((CHUNK, inner), BF16),
            pltpu.VMEM((CHUNK, inner), BF16),
            pltpu.VMEM((3 * CHUNK, inner), BF16),
            pltpu.VMEM((LANES, CHUNK), F32),
        ],
        input_output_aliases={len(operands) - 1: 0} if inside else {},
        compiler_params=pltpu.CompilerParams(vmem_limit_bytes=48 * 2**20),
        cost_estimate=pl.CostEstimate(
            flops=32768 * count * CHUNK * inner, bytes_accessed=16 * count * CHUNK * inner,
            transcendentals=0,
        ),
        name="mix_back",
    )(*operands)


def swap(value, axis, bit):
    size = lax.axis_size(axis)
    return lax.ppermute(value, axis, [(i, i ^ bit) for i in range(size)])


def bits_of(axis):
    size = lax.axis_size(axis)
    return [1 << k for k in range(size.bit_length() - 1)]


def join(value, axis, bit, dim):
    return beside(value, swap(value, axis, bit), axis, bit, dim)


def beside(value, other, axis, bit, dim):
    high = (lax.axis_index(axis) & bit) != 0
    return jnp.where(high, jnp.stack([other, value], axis=dim), jnp.stack([value, other], axis=dim))


def join_cols(value):
    for bit in bits_of("tensor"):
        other = swap(value, "tensor", bit)
        high = (lax.axis_index("tensor") & bit) != 0
        value = jnp.where(
            high,
            jnp.concatenate([other, value], axis=-1),
            jnp.concatenate([value, other], axis=-1),
        )
    return value


def join_dp(stack, bits, done):
    for bit in bits:
        stack = join(stack, "dp", bit, done)
        done += 1
    return stack


def side(axis, bit):
    return jnp.where((lax.axis_index(axis) & bit) != 0, 1, 0)


def fold_rows(value, bit, dim=0):
    mine = side("dp", bit)
    shape = value.shape
    pairs = value.reshape(*shape[:dim], shape[dim] // 2, 2, *shape[dim + 1 :])
    pick = lambda k: lax.dynamic_index_in_dim(pairs, k, dim + 1, keepdims=False)
    return pick(mine), pick(1 - mine)


def fold_cols(value, bit, rest=0):
    high = side("tensor", bit) == 1
    half = (value.shape[-1] - rest) // 2
    low_part, high_part = value[..., : half + rest], value[..., half:]
    return jnp.where(high, high_part, low_part), jnp.where(high, low_part, high_part)


def plus(keep, got):
    return (keep.astype(F32) + got.astype(F32)).astype(BF16)


def in_order(value, rest):
    high = side("tensor", lax.axis_size("tensor") // 2) == 1
    half = value.shape[-1] - rest
    turned = jnp.concatenate([value[..., rest:], value[..., :rest]], axis=-1)
    return jnp.where(high, turned, value)


def more_cols(value, rest=0):
    bits = bits_of("tensor")[-2::-1]
    if not bits:
        return value
    if rest:
        value = in_order(value, rest)
    for bit in bits:
        width = value.shape[-1] - rest
        keep, give = fold_cols(value[..., :width], bit)
        tail = value[..., width:]
        give = jnp.concatenate([give, tail], axis=-1)
        value = plus(jnp.concatenate([keep, tail], axis=-1), swap(give, "tensor", bit))
    return value


def local(
    hidden, input_gain, proj_gate, proj_inner, proj_shared, proj_rate, conv_inner,
    conv_inner_bias, conv_shared, conv_shared_bias, rate_bias, decay_log, skip_gain,
    output_gain, proj_output, cotangent,
):
    tensor_size = lax.axis_size("tensor")
    tensor_pos = lax.axis_index("tensor")
    rows, features = hidden.shape
    heads = rate_bias.shape[0]
    inner = output_gain.shape[0]
    shared = conv_shared.shape[1]
    head_dim = inner // heads
    conv_width = inner + shared
    per_seq = SEQ_LEN // rows
    seq_pos = lax.rem(tensor_pos, per_seq)
    part = inner // tensor_size
    rate_part = heads // tensor_size
    forward = [(i, i + 1) for i in range(tensor_size - 1)]
    backward = [(i + 1, i) for i in range(tensor_size - 1)]

    dp_bits = bits_of("dp")
    far, near = dp_bits[:0:-1], dp_bits[:1]
    dp_size, part_rows = lax.axis_size("dp"), proj_inner.shape[0]
    far_z, far_x = far[:-1], far[-1:]
    shared_part = shared // tensor_size
    rate_block = lax.dynamic_update_slice(
        jnp.zeros((part_rows, LANES), BF16), proj_rate, (0, tensor_pos * rate_part)
    )
    shared_block = lax.dynamic_slice_in_dim(proj_shared, tensor_pos * shared_part, shared_part, 1)
    piece = jnp.concatenate([proj_inner, shared_block, rate_block], axis=1)
    first_w = join_dp(piece, far_z, 0)
    first_w, both_w, rim = lax.optimization_barrier(
        (first_w, jnp.concatenate([proj_output, proj_gate], axis=1), hidden[rows - RIM :])
    )
    both_w = join_dp(both_w, far_z[:1], 0)
    upper, lower = join_cols(first_w[0]), join_dp(first_w[1], far_x, len(far_z) - 1)
    rim = lax.ppermute(rim, "tensor", forward)
    upper, lower, rim = lax.optimization_barrier((upper, lower, rim))
    upper, lower = join_dp(upper, far_x, len(far_z) - 1), join_cols(lower)
    first_w, both_w = lax.optimization_barrier((jnp.stack([upper, lower]), both_w))
    pieces = [
        first_w[..., k * piece.shape[1] : (k + 1) * piece.shape[1]] for k in range(tensor_size)
    ]
    inner_cols = [v[..., :part] for v in pieces]
    rate_cols = sum(v[..., part + shared_part :] for v in pieces)
    first_w = jnp.concatenate(
        inner_cols[: tensor_size // 2]
        + [v[..., part : part + shared_part] for v in pieces]
        + [rate_cols]
        + inner_cols[tensor_size // 2 :],
        axis=-1,
    )
    first_w = join_dp(first_w, near, len(far)).reshape(dp_size * part_rows, -1)
    first_w, both_w = lax.optimization_barrier((first_w, join_dp(both_w, far_z[1:], 1)))
    output_w, gate_w = both_w[..., :part], both_w[..., part:]
    gate_w = join_dp(gate_w, far_x, len(far_z))
    output_w = join_cols(output_w)

    rim = jnp.where(seq_pos == 0, jnp.zeros_like(rim), rim)
    extended = jnp.pad(
        jnp.concatenate([hidden, rim], axis=0), ((0, CHUNK - RIM), (0, 0))
    ).astype(F32)
    gain_in = input_gain.astype(F32)
    root = lax.rsqrt(jnp.mean(extended * extended, axis=-1, keepdims=True) + EPS)
    normed = (extended * root * gain_in).astype(BF16)

    proj = mm(normed, first_w).astype(BF16)
    proj, gate_w, output_w = lax.optimization_barrier((proj, gate_w, output_w))
    gate_w = join_cols(gate_w)
    output_w = join_dp(output_w, far_x, len(far_z))
    taps = jnp.concatenate([conv_inner, conv_shared], axis=1).astype(F32)
    bias = jnp.concatenate([conv_inner_bias, conv_shared_bias])[None].astype(F32)
    pad_heads = lambda v: jnp.pad(v, (0, LANES - heads))[None]
    rate_bias_row = pad_heads(rate_bias)
    decay_row = pad_heads(-jnp.exp(decay_log))
    skip_row = jnp.repeat(skip_gain, head_dim)[None]
    gain_row = output_gain[None].astype(F32)
    chunks = rows // CHUNK
    lead_count = chunks - max(chunks // 4, 1)
    consts = [taps, bias, rate_bias_row, decay_row]
    *held, final, total = mix_in(
        proj, rows, [jnp.zeros((LANES, inner), F32), jnp.zeros((1, LANES), F32)], consts, inner,
        heads, 0, lead_count,
    )
    final, gate_w, output_w = lax.optimization_barrier((final, gate_w, output_w))
    gate_near, output_near = swap(gate_w, "dp", near[0]), swap(output_w, "dp", near[0])
    x, bc, step, within, slope, final, total = mix_in(
        proj, rows, [final, total], consts, inner, heads, lead_count, chunks - lead_count, held
    )
    final, gate_near, output_near = lax.optimization_barrier((final, gate_near, output_near))
    whole = jnp.repeat(jnp.exp(total[0, :heads]), head_dim)[None]
    entry = jnp.zeros_like(final)
    for _ in range(per_seq - 1):
        sent = lax.ppermute((final + whole * entry).astype(BF16), "tensor", forward)
        entry = jnp.where(seq_pos == 0, 0.0, sent.astype(F32))

    gate_w = beside(gate_w, gate_near, "dp", near[0], len(far)).reshape(dp_size * part_rows, inner)
    output_w = beside(output_w, output_near, "dp", near[0], len(far))
    output_w = output_w.reshape(dp_size * part_rows, inner)
    gate = mm(normed[:rows], gate_w).astype(BF16)
    gon = mm(cotangent, output_w).astype(BF16)
    out_normed, grad_mixed, grad_gate, states, grad_entry, out_sums = mix_out(
        x, bc, step, within, gate, gon, entry, skip_row, gain_row, heads
    )
    exit_grad = jnp.zeros_like(grad_entry)
    for _ in range(per_seq - 1):
        sent = lax.ppermute((grad_entry + whole * exit_grad).astype(BF16), "tensor", backward)
        exit_grad = jnp.where(seq_pos == per_seq - 1, 0.0, sent.astype(F32))

    core, cross, long = dp_bits[0], dp_bits[1], dp_bits[2:]
    tensor_top = bits_of("tensor")[-1]
    blocks = lambda v: v.astype(BF16).reshape(dp_size, part_rows, -1)
    grad_out_w = blocks(mm(cotangent, out_normed, TN))
    grad_gate_w = mm(normed[:rows], grad_gate, TN)
    gain_gate = jnp.sum(grad_gate_w * gate_w.astype(F32), axis=1)
    grad_gate_w = blocks(grad_gate_w)
    keep_o, give_o = fold_rows(grad_out_w, core)
    keep_g, give_g = fold_rows(grad_gate_w, core)
    exit_grad, give_o, give_g = lax.optimization_barrier((exit_grad, give_o, give_g))
    got_o, got_g = swap(give_o, "dp", core), swap(give_g, "dp", core)

    consts = [skip_row, taps, rate_bias_row, decay_row]
    counts = [chunks // 4, (chunks - chunks // 4) // 2]
    counts.append(chunks - sum(counts))
    tops = [chunks - 1, chunks - 1 - counts[0], counts[2] - 1]
    carried = [
        exit_grad, jnp.zeros((8, conv_width), F32), jnp.zeros((8, conv_width), F32),
        jnp.zeros((8, LANES), F32),
    ]
    back = lambda k, *more: mix_back(
        x, bc, step, within, grad_mixed, states, proj, slope, carried, consts, heads, tops[k], counts[k],
        *more,
    )
    grad_proj, *carried = back(0, None, False)
    grad_proj, got_g, got_o = lax.optimization_barrier((grad_proj, got_g, got_o))
    keep_g, give_g = fold_rows(plus(keep_g, got_g), cross)
    keep_o, give_o = fold_cols(plus(keep_o, got_o), tensor_top)
    grad_proj, give_g, give_o = lax.optimization_barrier((grad_proj, give_g, give_o))
    got_g, got_o = swap(give_g, "dp", cross), swap(give_o, "tensor", tensor_top)
    grad_proj, *carried = back(1, grad_proj, False)
    grad_proj, got_g, got_o = lax.optimization_barrier((grad_proj, got_g, got_o))
    keep_g, give_g = fold_cols(plus(keep_g, got_g), tensor_top)
    keep_o, give_o = fold_rows(more_cols(plus(keep_o, got_o)), cross)
    grad_proj, give_g, give_o = lax.optimization_barrier((grad_proj, give_g, give_o))
    got_g, got_o = swap(give_g, "tensor", tensor_top), swap(give_o, "dp", cross)
    grad_proj, _, _, conv_sums, head_sums = back(2, grad_proj, True)
    grad_proj, got_g, got_o = lax.optimization_barrier((grad_proj, got_g, got_o))

    rest = shared + LANES
    first = mm(normed, grad_proj, TN)
    gain_first = jnp.sum(first * first_w.astype(F32), axis=1)
    first = blocks(first)
    keep, give = fold_rows(first, core)
    grad_proj, give = lax.optimization_barrier((grad_proj, give))
    got = swap(give, "dp", core)
    tail = jnp.concatenate(
        [
            conv_sums[:5, inner:].reshape(-1),
            head_sums[0, :heads],
            head_sums[1, :heads],
            jnp.sum(out_sums[1].reshape(heads, head_dim), axis=1),
            (gain_first + gain_gate) / gain_in,
        ]
    )
    packed = jnp.concatenate([conv_sums[:5, :inner].reshape(-1), out_sums[0], tail])
    packed = jnp.pad(packed, (0, -packed.shape[0] % 1024)).reshape(-1, LANES)

    got_s = swap(packed, "dp", core)
    grad_ext = mm(grad_proj, first_w, NT)
    grad_ext, got, got_s = lax.optimization_barrier((grad_ext, got, got_s))
    packed = packed + got_s
    first = plus(keep, got)
    first = first.reshape(first.shape[0] // 4, 2, 2, part_rows, first.shape[-1])
    pick = lambda v, k: lax.dynamic_index_in_dim(v, k, 1, keepdims=False)
    on_x = side("dp", cross)
    left, right = first[:, 1], first[:, 0]
    keep_l, give_l = pick(left, on_x), pick(left, 1 - on_x)
    keep_r, give_r = fold_cols(right, tensor_top, rest)
    give_l, give_r, grad_ext, grad_gate, got_o, got_g, packed, out_normed = (
        lax.optimization_barrier(
            (give_l, give_r, grad_ext, grad_gate, got_o, got_g, packed, out_normed)
        )
    )
    got_l, got_r = swap(give_l, "dp", cross), swap(give_r, "tensor", tensor_top)
    gate_back = mm(grad_gate, gate_w, NT)
    packed = packed + swap(packed, "dp", cross)
    pair = jnp.stack([more_cols(plus(keep_g, got_g)), plus(keep_o, got_o)])
    keep_p, give_p = fold_rows(pair, long[0], 1)
    got_p = swap(give_p, "dp", long[0])
    rim_grad = lax.ppermute(grad_ext[rows : rows + RIM], "tensor", backward)
    rim_grad = jnp.where(seq_pos == per_seq - 1, 0.0, rim_grad)
    grad_normed = grad_ext[:rows] + gate_back
    grad_normed = grad_normed + jnp.pad(rim_grad, ((rows - RIM, 0), (0, 0)))
    unit = hidden.astype(F32) * root[:rows]
    scaled = grad_normed * gain_in
    grad_hidden = (
        cotangent.astype(F32)
        + root[:rows] * (scaled - unit * jnp.mean(scaled * unit, axis=-1, keepdims=True))
    ).astype(BF16)

    output = (hidden.astype(F32) + mm(out_normed, output_w, NT)).astype(BF16)
    got_l, got_r, got_p, packed, output = lax.optimization_barrier(
        (got_l, got_r, got_p, packed, output)
    )
    pair = plus(keep_p, got_p)
    for bit in long[1:]:
        keep_p, give_p = fold_rows(pair, bit, 1)
        pair = plus(keep_p, swap(give_p, "dp", bit))
    left, right = plus(keep_l, got_l), more_cols(plus(keep_r, got_r), rest)
    keep_l, give_l = fold_cols(left, tensor_top, rest)
    keep_r, give_r = pick(right, on_x), pick(right, 1 - on_x)
    bits = bits_of("tensor")
    sums = [("tensor", bit) for bit in bits] + [("dp", bit) for bit in long]
    got_l, got_r, packed, pair = lax.optimization_barrier(
        (
            swap(give_l, "tensor", tensor_top),
            swap(give_r, "dp", cross),
            packed + swap(packed, *sums[0]),
            pair,
        )
    )
    left, right = more_cols(plus(keep_l, got_l), rest), plus(keep_r, got_r)
    on_z = side("dp", long[0]) == 1
    keep, give = jnp.where(on_z, left, right), jnp.where(on_z, right, left)
    for k, bit in enumerate(long[1:]):
        got, packed = lax.optimization_barrier(
            (swap(give, "dp", bit >> 1), packed + swap(packed, *sums[k + 1]))
        )
        keep, give = fold_rows(plus(keep, got), bit)
    got = swap(give, "dp", long[-1])
    for axis, bit in sums[len(long) :]:
        packed = packed + swap(packed, axis, bit)
    joined = (keep.astype(F32) + got.astype(F32)).reshape(part_rows, -1)
    if len(bits) == 1:
        joined = in_order(joined, rest)
    packed = packed.reshape(-1)
    pair = pair.astype(F32).reshape(2, part_rows, part)
    grad_gate_w, grad_out_w = pair[0], pair[1]
    grad_inner_w = joined[:, :part]
    grad_shared_w = joined[:, part : part + shared]
    grad_rate_w = lax.dynamic_slice_in_dim(
        joined[:, part + shared :], tensor_pos * rate_part, rate_part, 1
    )
    sizes = [4 * inner, inner, inner, 4 * shared, shared, heads, heads, heads, features]
    pieces, at = [], 0
    for size in sizes:
        pieces.append(packed[at : at + size])
        at += size
    (g_conv, g_conv_bias, g_out_gain, g_conv_sh, g_conv_sh_bias, g_rate_bias, g_decay, g_skip,
     g_gain_in) = pieces
    return (
        output, grad_hidden, g_gain_in, grad_gate_w, grad_inner_w, grad_shared_w, grad_rate_w,
        g_conv.reshape(4, inner), g_conv_bias, g_conv_sh.reshape(4, shared), g_conv_sh_bias,
        g_rate_bias, g_decay, g_skip, g_out_gain, grad_out_w,
    )


def solution(mesh):
    tokens = P(("dp", "tensor"), None)
    weight = P("dp", "tensor")
    in_specs = (
        tokens, P(), weight, weight, P("dp", None), weight, P(), P(), P(), P(), P(), P(), P(),
        P(), weight, tokens,
    )
    out_specs = (
        tokens, tokens, P(), weight, weight, P("dp", None), weight, P(), P(), P(), P(), P(),
        P(), P(), P(), weight,
    )
    return jax.shard_map(local, mesh=mesh, in_specs=in_specs, out_specs=out_specs, check_vma=False)
```

```python
import functools

import jax
import jax.numpy as jnp
from jax import lax
from jax.experimental import pallas as pl
from jax.experimental.pallas import tpu as pltpu
from jax.sharding import PartitionSpec as P

SEQ_LEN = 2048
CHUNK = 128
RIM = 16
LANES = 128
EPS = 1e-05
F32 = jnp.float32
BF16 = jnp.bfloat16


def mm(left, right, contract=((1,), (0,))):
    return lax.dot_general(left, right, (contract, ((), ())), preferred_element_type=F32)


NT = ((1,), (1,))
TN = ((0,), (0,))


def split3(value):
    high = value.astype(BF16)
    rest = value - high.astype(F32)
    mid = rest.astype(BF16)
    return high, mid, (rest - mid.astype(F32)).astype(BF16)


def exact_left(ones, value):
    high, mid, low = split3(value)
    return mm(ones, high) + mm(ones, mid) + mm(ones, low)


def exact_right(value, ones):
    high, mid, low = split3(value)
    return mm(high, ones) + mm(mid, ones) + mm(low, ones)


def spread_matrix(heads, inner):
    head_dim = inner // heads
    row = lax.broadcasted_iota(jnp.int32, (LANES, inner), 0)
    col = lax.broadcasted_iota(jnp.int32, (LANES, inner), 1)
    return ((col >= row * head_dim) & (col < (row + 1) * head_dim)).astype(BF16)


def iota2(shape, dim):
    return lax.broadcasted_iota(jnp.int32, shape, dim)


def softplus(v):
    return jnp.maximum(v, 0.0) + jnp.log1p(jnp.exp(-jnp.abs(v)))


def conv_rows(ext_ref, taps, bias, lo, width, rows):
    total = bias
    block = ext_ref[:, pl.ds(lo, width)]
    for k in range(4):
        total = total + taps[k : k + 1, :] * (pltpu.roll(block, 3 - k, 0) if k < 3 else block)[8:]
    return total


def spread_columns(target_ref, rows, block, inner):
    half, shared = inner // 2, 2 * LANES
    target_ref[rows, :half] = block[:, :half]
    target_ref[rows, half:inner] = block[:, half + shared + LANES :]
    target_ref[rows, inner:] = block[:, half : half + shared]


def column_of(lo, inner):
    half = inner // 2
    if lo >= inner:
        return lo - inner + half
    return lo if lo < half else lo + 3 * LANES


def mix_in_kernel(
    inner, heads,
    proj_ref, rim_ref, final_in_ref, total_in_ref, tap_ref, bias_ref, rate_bias_ref, decay_ref,
    *rest,
):
    x_ref, bc_ref, step_ref, within_ref, slope_ref, final_ref, total_ref, ext_ref, u_ref = rest[-9:]
    i = pl.program_id(0)
    shared = 2 * LANES

    @pl.when(i == 0)
    def _():
        spread_columns(ext_ref, slice(0, 8), rim_ref[...].astype(F32)[RIM - 8 :], inner)
        final_ref[...] = final_in_ref[...]
        total_ref[...] = total_in_ref[...]

    @pl.when(i > 0)
    def _():
        ext_ref[0:8, :] = ext_ref[CHUNK : CHUNK + 8, :]

    spread_columns(ext_ref, slice(8, CHUNK + 8), proj_ref[...].astype(F32), inner)
    at = inner // 2 + shared
    step = softplus(proj_ref[:, at : at + LANES].astype(F32) + rate_bias_ref[...])
    log_decay = step * decay_ref[...]
    lower = (iota2((CHUNK, CHUNK), 0) >= iota2((CHUNK, CHUNK), 1)).astype(BF16)
    within = exact_left(lower, log_decay)
    step_ref[...] = step
    within_ref[...] = within
    last = within[CHUNK - 1 :, :]
    total_ref[...] += last
    weight = step * jnp.exp(last - within)

    pre = conv_rows(ext_ref, tap_ref[:, inner:], bias_ref[:, inner:], inner, shared, CHUNK)
    sig = jax.nn.sigmoid(pre)
    bc = (pre * sig).astype(BF16)
    bc_ref[...] = bc
    slope_ref[:, inner:] = (sig * (1.0 + pre * (1.0 - sig))).astype(BF16)
    first = iota2((CHUNK, LANES), 1) < LANES // 2
    for p in range(inner // LANES):
        lo = p * LANES
        pre = conv_rows(
            ext_ref, tap_ref[:, lo : lo + LANES], bias_ref[:, lo : lo + LANES], lo, LANES, CHUNK
        )
        sig = jax.nn.sigmoid(pre)
        act = pre * sig
        x = act.astype(BF16)
        x_ref[:, lo : lo + LANES] = x
        slope_ref[:, lo : lo + LANES] = (sig + act * (1.0 - sig)).astype(BF16)
        w = jnp.where(
            first,
            jnp.broadcast_to(weight[:, 2 * p : 2 * p + 1], (CHUNK, LANES)),
            jnp.broadcast_to(weight[:, 2 * p + 1 : 2 * p + 2], (CHUNK, LANES)),
        )
        u_ref[:, lo : lo + LANES] = (x.astype(F32) * w).astype(BF16)
    factor = exact_right(jnp.exp(jnp.broadcast_to(last, (8, LANES))), spread_matrix(heads, inner))
    final_ref[...] = factor[0:1, :] * final_ref[...] + mm(bc[:, :LANES], u_ref[...], TN)


def mix_in(proj, rows, carried, consts, inner, heads, start, count, held=()):
    width = proj.shape[1]
    full = lambda shape: pl.BlockSpec(shape, lambda i: (0,) * len(shape))
    block = lambda w: pl.BlockSpec((CHUNK, w), lambda i: (start + i, 0))
    before = start * CHUNK // RIM - 1 if start else rows // RIM
    operands = [proj, proj, *carried, *consts, *held]
    return pl.pallas_call(
        functools.partial(mix_in_kernel, inner, heads),
        grid=(count,),
        in_specs=[
            block(width),
            pl.BlockSpec((RIM, width), lambda i: (before, 0)),
            *[full(v.shape) for v in (*carried, *consts)],
            *[pl.BlockSpec(memory_space=pl.ANY) for _ in held],
        ],
        out_specs=[
            block(inner), block(2 * LANES), block(LANES), block(LANES), block(inner + 2 * LANES),
            full((LANES, inner)), full((1, LANES)),
        ],
        out_shape=[
            jax.ShapeDtypeStruct((rows, inner), BF16),
            jax.ShapeDtypeStruct((rows, 2 * LANES), BF16),
            jax.ShapeDtypeStruct((rows, LANES), F32),
            jax.ShapeDtypeStruct((rows, LANES), F32),
            jax.ShapeDtypeStruct((rows, inner + 2 * LANES), BF16),
            jax.ShapeDtypeStruct((LANES, inner), F32),
            jax.ShapeDtypeStruct((1, LANES), F32),
        ],
        input_output_aliases={len(operands) - len(held) + k: k for k in range(len(held))},
        scratch_shapes=[
            pltpu.VMEM((CHUNK + 8, inner + 2 * LANES), F32),
            pltpu.VMEM((CHUNK, inner), BF16),
        ],
        compiler_params=pltpu.CompilerParams(vmem_limit_bytes=48 * 2**20),
        cost_estimate=pl.CostEstimate(
            flops=14000 * count * CHUNK * inner, bytes_accessed=8 * count * CHUNK * inner, transcendentals=0
        ),
        name="mix_in",
    )(*operands)


def mix_out_kernel(
    inner, heads,
    x_ref, bc_ref, step_ref, within_ref, gate_ref, gon_ref, entry_ref, skip_ref, gain_ref,
    normed_ref, gm_ref, gg_ref, state_ref, grad_entry_ref, sums_ref,
    hold_ref, y_ref, u_ref, prefix_ref, grow_ref, sig_ref,
):
    i = pl.program_id(0)

    @pl.when(i == 0)
    def _():
        hold_ref[...] = entry_ref[...].astype(F32)
        grad_entry_ref[...] = jnp.zeros_like(grad_entry_ref)
        sums_ref[...] = jnp.zeros_like(sums_ref)
        prefix_ref[...] = jnp.zeros_like(prefix_ref)

    spread = spread_matrix(heads, inner)
    key, query = bc_ref[:, :LANES], bc_ref[:, LANES:]
    within = within_ref[...]
    within_t = within.T
    last = within[CHUNK - 1 :, :]
    state = hold_ref[...].astype(BF16)
    state_ref[0] = state
    y_ref[...] = mm(query, state)
    scores = mm(query, key, NT)
    causal = iota2((CHUNK, CHUNK), 0) >= iota2((CHUNK, CHUNK), 1)
    first = iota2((CHUNK, LANES), 1) < LANES // 2
    zero = jnp.zeros((CHUNK, LANES), BF16)
    for p in range(inner // LANES):
        lo = p * LANES
        slab = slice(lo, lo + LANES)
        cols, weights = [], []
        for h in (2 * p, 2 * p + 1):
            col = jnp.broadcast_to(within[:, h : h + 1], (CHUNK, CHUNK))
            gap = jnp.where(causal, col - within_t[h : h + 1, :], -1e30)
            weights.append((scores * jnp.exp(gap)).astype(BF16))
            cols.append(col)
        a = jnp.where(first, cols[0], cols[1])
        d = jnp.where(
            first,
            jnp.broadcast_to(step_ref[:, 2 * p : 2 * p + 1], (CHUNK, LANES)),
            jnp.broadcast_to(step_ref[:, 2 * p + 1 : 2 * p + 2], (CHUNK, LANES)),
        )
        x = x_ref[:, slab].astype(F32)
        u = x * d
        ub = u.astype(BF16)
        u_ref[:, slab] = (u * jnp.exp(a[CHUNK - 1 :, :] - a)).astype(BF16)
        both = mm(jnp.concatenate(weights, axis=0), ub)
        diagonal = jnp.where(first, both[:CHUNK], both[CHUNK:])
        grow = jnp.exp(a)
        grow_ref[:, slab] = grow
        y_ref[:, slab] = diagonal + grow * y_ref[:, slab] + skip_ref[:, slab] * x
    factors = exact_right(
        jnp.exp(jnp.concatenate([last, prefix_ref[...], jnp.zeros((6, LANES), F32)], axis=0)),
        spread,
    )
    prefix_ref[...] += last
    hold_ref[...] = factors[0:1, :] * hold_ref[...] + mm(key, u_ref[...], TN)

    square = jnp.zeros((CHUNK, LANES), F32)
    dot = jnp.zeros((CHUNK, LANES), F32)
    for p in range(inner // LANES):
        slab = slice(p * LANES, (p + 1) * LANES)
        z = gate_ref[:, slab].astype(F32)
        m = y_ref[:, slab].astype(BF16).astype(F32)
        sig = jax.nn.sigmoid(z)
        sig_ref[:, slab] = sig
        gated = m * (z * sig)
        square = square + gated * gated
        dot = dot + gain_ref[:, slab] * gon_ref[:, slab].astype(F32) * gated
    square = jnp.sum(square, axis=1, keepdims=True)
    dot = jnp.sum(dot, axis=1, keepdims=True)
    root = lax.rsqrt(square / inner + EPS)
    pull = root * root * root * dot / inner
    for p in range(inner // LANES):
        slab = slice(p * LANES, (p + 1) * LANES)
        z = gate_ref[:, slab].astype(F32)
        m = y_ref[:, slab].astype(BF16).astype(F32)
        sig = sig_ref[:, slab]
        act = z * sig
        gated = m * act
        gon = gon_ref[:, slab].astype(F32)
        unit = gated * root
        normed_ref[:, slab] = (unit * gain_ref[:, slab]).astype(BF16)
        grad = root * gain_ref[:, slab] * gon - gated * pull
        gm = (grad * act).astype(BF16)
        gm_ref[:, slab] = gm
        gg_ref[:, slab] = (grad * m * (sig * (1.0 + z * (1.0 - sig)))).astype(BF16)
        gmf = gm.astype(F32)
        sums_ref[0:1, slab] += jnp.sum(gon * unit, axis=0, keepdims=True)
        sums_ref[1:2, slab] += jnp.sum(gmf * x_ref[:, slab].astype(F32), axis=0, keepdims=True)
        u_ref[:, slab] = (gmf * grow_ref[:, slab]).astype(BF16)
    grad_entry_ref[...] += factors[1:2, :] * mm(query, u_ref[...], TN)


def mix_out(x, bc, step, within, gate, gon, entry, skip, gain, heads):
    rows, inner = x.shape
    chunks = rows // CHUNK
    full = lambda shape: pl.BlockSpec(shape, lambda i: (0,) * len(shape))
    block = lambda width: pl.BlockSpec((CHUNK, width), lambda i: (i, 0))
    return pl.pallas_call(
        functools.partial(mix_out_kernel, inner, heads),
        grid=(chunks,),
        in_specs=[
            block(inner), block(2 * LANES), block(LANES), block(LANES), block(inner), block(inner),
            full(entry.shape), full(skip.shape), full(gain.shape),
        ],
        out_specs=[
            block(inner), block(inner), block(inner),
            pl.BlockSpec((1, LANES, inner), lambda i: (i, 0, 0)),
            full((LANES, inner)), full((8, inner)),
        ],
        out_shape=[
            jax.ShapeDtypeStruct((rows, inner), BF16),
            jax.ShapeDtypeStruct((rows, inner), BF16),
            jax.ShapeDtypeStruct((rows, inner), BF16),
            jax.ShapeDtypeStruct((chunks, LANES, inner), BF16),
            jax.ShapeDtypeStruct((LANES, inner), F32),
            jax.ShapeDtypeStruct((8, inner), F32),
        ],
        scratch_shapes=[
            pltpu.VMEM((LANES, inner), F32),
            pltpu.VMEM((CHUNK, inner), F32),
            pltpu.VMEM((CHUNK, inner), BF16),
            pltpu.VMEM((1, LANES), F32),
            pltpu.VMEM((CHUNK, inner), F32),
            pltpu.VMEM((CHUNK, inner), F32),
        ],
        compiler_params=pltpu.CompilerParams(vmem_limit_bytes=48 * 2**20),
        cost_estimate=pl.CostEstimate(
            flops=17000 * rows * inner, bytes_accessed=16 * rows * inner, transcendentals=0
        ),
        name="mix_out",
    )(x, bc, step, within, gate, gon, entry, skip, gain)


def mix_back_kernel(
    inner, heads, count, inside, rim_step,
    x_ref, bc_ref, step_ref, within_ref, gm_ref, state_ref, proj_ref, slope_ref, rim_ref,
    exit_ref, next_ref, sums_in_ref, heads_in_ref,
    skip_ref, tap_ref, rate_bias_ref, decay_ref,
    *rest,
):
    if inside:
        rest = rest[1:]
    (
        gproj_ref, hold_ref, head_ref, sums_ref, heads_ref,
        ext_ref, ahead_ref, cs_ref, bg_ref, ue_ref, ge_ref, prod_ref, rows_ref,
    ) = rest
    j = pl.program_id(0)
    shared = 2 * LANES
    conv_width = inner + shared

    @pl.when(j == 0)
    def _():
        hold_ref[...] = exit_ref[...].astype(F32)
        sums_ref[...] = sums_in_ref[...]
        heads_ref[...] = heads_in_ref[...]
        ahead_ref[CHUNK:, :] = next_ref[...]
        rows_ref[...] = jnp.zeros_like(rows_ref)

    @pl.when((j > 0) & (j < count))
    def _():
        ahead_ref[CHUNK:, :] = ahead_ref[0:8, :]

    @pl.when(j < count)
    def _():
        spread = spread_matrix(heads, inner)
        key, query = bc_ref[:, :LANES], bc_ref[:, LANES:]
        within = within_ref[...]
        within_t = within.T
        step = step_ref[...]
        last = within[CHUNK - 1 :, :]
        state = state_ref[0]
        hold = hold_ref[...]
        exit_grad = hold.astype(BF16)
        cs_ref[...] = mm(query, state)
        bg_ref[...] = mm(key, exit_grad)
        scores_t = mm(key, query, NT)
        causal_t = iota2((CHUNK, CHUNK), 0) <= iota2((CHUNK, CHUNK), 1)
        first = iota2((CHUNK, LANES), 1) < LANES // 2
        lane = iota2((2 * CHUNK, LANES), 1)
        upper_half = iota2((2 * CHUNK, LANES), 0) >= CHUNK
        zero = jnp.zeros((CHUNK, LANES), BF16)
        grad_scores_t = jnp.zeros((CHUNK, CHUNK), F32)
        col_sums = jnp.zeros((CHUNK, LANES), F32)
        for p in range(inner // LANES):
            slab = slice(p * LANES, (p + 1) * LANES)
            x = x_ref[:, slab].astype(F32)
            gb = gm_ref[:, slab]
            g = gb.astype(F32)
            cols = [
                jnp.broadcast_to(within[:, h : h + 1], (CHUNK, LANES)) for h in (2 * p, 2 * p + 1)
            ]
            a = jnp.where(first, cols[0], cols[1])
            d = jnp.where(
                first,
                jnp.broadcast_to(step[:, 2 * p : 2 * p + 1], (CHUNK, LANES)),
                jnp.broadcast_to(step[:, 2 * p + 1 : 2 * p + 2], (CHUNK, LANES)),
            )
            u = x * d
            ub = u.astype(BF16)
            to_end = jnp.exp(a[CHUNK - 1 :, :] - a)
            ge = g * jnp.exp(a)
            ge_ref[:, slab] = ge.astype(BF16)
            ue_ref[:, slab] = (u * to_end).astype(BF16)
            ucat = jnp.concatenate([jnp.where(first, ub, zero), jnp.where(first, zero, ub)], axis=0)
            reach_t = mm(ucat, gb, NT)
            pieces, moves = [], []
            for q, h in enumerate((2 * p, 2 * p + 1)):
                gap = jnp.where(causal_t, within_t[h : h + 1, :] - cols[q], -1e30)
                weight = jnp.exp(gap)
                grad_score = reach_t[q * CHUNK : (q + 1) * CHUNK] * weight
                grad_scores_t = grad_scores_t + grad_score
                pieces.append((scores_t * weight).astype(BF16))
                move = grad_score * scores_t
                moves.append(move)
                rows_ref[h : h + 1, :] = jnp.sum(move, axis=0, keepdims=True)
                col = jnp.sum(move, axis=1, keepdims=True)
                col_sums = jnp.where(lane[:CHUNK] == h, col, col_sums)
            pick = (lane == jnp.where(upper_half, 2 * p + 1, 2 * p)).astype(BF16)
            grad_state_u = to_end * bg_ref[:, slab]
            both = mm(jnp.concatenate(pieces, axis=0), gb)
            grad_u = jnp.where(first, both[:CHUNK], both[CHUNK:]) + grad_state_u
            prod_ref[0:CHUNK, slab] = (x * grad_u).astype(BF16)
            prod_ref[CHUNK : 2 * CHUNK, slab] = (u * grad_state_u).astype(BF16)
            prod_ref[2 * CHUNK :, slab] = (ge * cs_ref[:, slab]).astype(BF16)
            grad_x = d * grad_u + skip_ref[:, slab] * g
            ahead_ref[0:CHUNK, slab] = grad_x * slope_ref[:, slab].astype(F32)

        by_head = mm(prod_ref[...], spread, NT)
        grad_step = by_head[0:CHUNK]
        from_state = by_head[CHUNK : 2 * CHUNK]
        from_entry = by_head[2 * CHUNK :]
        factor = exact_right(jnp.exp(jnp.broadcast_to(last, (8, LANES))), spread)[0:1, :]
        whole = jnp.sum(hold * state.astype(F32), axis=0, keepdims=True) * factor
        whole = jnp.broadcast_to(whole, (8, inner))
        high, mid, _ = split3(whole)
        whole = (mm(high, spread, NT) + mm(mid, spread, NT))[0:1, :]
        later = (iota2((CHUNK, CHUNK), 0) <= iota2((CHUNK, CHUNK), 1)).astype(BF16)
        earlier = (iota2((CHUNK, CHUNK), 0) > iota2((CHUNK, CHUNK), 1)).astype(BF16)
        row_sums = rows_ref[...].T
        grad_log = (
            exact_left(later, row_sums - col_sums + from_entry)
            + exact_left(earlier, from_state)
            + whole
        )
        decay = decay_ref[...]
        grad_step = grad_step + grad_log * decay
        rates = slice(inner // 2 + shared, inner // 2 + shared + LANES)
        squash = jax.nn.sigmoid(proj_ref[:, rates].astype(F32) + rate_bias_ref[...])
        grad_rate = grad_step * squash
        gproj_ref[:, rates] = grad_rate.astype(BF16)
        heads_ref[0:1, :] += jnp.sum(grad_rate, axis=0, keepdims=True)
        heads_ref[1:2, :] += jnp.sum(grad_log * step, axis=0, keepdims=True) * decay

        gsb = grad_scores_t.astype(BF16)
        grad_key = mm(ue_ref[...], exit_grad, NT) + mm(gsb, query)
        grad_query = mm(ge_ref[...], state, NT) + mm(gsb, key, TN)
        hold_ref[...] = factor * hold + mm(query, ge_ref[...], TN)

        slope = slope_ref[:, inner:].astype(F32)
        ahead_ref[0:CHUNK, inner:] = jnp.concatenate([grad_key, grad_query], axis=1) * slope

        for p in range(conv_width // LANES):
            slab = slice(p * LANES, (p + 1) * LANES)
            lo = column_of(p * LANES, inner)
            values = proj_ref[:, lo : lo + LANES].astype(F32)
            total = jnp.zeros((CHUNK, LANES), F32)
            ahead = ahead_ref[:, slab]
            for k in range(4):
                moved = pltpu.roll(ahead, (k - 3) % (CHUNK + 8), 0)[:CHUNK] if k < 3 else ahead[:CHUNK]
                total = total + tap_ref[k : k + 1, slab] * moved
                sums_ref[k : k + 1, slab] += jnp.sum(values * moved, axis=0, keepdims=True)
                if k == 3:
                    sums_ref[4:5, slab] += jnp.sum(moved, axis=0, keepdims=True)
            gproj_ref[:, lo : lo + LANES] = total.astype(BF16)
        head_ref[...] = ahead_ref[0:8, :]

    if not rim_step:
        return

    @pl.when(j == count)
    def _():
        gproj_ref[...] = jnp.zeros_like(gproj_ref)
        head = ahead_ref[0:8, :]
        at = iota2((8, conv_width), 0)
        spread_columns(ext_ref, slice(0, 8), rim_ref[...].astype(F32)[RIM - 8 :], inner)
        values = ext_ref[0:8, :]
        total = jnp.zeros((8, conv_width), F32)
        for k in range(3):
            moved = jnp.zeros((8, conv_width), F32)
            for r in range(5 + k, 8):
                t = r - 5 - k
                moved = moved + jnp.where(at == r, head[t : t + 1, :], 0.0)
            total = total + tap_ref[k : k + 1, :] * moved
            sums_ref[k : k + 1, :] += jnp.sum(values * moved, axis=0, keepdims=True)
        total = jnp.concatenate([jnp.zeros((RIM - 8, conv_width), F32), total], axis=0)
        total = total.astype(BF16)
        half = inner // 2
        gproj_ref[0:RIM, :half] = total[:, :half]
        gproj_ref[0:RIM, half : half + shared] = total[:, inner:]
        gproj_ref[0:RIM, half + shared + LANES :] = total[:, half:inner]


def mix_back(x, bc, step, within, gm, state, proj, slope, carried, consts, heads, top, count, gproj,
             rim_step):
    inside = gproj is not None
    rows, inner = x.shape
    width = proj.shape[1]
    chunks = rows // CHUNK
    conv_width = inner + 2 * LANES
    full = lambda shape: pl.BlockSpec(shape, lambda j: (0,) * len(shape))
    at = lambda j: jnp.maximum(top - j, top - count + 1)
    block = lambda w: pl.BlockSpec((CHUNK, w), lambda j: (at(j), 0))
    operands = [x, bc, step, within, gm, state, proj, slope, proj, *carried, *consts]
    in_specs = [
        block(inner), block(2 * LANES), block(LANES), block(LANES), block(inner),
        pl.BlockSpec((1, LANES, inner), lambda j: (at(j), 0, 0)),
        block(width),
        block(conv_width),
        pl.BlockSpec((RIM, width), lambda j: (rows // RIM, 0)),
        *[full(v.shape) for v in (*carried, *consts)],
    ]
    if inside:
        operands.append(gproj)
        in_specs.append(pl.BlockSpec(memory_space=pl.ANY))
    return pl.pallas_call(
        functools.partial(mix_back_kernel, inner, heads, count, inside, rim_step),
        grid=(count + 1 if rim_step else count,),
        in_specs=in_specs,
        out_specs=[
            pl.BlockSpec((CHUNK, width), lambda j: (jnp.where(j == count, chunks, at(j)), 0)),
            full((LANES, inner)), full((8, conv_width)), full((8, conv_width)), full((8, LANES)),
        ],
        out_shape=[
            jax.ShapeDtypeStruct((rows + CHUNK, width), BF16),
            jax.ShapeDtypeStruct((LANES, inner), F32),
            jax.ShapeDtypeStruct((8, conv_width), F32),
            jax.ShapeDtypeStruct((8, conv_width), F32),
            jax.ShapeDtypeStruct((8, LANES), F32),
        ],
        scratch_shapes=[
            pltpu.VMEM((8, conv_width), F32),
            pltpu.VMEM((CHUNK + 8, conv_width), F32),
            pltpu.VMEM((CHUNK, inner), F32),
            pltpu.VMEM((CHUNK, inner), F32),
            pltpu.VMEM((CHUNK, inner), BF16),
            pltpu.VMEM((CHUNK, inner), BF16),
            pltpu.VMEM((3 * CHUNK, inner), BF16),
            pltpu.VMEM((LANES, CHUNK), F32),
        ],
        input_output_aliases={len(operands) - 1: 0} if inside else {},
        compiler_params=pltpu.CompilerParams(vmem_limit_bytes=48 * 2**20),
        cost_estimate=pl.CostEstimate(
            flops=32768 * count * CHUNK * inner, bytes_accessed=16 * count * CHUNK * inner,
            transcendentals=0,
        ),
        name="mix_back",
    )(*operands)


def swap(value, axis, bit):
    size = lax.axis_size(axis)
    return lax.ppermute(value, axis, [(i, i ^ bit) for i in range(size)])


def bits_of(axis):
    size = lax.axis_size(axis)
    return [1 << k for k in range(size.bit_length() - 1)]


def join(value, axis, bit, dim):
    return beside(value, swap(value, axis, bit), axis, bit, dim)


def beside(value, other, axis, bit, dim):
    high = (lax.axis_index(axis) & bit) != 0
    return jnp.where(high, jnp.stack([other, value], axis=dim), jnp.stack([value, other], axis=dim))


def join_cols(value):
    for bit in bits_of("tensor"):
        other = swap(value, "tensor", bit)
        high = (lax.axis_index("tensor") & bit) != 0
        value = jnp.where(
            high,
            jnp.concatenate([other, value], axis=-1),
            jnp.concatenate([value, other], axis=-1),
        )
    return value


def join_dp(stack, bits, done):
    for bit in bits:
        stack = join(stack, "dp", bit, done)
        done += 1
    return stack


def side(axis, bit):
    return jnp.where((lax.axis_index(axis) & bit) != 0, 1, 0)


def fold_rows(value, bit, dim=0):
    mine = side("dp", bit)
    shape = value.shape
    pairs = value.reshape(*shape[:dim], shape[dim] // 2, 2, *shape[dim + 1 :])
    pick = lambda k: lax.dynamic_index_in_dim(pairs, k, dim + 1, keepdims=False)
    return pick(mine), pick(1 - mine)


def fold_cols(value, bit, rest=0):
    high = side("tensor", bit) == 1
    half = (value.shape[-1] - rest) // 2
    low_part, high_part = value[..., : half + rest], value[..., half:]
    return jnp.where(high, high_part, low_part), jnp.where(high, low_part, high_part)


def plus(keep, got):
    return (keep.astype(F32) + got.astype(F32)).astype(BF16)


def in_order(value, rest):
    high = side("tensor", lax.axis_size("tensor") // 2) == 1
    half = value.shape[-1] - rest
    turned = jnp.concatenate([value[..., rest:], value[..., :rest]], axis=-1)
    return jnp.where(high, turned, value)


def more_cols(value, rest=0):
    bits = bits_of("tensor")[-2::-1]
    if not bits:
        return value
    if rest:
        value = in_order(value, rest)
    for bit in bits:
        width = value.shape[-1] - rest
        keep, give = fold_cols(value[..., :width], bit)
        tail = value[..., width:]
        give = jnp.concatenate([give, tail], axis=-1)
        value = plus(jnp.concatenate([keep, tail], axis=-1), swap(give, "tensor", bit))
    return value


def local(
    hidden, input_gain, proj_gate, proj_inner, proj_shared, proj_rate, conv_inner,
    conv_inner_bias, conv_shared, conv_shared_bias, rate_bias, decay_log, skip_gain,
    output_gain, proj_output, cotangent,
):
    tensor_size = lax.axis_size("tensor")
    tensor_pos = lax.axis_index("tensor")
    rows, features = hidden.shape
    heads = rate_bias.shape[0]
    inner = output_gain.shape[0]
    shared = conv_shared.shape[1]
    head_dim = inner // heads
    conv_width = inner + shared
    per_seq = SEQ_LEN // rows
    seq_pos = lax.rem(tensor_pos, per_seq)
    part = inner // tensor_size
    rate_part = heads // tensor_size
    forward = [(i, i + 1) for i in range(tensor_size - 1)]
    backward = [(i + 1, i) for i in range(tensor_size - 1)]

    dp_bits = bits_of("dp")
    far, near = dp_bits[:0:-1], dp_bits[:1]
    dp_size, part_rows = lax.axis_size("dp"), proj_inner.shape[0]
    far_z, far_x = far[:-1], far[-1:]
    shared_part = shared // tensor_size
    rate_block = lax.dynamic_update_slice(
        jnp.zeros((part_rows, LANES), BF16), proj_rate, (0, tensor_pos * rate_part)
    )
    shared_block = lax.dynamic_slice_in_dim(proj_shared, tensor_pos * shared_part, shared_part, 1)
    piece = jnp.concatenate([proj_inner, shared_block, rate_block], axis=1)
    first_w = join_dp(piece, far_z, 0)
    first_w, both_w, rim = lax.optimization_barrier(
        (first_w, jnp.concatenate([proj_output, proj_gate], axis=1), hidden[rows - RIM :])
    )
    both_w = join_dp(both_w, far_z[:1], 0)
    upper, lower = join_cols(first_w[0]), join_dp(first_w[1], far_x, len(far_z) - 1)
    rim = lax.ppermute(rim, "tensor", forward)
    upper, lower, rim = lax.optimization_barrier((upper, lower, rim))
    upper, lower = join_dp(upper, far_x, len(far_z) - 1), join_cols(lower)
    first_w, both_w = lax.optimization_barrier((jnp.stack([upper, lower]), both_w))
    pieces = [
        first_w[..., k * piece.shape[1] : (k + 1) * piece.shape[1]] for k in range(tensor_size)
    ]
    inner_cols = [v[..., :part] for v in pieces]
    rate_cols = sum(v[..., part + shared_part :] for v in pieces)
    first_w = jnp.concatenate(
        inner_cols[: tensor_size // 2]
        + [v[..., part : part + shared_part] for v in pieces]
        + [rate_cols]
        + inner_cols[tensor_size // 2 :],
        axis=-1,
    )
    first_w = join_dp(first_w, near, len(far)).reshape(dp_size * part_rows, -1)
    first_w, both_w = lax.optimization_barrier((first_w, join_dp(both_w, far_z[1:], 1)))
    output_w, gate_w = both_w[..., :part], both_w[..., part:]
    gate_w = join_dp(gate_w, far_x, len(far_z))
    output_w = join_cols(output_w)

    rim = jnp.where(seq_pos == 0, jnp.zeros_like(rim), rim)
    extended = jnp.pad(
        jnp.concatenate([hidden, rim], axis=0), ((0, CHUNK - RIM), (0, 0))
    ).astype(F32)
    gain_in = input_gain.astype(F32)
    root = lax.rsqrt(jnp.mean(extended * extended, axis=-1, keepdims=True) + EPS)
    normed = (extended * root * gain_in).astype(BF16)

    proj = mm(normed, first_w).astype(BF16)
    proj, gate_w, output_w = lax.optimization_barrier((proj, gate_w, output_w))
    gate_w = join_cols(gate_w)
    output_w = join_dp(output_w, far_x, len(far_z))
    taps = jnp.concatenate([conv_inner, conv_shared], axis=1).astype(F32)
    bias = jnp.concatenate([conv_inner_bias, conv_shared_bias])[None].astype(F32)
    pad_heads = lambda v: jnp.pad(v, (0, LANES - heads))[None]
    rate_bias_row = pad_heads(rate_bias)
    decay_row = pad_heads(-jnp.exp(decay_log))
    skip_row = jnp.repeat(skip_gain, head_dim)[None]
    gain_row = output_gain[None].astype(F32)
    chunks = rows // CHUNK
    lead_count = chunks - max(chunks // 4, 1)
    consts = [taps, bias, rate_bias_row, decay_row]
    *held, final, total = mix_in(
        proj, rows, [jnp.zeros((LANES, inner), F32), jnp.zeros((1, LANES), F32)], consts, inner,
        heads, 0, lead_count,
    )
    final, gate_w, output_w = lax.optimization_barrier((final, gate_w, output_w))
    gate_near, output_near = swap(gate_w, "dp", near[0]), swap(output_w, "dp", near[0])
    x, bc, step, within, slope, final, total = mix_in(
        proj, rows, [final, total], consts, inner, heads, lead_count, chunks - lead_count, held
    )
    final, gate_near, output_near = lax.optimization_barrier((final, gate_near, output_near))
    whole = jnp.repeat(jnp.exp(total[0, :heads]), head_dim)[None]
    entry = jnp.zeros_like(final)
    for _ in range(per_seq - 1):
        sent = lax.ppermute((final + whole * entry).astype(BF16), "tensor", forward)
        entry = jnp.where(seq_pos == 0, 0.0, sent.astype(F32))

    gate_w = beside(gate_w, gate_near, "dp", near[0], len(far)).reshape(dp_size * part_rows, inner)
    output_w = beside(output_w, output_near, "dp", near[0], len(far))
    output_w = output_w.reshape(dp_size * part_rows, inner)
    gate = mm(normed[:rows], gate_w).astype(BF16)
    gon = mm(cotangent, output_w).astype(BF16)
    out_normed, grad_mixed, grad_gate, states, grad_entry, out_sums = mix_out(
        x, bc, step, within, gate, gon, entry, skip_row, gain_row, heads
    )
    exit_grad = jnp.zeros_like(grad_entry)
    for _ in range(per_seq - 1):
        sent = lax.ppermute((grad_entry + whole * exit_grad).astype(BF16), "tensor", backward)
        exit_grad = jnp.where(seq_pos == per_seq - 1, 0.0, sent.astype(F32))

    core, cross, long = dp_bits[0], dp_bits[1], dp_bits[2:]
    tensor_top = bits_of("tensor")[-1]
    blocks = lambda v: v.astype(BF16).reshape(dp_size, part_rows, -1)
    grad_out_w = blocks(mm(cotangent, out_normed, TN))
    grad_gate_w = mm(normed[:rows], grad_gate, TN)
    gain_gate = jnp.sum(grad_gate_w * gate_w.astype(F32), axis=1)
    grad_gate_w = blocks(grad_gate_w)
    keep_o, give_o = fold_rows(grad_out_w, core)
    keep_g, give_g = fold_rows(grad_gate_w, core)
    exit_grad, give_o, give_g = lax.optimization_barrier((exit_grad, give_o, give_g))
    got_o, got_g = swap(give_o, "dp", core), swap(give_g, "dp", core)

    consts = [skip_row, taps, rate_bias_row, decay_row]
    counts = [chunks // 4, (chunks - chunks // 4) // 2]
    counts.append(chunks - sum(counts))
    tops = [chunks - 1, chunks - 1 - counts[0], counts[2] - 1]
    carried = [
        exit_grad, jnp.zeros((8, conv_width), F32), jnp.zeros((8, conv_width), F32),
        jnp.zeros((8, LANES), F32),
    ]
    back = lambda k, *more: mix_back(
        x, bc, step, within, grad_mixed, states, proj, slope, carried, consts, heads, tops[k], counts[k],
        *more,
    )
    grad_proj, *carried = back(0, None, False)
    grad_proj, got_g, got_o = lax.optimization_barrier((grad_proj, got_g, got_o))
    keep_g, give_g = fold_rows(plus(keep_g, got_g), cross)
    keep_o, give_o = fold_cols(plus(keep_o, got_o), tensor_top)
    grad_proj, give_g, give_o = lax.optimization_barrier((grad_proj, give_g, give_o))
    got_g, got_o = swap(give_g, "dp", cross), swap(give_o, "tensor", tensor_top)
    grad_proj, *carried = back(1, grad_proj, False)
    grad_proj, got_g, got_o = lax.optimization_barrier((grad_proj, got_g, got_o))
    keep_g, give_g = fold_cols(plus(keep_g, got_g), tensor_top)
    keep_o, give_o = fold_rows(more_cols(plus(keep_o, got_o)), cross)
    grad_proj, give_g, give_o = lax.optimization_barrier((grad_proj, give_g, give_o))
    got_g, got_o = swap(give_g, "tensor", tensor_top), swap(give_o, "dp", cross)
    grad_proj, _, _, conv_sums, head_sums = back(2, grad_proj, True)
    grad_proj, got_g, got_o = lax.optimization_barrier((grad_proj, got_g, got_o))

    rest = shared + LANES
    first = mm(normed, grad_proj, TN)
    gain_first = jnp.sum(first * first_w.astype(F32), axis=1)
    first = blocks(first)
    keep, give = fold_rows(first, core)
    grad_proj, give = lax.optimization_barrier((grad_proj, give))
    got = swap(give, "dp", core)
    tail = jnp.concatenate(
        [
            conv_sums[:5, inner:].reshape(-1),
            head_sums[0, :heads],
            head_sums[1, :heads],
            jnp.sum(out_sums[1].reshape(heads, head_dim), axis=1),
            (gain_first + gain_gate) / gain_in,
        ]
    )
    packed = jnp.concatenate([conv_sums[:5, :inner].reshape(-1), out_sums[0], tail])
    packed = jnp.pad(packed, (0, -packed.shape[0] % 1024)).reshape(-1, LANES)

    got_s = swap(packed, "dp", core)
    grad_ext = mm(grad_proj, first_w, NT)
    grad_ext, got, got_s = lax.optimization_barrier((grad_ext, got, got_s))
    packed = packed + got_s
    first = plus(keep, got)
    first = first.reshape(first.shape[0] // 4, 2, 2, part_rows, first.shape[-1])
    pick = lambda v, k: lax.dynamic_index_in_dim(v, k, 1, keepdims=False)
    on_x = side("dp", cross)
    left, right = first[:, 1], first[:, 0]
    keep_l, give_l = pick(left, on_x), pick(left, 1 - on_x)
    keep_r, give_r = fold_cols(right, tensor_top, rest)
    give_l, give_r, grad_ext, grad_gate, got_o, got_g, packed, out_normed = (
        lax.optimization_barrier(
            (give_l, give_r, grad_ext, grad_gate, got_o, got_g, packed, out_normed)
        )
    )
    got_l, got_r = swap(give_l, "dp", cross), swap(give_r, "tensor", tensor_top)
    gate_back = mm(grad_gate, gate_w, NT)
    packed = packed + swap(packed, "dp", cross)
    pair = jnp.stack([more_cols(plus(keep_g, got_g)), plus(keep_o, got_o)])
    keep_p, give_p = fold_rows(pair, long[0], 1)
    got_p = swap(give_p, "dp", long[0])
    rim_grad = lax.ppermute(grad_ext[rows : rows + RIM], "tensor", backward)
    rim_grad = jnp.where(seq_pos == per_seq - 1, 0.0, rim_grad)
    grad_normed = grad_ext[:rows] + gate_back
    grad_normed = grad_normed + jnp.pad(rim_grad, ((rows - RIM, 0), (0, 0)))
    unit = hidden.astype(F32) * root[:rows]
    scaled = grad_normed * gain_in
    grad_hidden = (
        cotangent.astype(F32)
        + root[:rows] * (scaled - unit * jnp.mean(scaled * unit, axis=-1, keepdims=True))
    ).astype(BF16)

    output = (hidden.astype(F32) + mm(out_normed, output_w, NT)).astype(BF16)
    got_l, got_r, got_p, packed, output = lax.optimization_barrier(
        (got_l, got_r, got_p, packed, output)
    )
    pair = plus(keep_p, got_p)
    for bit in long[1:]:
        keep_p, give_p = fold_rows(pair, bit, 1)
        pair = plus(keep_p, swap(give_p, "dp", bit))
    left, right = plus(keep_l, got_l), more_cols(plus(keep_r, got_r), rest)
    keep_l, give_l = fold_cols(left, tensor_top, rest)
    keep_r, give_r = pick(right, on_x), pick(right, 1 - on_x)
    bits = bits_of("tensor")
    sums = [("tensor", bit) for bit in bits] + [("dp", bit) for bit in long]
    got_l, got_r, packed, pair = lax.optimization_barrier(
        (
            swap(give_l, "tensor", tensor_top),
            swap(give_r, "dp", cross),
            packed + swap(packed, *sums[0]),
            pair,
        )
    )
    left, right = more_cols(plus(keep_l, got_l), rest), plus(keep_r, got_r)
    on_z = side("dp", long[0]) == 1
    keep, give = jnp.where(on_z, left, right), jnp.where(on_z, right, left)
    for k, bit in enumerate(long[1:]):
        got, packed = lax.optimization_barrier(
            (swap(give, "dp", bit >> 1), packed + swap(packed, *sums[k + 1]))
        )
        keep, give = fold_rows(plus(keep, got), bit)
    got = swap(give, "dp", long[-1])
    for axis, bit in sums[len(long) :]:
        packed = packed + swap(packed, axis, bit)
    joined = (keep.astype(F32) + got.astype(F32)).reshape(part_rows, -1)
    if len(bits) == 1:
        joined = in_order(joined, rest)
    packed = packed.reshape(-1)
    pair = pair.astype(F32).reshape(2, part_rows, part)
    grad_gate_w, grad_out_w = pair[0], pair[1]
    grad_inner_w = joined[:, :part]
    grad_shared_w = joined[:, part : part + shared]
    grad_rate_w = lax.dynamic_slice_in_dim(
        joined[:, part + shared :], tensor_pos * rate_part, rate_part, 1
    )
    sizes = [4 * inner, inner, inner, 4 * shared, shared, heads, heads, heads, features]
    pieces, at = [], 0
    for size in sizes:
        pieces.append(packed[at : at + size])
        at += size
    (g_conv, g_conv_bias, g_out_gain, g_conv_sh, g_conv_sh_bias, g_rate_bias, g_decay, g_skip,
     g_gain_in) = pieces
    return (
        output, grad_hidden, g_gain_in, grad_gate_w, grad_inner_w, grad_shared_w, grad_rate_w,
        g_conv.reshape(4, inner), g_conv_bias, g_conv_sh.reshape(4, shared), g_conv_sh_bias,
        g_rate_bias, g_decay, g_skip, g_out_gain, grad_out_w,
    )


def solution(mesh):
    tokens = P(("dp", "tensor"), None)
    weight = P("dp", "tensor")
    in_specs = (
        tokens, P(), weight, weight, P("dp", None), weight, P(), P(), P(), P(), P(), P(), P(),
        P(), weight, tokens,
    )
    out_specs = (
        tokens, tokens, P(), weight, weight, P("dp", None), weight, P(), P(), P(), P(), P(),
        P(), P(), P(), weight,
    )
    return jax.shard_map(local, mesh=mesh, in_specs=in_specs, out_specs=out_specs, check_vma=False)
```
